32 devices in a mesh: seq: 8 (over z, x), mp: 4 (over y, core).
Axes of the slice: x: 2, y: 2, z: 4, core: 2. Of those that a mesh axis runs over, the one named last changes fastest.
Arguments:
- inputs: bfloat16 [1024, 4, 8192], P('mp', None, 'seq'), may hold values from -12 to 12
- valid: int32 [4, 8192], P(None, 'seq'), may hold values from 0 to 1, as said below
- cotangent: bfloat16 [1024, 4, 8192], P('mp', None, 'seq'), may hold values from -6 to 6
- first_gain: float32 [1024], P('mp'), may hold values from 0.25 to 1.75
- step_size: float32 [1024], P('mp'), may hold values from 0.001 to 0.1
- decay_rate: float32 [1024, 32], P('mp'), may hold values from 0.2 to 1
- frequency: float32 [1024, 32], P('mp'), may hold values from 0 to 50
- readout_real: float32 [1024, 32], P('mp'), may hold values from -3 to 3
- readout_imag: float32 [1024, 32], P('mp'), may hold values from -3 to 3
- skip_weight: float32 [1024], P('mp'), may hold values from -4 to 4
- gated_weight: bfloat16 [1024, 2, 1024], P(None, None, 'mp'), may hold values from -0.1875 to 0.1875
- gated_bias: float32 [2, 1024], P(None, 'mp'), may hold values from -2 to 2
- second_gain: float32 [1024], P('mp'), may hold values from 0.25 to 1.75
- expand_weight: bfloat16 [1024, 4096], P(None, 'mp'), may hold values from -0.1875 to 0.1875
- expand_bias: float32 [4096], P('mp'), may hold values from -2 to 2
- shrink_weight: bfloat16 [4096, 1024], P('mp'), may hold values from -0.09375 to 0.09375
- shrink_bias: float32 [1024], P('mp'), may hold values from -2 to 2
Outputs:
- result: bfloat16 [1024, 4, 8192], P('mp', None, 'seq')
- grad_inputs: float32 [1024, 4, 8192], P('mp', None, 'seq')
- grad_first_gain: float32 [1024], P('mp')
- grad_step_size: float32 [1024], P('mp')
- grad_decay_rate: float32 [1024, 32], P('mp')
- grad_frequency: float32 [1024, 32], P('mp')
- grad_readout_real: float32 [1024, 32], P('mp')
- grad_readout_imag: float32 [1024, 32], P('mp')
- grad_skip_weight: float32 [1024], P('mp')
- grad_gated_weight: float32 [1024, 2, 1024], P(None, None, 'mp')
- grad_gated_bias: float32 [2, 1024], P(None, 'mp')
- grad_second_gain: float32 [1024], P('mp')
- grad_expand_weight: float32 [1024, 4096], P(None, 'mp')
- grad_expand_bias: float32 [4096], P('mp')
- grad_shrink_weight: float32 [4096, 1024], P('mp')
- grad_shrink_bias: float32 [1024], P('mp')
- rms_input: float32 [], replicated
- rms_branch: float32 [], replicated
- rms_feed: float32 [], replicated
The draws below stay inside these ranges and needn't reach their ends.
Inputs may be any that keep to these rules, and one draw needn't show every extreme that they name: In each context the valid tokens are the first ones up to the context's length and the rest are invalid; every length is at least 6144, and one context, drawn from the seed, is valid at every position.
All inputs are finite; a program needn't handle non-finite values.
Results may differ from the reference program's by a relative error of at most 0.0081.
Values may be sent and summed in bfloat16 or wider, within the bound.
No kernel may reach another device: no remote copies, remote signals or barrier semaphores. Data moves between devices by JAX's collectives and lax.ppermute only.
A program may use at most 256 MiB of HBM per device.

```python
import math
import jax
import jax.numpy as jnp
from jax import lax

D = 1024
L = 8192
FF = 4096
N2 = 32
CTX = 4


def draw_inputs(key, part):
    key = jax.random.fold_in(key, 11)
    placing = jnp.arange(L, dtype=jnp.float32) / (L - 1)
    base = jnp.clip(jax.random.normal(key, (D, CTX, L), jnp.float32), -6.0, 6.0)
    scaling = 0.5 * jnp.exp(placing * jnp.log(4.0))
    return (base * scaling).astype(jnp.bfloat16)


def draw_valid(key, part):
    key = jax.random.fold_in(key, 23)
    length_key, pick_key = jax.random.split(key)
    lengths = jax.random.randint(length_key, (CTX,), 3 * L // 4, L + 1)
    chosen = jax.random.randint(pick_key, (), 0, CTX)
    lengths = jnp.where(jnp.arange(CTX) == chosen, L, lengths)
    return (jnp.arange(L)[None, :] < lengths[:, None]).astype(jnp.int32)


def level_of(stream_key, extent, cuts, low, top_value):
    loudness = 1.0
    for position, parts in cuts:
        draws = jax.random.uniform(jax.random.fold_in(jax.random.fold_in(stream_key, 6), position), (parts,), jnp.float32, low / len(cuts), top_value / len(cuts))
        loudness = loudness * jnp.repeat(jnp.exp(draws), extent[position] // parts).reshape((-1,) + (1,) * (len(extent) - 1 - position))
    return loudness


def scatter_about(stream_key, dims, scale, bound, cuts=(), held_as=jnp.bfloat16):
    array = jax.random.normal(stream_key, dims, jnp.float32) * scale
    if len(cuts) > 0:
        array = level_of(stream_key, dims, cuts, -0.22, 0.18) * array
    return jnp.clip(array, min=-bound, max=bound).astype(held_as)


def setup_inputs(seed: int = 0) -> dict:
    key_of = jax.random.split(jax.random.key(seed), 18)
    inputs = draw_inputs(jax.random.fold_in(key_of[17], 71), 0)
    valid = draw_valid(jax.random.fold_in(key_of[17], 71), 0)
    cotangent = scatter_about(key_of[2], (D, CTX, L), 1.0, 6.0, ((0, 4), (2, 8)))
    first_gain = jnp.clip(1.0 + 0.15 * jax.random.normal(key_of[3], (D,), jnp.float32), 0.25, 1.75)
    step_size = jnp.clip(jnp.exp(math.log(0.1) - 4.6051702 * jax.random.uniform(key_of[4], (D,), jnp.float32) ** level_of(key_of[4], (D,), ((0, 4),), -0.2, 0.2)), 0.001, 0.1)
    decay_rate = jnp.clip(jnp.exp(math.log(1.0) - 1.609438 * jax.random.uniform(key_of[5], (D, N2), jnp.float32) ** level_of(key_of[5], (D, N2), ((0, 4),), -0.2, 0.2)), 0.2, 1.0)
    frequency = jnp.clip(50.0 * jax.random.uniform(key_of[6], (D, N2), jnp.float32) ** level_of(key_of[6], (D, N2), ((0, 4),), -0.2, 0.2), 0.0, 50.0)
    readout_real = scatter_about(key_of[7], (D, N2), 0.5, 3.0, ((0, 4),), jnp.float32)
    readout_imag = scatter_about(key_of[8], (D, N2), 0.5, 3.0, ((0, 4),), jnp.float32)
    skip_weight = scatter_about(key_of[9], (D,), 1.0, 4.0, ((0, 4),), jnp.float32)
    gated_weight = scatter_about(key_of[10], (D, 2, D), D ** -0.5, 0.1875, ((2, 4),))
    gated_bias = scatter_about(key_of[11], (2, D), 0.3, 2.0, ((1, 4),), jnp.float32)
    second_gain = jnp.clip(1.0 + 0.15 * jax.random.normal(key_of[12], (D,), jnp.float32), 0.25, 1.75)
    expand_weight = scatter_about(key_of[13], (D, FF), D ** -0.5, 0.1875, ((1, 4),))
    expand_bias = scatter_about(key_of[14], (FF,), 0.3, 2.0, ((0, 4),), jnp.float32)
    shrink_weight = scatter_about(key_of[15], (FF, D), FF ** -0.5, 0.09375, ((0, 4),))
    shrink_bias = scatter_about(key_of[16], (D,), 0.3, 2.0, ((0, 4),), jnp.float32)
    return dict(inputs=inputs, valid=valid, cotangent=cotangent, first_gain=first_gain, step_size=step_size, decay_rate=decay_rate, frequency=frequency, readout_real=readout_real, readout_imag=readout_imag, skip_weight=skip_weight, gated_weight=gated_weight, gated_bias=gated_bias, second_gain=second_gain, expand_weight=expand_weight, expand_bias=expand_bias, shrink_weight=shrink_weight, shrink_bias=shrink_bias)


@jax.custom_vjp
def low(v):
    return lax.optimization_barrier(v.astype(jnp.bfloat16)).astype(jnp.float32)

@jax.custom_vjp
def low_back(v):
    return v

def low_keep(v):
    return (low(v), None)

def low_pass(kept, grad):
    return (grad,)

def back_keep(v):
    return (v, None)

def back_low(kept, grad):
    return (low(grad),)
low.defvjp(low_keep, low_pass)
low_back.defvjp(back_keep, back_low)
highest = lax.Precision.HIGHEST
epsilon = 1e-05

def kernel_block(step_size, decay_rate, frequency, readout_real, readout_imag):
    real_part = -decay_rate
    imag_part = frequency
    scaled_real = step_size[:, None] * real_part
    scaled_imag = step_size[:, None] * imag_part
    growth = jnp.exp(scaled_real)
    minus_real = growth * jnp.cos(scaled_imag) - 1.0
    minus_imag = growth * jnp.sin(scaled_imag)
    modulus = real_part * real_part + imag_part * imag_part
    ratio_real = (minus_real * real_part + minus_imag * imag_part) / modulus
    ratio_imag = (minus_imag * real_part - minus_real * imag_part) / modulus
    coeff_real = readout_real * ratio_real - readout_imag * ratio_imag
    coeff_imag = readout_real * ratio_imag + readout_imag * ratio_real
    positions = jnp.arange(L, dtype=jnp.float32)
    envelope = jnp.exp(scaled_real[:, :, None] * positions)
    angles = scaled_imag[:, :, None] * positions
    waves = coeff_real[:, :, None] * jnp.cos(angles) - coeff_imag[:, :, None] * jnp.sin(angles)
    return 2.0 * lax.optimization_barrier(jnp.sum(envelope * waves, axis=1))

def reference(inputs, valid, cotangent, first_gain, step_size, decay_rate, frequency, readout_real, readout_imag, skip_weight, gated_weight, gated_bias, second_gain, expand_weight, expand_bias, shrink_weight, shrink_bias):
    masks = valid.astype(jnp.float32)
    samples = jnp.moveaxis(inputs.astype(jnp.float32), 1, 0)
    params = (first_gain.astype(jnp.float32), step_size.astype(jnp.float32), decay_rate.astype(jnp.float32), frequency.astype(jnp.float32), readout_real.astype(jnp.float32), readout_imag.astype(jnp.float32), skip_weight.astype(jnp.float32), gated_weight.astype(jnp.float32), gated_bias.astype(jnp.float32), second_gain.astype(jnp.float32), expand_weight.astype(jnp.float32), expand_bias.astype(jnp.float32), shrink_weight.astype(jnp.float32), shrink_bias.astype(jnp.float32))

    def forward(gain_one, steps, decays, freqs, out_real, out_imag, skips, gate_w, gate_b, gain_two, up_w, up_b, down_w, down_b, contexts):
        width = 32
        groups = D // width
        blocks = (steps.reshape(groups, width), decays.reshape(groups, width, N2), freqs.reshape(groups, width, N2), out_real.reshape(groups, width, N2), out_imag.reshape(groups, width, N2))
        kernels = lax.map(jax.checkpoint(lambda pieces: kernel_block(*pieces)), blocks).reshape(D, L)
        kernel_spec = jnp.fft.rfft(kernels, n=2 * L, axis=1)

        def context(sample, weights_mask):
            scale_one = lax.rsqrt(lax.optimization_barrier(jnp.mean(sample * sample, axis=0)) + epsilon)
            normed_one = low_back(low(sample * scale_one * gain_one[:, None]))
            spec = jnp.fft.rfft(normed_one, n=2 * L, axis=1)
            conv = jnp.fft.irfft(spec * kernel_spec, n=2 * L, axis=1)[:, :L]
            mixed = low_back(low(conv + skips[:, None] * normed_one))
            lifted_one = low(jax.nn.gelu(mixed))
            projected = low_back(jnp.einsum('dko,dl->kol', gate_w, lifted_one, precision=highest) + gate_b[:, :, None])
            branch = projected[0] * jax.nn.sigmoid(projected[1])
            hidden = sample + branch
            scale_two = lax.rsqrt(lax.optimization_barrier(jnp.mean(hidden * hidden, axis=0)) + epsilon)
            normed_two = low(hidden * scale_two * gain_two[:, None])
            expanded = low_back(jnp.dot(up_w.T, normed_two, precision=highest) + up_b[:, None])
            lifted_three = low(jax.nn.gelu(expanded))
            feed = jnp.dot(down_w.T, lifted_three, precision=highest) + down_b[:, None]
            output = hidden + feed
            stats = jnp.stack([jnp.sum(weights_mask * lax.optimization_barrier(jnp.sum(sample * sample, axis=0))), jnp.sum(weights_mask * lax.optimization_barrier(jnp.sum(branch * branch, axis=0))), jnp.sum(weights_mask * lax.optimization_barrier(jnp.sum(feed * feed, axis=0)))])
            return (output, stats)

        def scan_step(carry, item):
            output, stats = jax.checkpoint(context)(item[0], item[1])
            return (carry + stats, output)
        totals, outputs = lax.scan(scan_step, jnp.zeros((3,), jnp.float32), (contexts, masks))
        return (outputs, totals)
    primal_out, pullback, totals = jax.vjp(forward, *params, samples, has_aux=True)
    upstream = jnp.moveaxis(cotangent.astype(jnp.float32), 1, 0) * masks[:, None, :]
    grads = pullback(upstream)
    result = jnp.moveaxis(primal_out, 0, 1).astype(jnp.bfloat16)
    grad_inputs = jnp.moveaxis(grads[14], 0, 1)
    count = jnp.sum(masks)
    rms = jnp.sqrt(totals / (count * D))
    return (result, grad_inputs, grads[0], grads[1], grads[2], grads[3], grads[4], grads[5], grads[6], grads[7], grads[8], grads[9], grads[10], grads[11], grads[12], grads[13], rms[0], rms[1], rms[2])
```

```python
import functools

import jax
import jax.numpy as jnp
from jax import lax
from jax.experimental import pallas as pl
from jax.experimental.pallas import tpu as pltpu
from jax.sharding import PartitionSpec as P

D = 1024
epsilon = 1e-05
CHUNK = 128
f32 = jnp.float32
bf16 = jnp.bfloat16


def contract(left, right, left_dim, right_dim):
    return lax.dot_general(
        left, right, (((left_dim,), (right_dim,)), ((), ())), preferred_element_type=f32
    )


def nt(left, right):
    return lax.dot_general(left, right, (((1,), (1,)), ((), ())), preferred_element_type=f32)


def nn(left, right):
    return lax.dot_general(left, right, (((1,), (0,)), ((), ())), preferred_element_type=f32)


def tn(left, right):
    return lax.dot_general(left, right, (((0,), (0,)), ((), ())), preferred_element_type=f32)


def gelu_pair(v):
    k0 = 0.7978845608028654
    k1 = 0.044715
    square = v * v
    t = jnp.tanh(k0 * v * (1.0 + k1 * square))
    half = 0.5 * (1.0 + t)
    return v * half, half + 0.5 * v * (1.0 - t * t) * k0 * (1.0 + 3.0 * k1 * square)


def cmul(a, b):
    return (a[0] * b[0] - a[1] * b[1], a[0] * b[1] + a[1] * b[0])


def cadd(a, b):
    return (a[0] + b[0], a[1] + b[1])


def discretized(step, decay, freq):
    return step[:, None] * (-decay), step[:, None] * freq


def coefficients(step, decay, freq, out_real, out_imag):
    a_real, a_imag = -decay, freq
    w_real, w_imag = discretized(step, decay, freq)
    growth = jnp.exp(w_real)
    minus_real = growth * jnp.cos(w_imag) - 1.0
    minus_imag = growth * jnp.sin(w_imag)
    modulus = a_real * a_real + a_imag * a_imag
    ratio_real = (minus_real * a_real + minus_imag * a_imag) / modulus
    ratio_imag = (minus_imag * a_real - minus_real * a_imag) / modulus
    return (
        out_real * ratio_real - out_imag * ratio_imag,
        out_real * ratio_imag + out_imag * ratio_real,
    )


def power(w, exponent):
    envelope = jnp.exp(w[0] * exponent)
    return envelope * jnp.cos(w[1] * exponent), envelope * jnp.sin(w[1] * exponent)


def states_kernel(u_ref, e2_ref, q_ref):
    for i in range(u_ref.shape[0]):
        q_ref[i] = nt(u_ref[i], e2_ref[i])


def toeplitz(taps):
    size = taps.shape[-1]
    rolled = pltpu.roll(
        jnp.broadcast_to(taps, (size, size)), 0, 1, stride=1, stride_axis=0
    )
    rows = lax.broadcasted_iota(jnp.int32, (size, size), 0)
    lanes = lax.broadcasted_iota(jnp.int32, (size, size), 1)
    return jnp.where(lanes >= rows, rolled, 0.0).astype(bf16)


def mix_kernel(u_ref, x_ref, e1_ref, taps_ref, skip_ref, mixed_ref, lifted_ref):
    for i in range(u_ref.shape[0]):
        u = u_ref[i]
        y = nn(u, toeplitz(taps_ref[i : i + 1, :]))
        y = y + nn(x_ref[i].astype(bf16), e1_ref[i])
        mixed = (y + skip_ref[i : i + 1, :] * u.astype(f32)).astype(bf16)
        mixed_ref[i] = mixed
        lifted_ref[i] = gelu_pair(mixed.astype(f32))[0].astype(bf16)


def adjoint_kernel(g_ref, u_ref, e1_ref, e2_ref, p_ref, pa_ref, qp_ref, diag_ref, skip_ref):
    size = g_ref.shape[2]
    rows = g_ref.shape[1]
    lanes = lax.broadcasted_iota(jnp.int32, (rows, size), 1).astype(f32)
    row_id = lax.broadcasted_iota(jnp.int32, (size, size), 0)
    lane_id = lax.broadcasted_iota(jnp.int32, (size, size), 1)
    keep = lane_id <= row_id
    flip = jnp.where(lane_id + row_id == size - 1, 1.0, 0.0).astype(bf16)
    for i in range(g_ref.shape[0]):
        g = g_ref[i]
        u = u_ref[i]
        gf = g.astype(f32)
        uf = u.astype(f32)
        p_ref[i] = nt(g, e1_ref[i])
        pa_ref[i] = nt((gf * lanes).astype(bf16), e1_ref[i])
        qp_ref[i] = nt((uf * lanes).astype(bf16), e2_ref[i])
        outer = tn(nn(u, flip).astype(bf16), g)
        rolled = pltpu.roll(outer, 1, 1, stride=1, stride_axis=0)
        diag_ref[i : i + 1, :] = jnp.sum(jnp.where(keep, rolled, 0.0), axis=0, keepdims=True)
        skip_ref[i : i + 1, :] = jnp.sum(gf * uf, axis=0, keepdims=True)


def back_kernel(g_ref, x_ref, e2_ref, taps_ref, skip_ref, out_ref):
    for i in range(g_ref.shape[0]):
        g = g_ref[i]
        y = nt(g, toeplitz(taps_ref[i : i + 1, :]))
        y = y + nn(x_ref[i].astype(bf16), e2_ref[i])
        out_ref[i] = (y + skip_ref[i : i + 1, :] * g.astype(f32)).astype(bf16)


def by_channel(kernel, block, args, outs, flops):
    channels = args[0].shape[0]
    block = min(block, channels)

    def spec(shape):
        rest = len(shape) - 1
        return pl.BlockSpec((block,) + tuple(shape[1:]), lambda i: (i,) + (0,) * rest)

    moved = sum(a.size * a.dtype.itemsize for a in args) + sum(
        o.size * o.dtype.itemsize for o in outs
    )
    return pl.pallas_call(
        kernel,
        grid=(channels // block,),
        in_specs=[spec(a.shape) for a in args],
        out_specs=[spec(o.shape) for o in outs],
        out_shape=outs,
        compiler_params=pltpu.CompilerParams(vmem_limit_bytes=40 * 1024 * 1024),
        cost_estimate=pl.CostEstimate(flops=flops, bytes_accessed=moved, transcendentals=0),
    )(*args)


def swap(values, axis, bit):
    size = lax.axis_size(axis)
    return lax.ppermute(values, axis, [(i, i ^ bit) for i in range(size)])


def take(values, index):
    return lax.dynamic_index_in_dim(values, index, 0, keepdims=False)


def scattered_sum(blocks, axis):
    size = lax.axis_size(axis)
    me = lax.axis_index(axis)
    bit = 1
    while bit < size:
        pairs = blocks.reshape((blocks.shape[0] // 2, 2) + blocks.shape[1:]).swapaxes(0, 1)
        mine = (me // bit) % 2
        there = swap(take(pairs, 1 - mine), axis, bit)
        blocks = (take(pairs, mine).astype(f32) + there.astype(f32)).astype(bf16)
        bit *= 2
    return blocks[0]


def gathered(block, axis):
    size = lax.axis_size(axis)
    me = lax.axis_index(axis)
    blocks = block[None]
    bit = size // 2
    while bit >= 1:
        there = swap(blocks, axis, bit)
        mine = (me // bit) % 2
        first = jnp.where(mine == 0, blocks, there)
        second = jnp.where(mine == 0, there, blocks)
        blocks = jnp.stack([first, second], axis=1).reshape((-1,) + block.shape)
        bit //= 2
    return blocks


def axis_total(values, axis):
    bit = 1
    while bit < lax.axis_size(axis):
        values = jax.tree.map(lambda v: v + swap(v, axis, bit), values)
        bit *= 2
    return values


def weight_total(terms):
    shape = terms.shape[1:]
    seq, mp = lax.axis_size("seq"), lax.axis_size("mp")
    parts = terms.reshape(mp, seq, -1, shape[-1])
    parts = scattered_sum(parts.swapaxes(0, 1), "seq")
    part = scattered_sum(parts, "mp")
    return gathered(part, "seq").reshape(shape).astype(f32)


def shards(
    inputs,
    valid,
    cotangent,
    first_gain,
    step_size,
    decay_rate,
    frequency,
    readout_real,
    readout_imag,
    skip_weight,
    gated_weight,
    gated_bias,
    second_gain,
    expand_weight,
    expand_bias,
    shrink_weight,
    shrink_bias,
):
    mp = lax.axis_size("mp")
    seq = lax.axis_size("seq")
    mp_me = lax.axis_index("mp")
    seq_me = lax.axis_index("seq")
    features, contexts, local = inputs.shape
    chunk = min(CHUNK, local)
    chunks = local // chunk
    rows = contexts * chunks
    modes = decay_rate.shape[1]
    own_contexts = contexts // mp
    tokens = own_contexts * local

    def exchanged(values):
        moved = lax.all_to_all(values, "mp", 0, 0, tiled=True)
        moved = moved.reshape(mp, own_contexts, features, local).swapaxes(1, 2)
        return moved.reshape(mp * features, tokens)

    def returned(values):
        moved = values.reshape(mp, features, own_contexts, local).swapaxes(1, 2)
        moved = moved.reshape(mp * own_contexts, features, local)
        return lax.all_to_all(moved, "mp", 0, 0, tiled=True)

    def to_rows(values):
        return values.reshape(features, rows, chunk)

    def rows_to_tokens(values):
        return exchanged(values.reshape(features, contexts, local).swapaxes(0, 1))

    def tokens_to_rows(values):
        return to_rows(returned(values).swapaxes(0, 1))

    whole_gated = lax.all_gather(gated_weight, "mp", axis=0)
    whole_expand = lax.all_gather(expand_weight, "mp", axis=0)
    whole_shrink = lax.all_gather(shrink_weight, "mp", axis=0)
    small = lax.all_gather(
        jnp.concatenate(
            [gated_bias.reshape(-1), second_gain, expand_bias, shrink_bias]
        ),
        "mp",
        axis=0,
    )
    cut = [0, 2 * features]
    cut += [cut[-1] + features]
    cut += [cut[-1] + expand_bias.shape[0]]
    whole_gated_bias = small[:, : cut[1]].reshape(mp, 2, features).swapaxes(0, 1).reshape(2, D)
    whole_gain_two = small[:, cut[1] : cut[2]].reshape(D)
    whole_expand_bias = small[:, cut[2] : cut[3]].reshape(-1)
    whole_shrink_bias = small[:, cut[3] :].reshape(D)
    gated_flat = whole_gated.transpose(2, 1, 0, 3).reshape(2, D, D)
    expand_flat = whole_expand.swapaxes(0, 1).reshape(D, -1)
    shrink_flat = whole_shrink.reshape(-1, D)

    residual = to_rows(inputs).astype(f32)
    square_one = axis_total(jnp.sum(residual * residual, axis=0), "mp")
    scale_one = lax.rsqrt(square_one / D + epsilon)
    normed_one = (residual * scale_one * first_gain[:, None, None]).astype(bf16)

    w = discretized(step_size, decay_rate, frequency)
    coeff = coefficients(step_size, decay_rate, frequency, readout_real, readout_imag)
    places = jnp.arange(chunk, dtype=f32)
    wide = (w[0][:, :, None], w[1][:, :, None])
    ahead = power(wide, places + 1.0)
    behind = power(wide, chunk - 1.0 - places)
    level = power(wide, places)
    taps = 2.0 * jnp.sum(
        coeff[0][:, :, None] * level[0] - coeff[1][:, :, None] * level[1], axis=1
    )
    table_one = jnp.concatenate(ahead, axis=1).astype(bf16)
    table_two = jnp.concatenate(behind, axis=1).astype(bf16)
    z_chunk = power(w, float(chunk))
    z_chunks = [power(w, float(chunk * i)) for i in range(chunks + 1)]
    double = (2.0 * coeff[0], 2.0 * coeff[1])

    def halves(values):
        values = values.reshape(features, contexts, chunks, 2 * modes)
        return values[..., :modes], values[..., modes:]

    def per_mode(pair):
        return pair[0][:, None], pair[1][:, None]

    def scan(terms, backward):
        order = range(chunks - 1, -1, -1) if backward else range(chunks)
        state = (jnp.zeros((features, contexts, modes), f32),) * 2
        before = [None] * chunks
        for i in order:
            before[i] = state
            state = cadd(
                cmul(per_mode(z_chunk), state), (terms[0][:, :, i], terms[1][:, :, i])
            )
        return before, state

    def incoming(end, backward):
        gathered_ends = lax.all_gather(jnp.stack(end), "seq", axis=0)
        total = (jnp.zeros_like(end[0]),) * 2
        for k in range(seq):
            gap = (k - seq_me - 1) if backward else (seq_me - 1 - k)
            factor = power(w, jnp.maximum(gap, 0).astype(f32) * local)
            keep = (gap >= 0).astype(f32)
            factor = (keep * factor[0], keep * factor[1])
            total = cadd(total, cmul(per_mode(factor), (gathered_ends[k, 0], gathered_ends[k, 1])))
        return total

    def spread(before, into, backward):
        states = []
        for i in range(chunks):
            gap = chunks - 1 - i if backward else i
            states.append(cadd(before[i], cmul(per_mode(z_chunks[gap]), into)))
        return (
            jnp.stack([s[0] for s in states], axis=2),
            jnp.stack([s[1] for s in states], axis=2),
        )

    def scaled(states):
        pair = cmul((double[0][:, None, None], double[1][:, None, None]), states)
        return jnp.concatenate([pair[0], -pair[1]], axis=-1).reshape(features, rows, 2 * modes)

    def out(shape, dtype):
        return jax.ShapeDtypeStruct(shape, dtype)

    block = 16
    state_shape = out((features, rows, 2 * modes), f32)
    row_shape = out((features, rows, chunk), bf16)
    skip_wide = jnp.broadcast_to(skip_weight[:, None], (features, chunk))
    (terms,) = by_channel(
        states_kernel, block, (normed_one, table_two), [state_shape], features * rows * 16384
    )
    before, end = scan(halves(terms), False)
    states = spread(before, incoming(end, False), False)
    mixed, lifted_one = by_channel(
        mix_kernel,
        block,
        (normed_one, scaled(states), table_one, taps, skip_wide),
        [row_shape, row_shape],
        features * rows * 65536,
    )

    whole_residual = exchanged(inputs.swapaxes(0, 1)).astype(f32)
    own_valid = lax.dynamic_slice_in_dim(valid, mp_me * own_contexts, own_contexts, 0)
    own_valid = own_valid.reshape(tokens).astype(f32)
    upstream = exchanged(cotangent.swapaxes(0, 1)) * own_valid.astype(bf16)
    upstream_f = upstream.astype(f32)
    whole_one = rows_to_tokens(lifted_one)
    value_part = contract(gated_flat[0], whole_one, 0, 0) + whole_gated_bias[0][:, None]
    gate_part = contract(gated_flat[1], whole_one, 0, 0) + whole_gated_bias[1][:, None]
    opening = jax.nn.sigmoid(gate_part)
    branch = value_part * opening
    hidden = whole_residual + branch
    scale_two = lax.rsqrt(jnp.sum(hidden * hidden, axis=0) / D + epsilon)
    normed_two = (hidden * scale_two * whole_gain_two[:, None]).astype(bf16)
    expanded = contract(expand_flat, normed_two, 0, 0) + whole_expand_bias[:, None]
    lifted_three = gelu_pair(expanded)[0].astype(bf16)
    feed = contract(shrink_flat, lifted_three, 0, 0) + whole_shrink_bias[:, None]
    result = returned((hidden + feed).astype(bf16)).swapaxes(0, 1)

    grad_shrink = contract(lifted_three, upstream, 1, 1)
    grad_shrink_bias = jnp.sum(upstream_f, axis=1)
    grad_lifted_three = contract(shrink_flat, upstream, 1, 0)
    grad_expanded = (grad_lifted_three * gelu_pair(expanded)[1]).astype(bf16)
    grad_expand_bias = jnp.sum(grad_expanded.astype(f32), axis=1)
    grad_expand = contract(normed_two, grad_expanded, 1, 1)
    grad_normed_two = contract(expand_flat, grad_expanded, 1, 0)
    grad_second_gain = jnp.sum(grad_normed_two * hidden * scale_two, axis=1)
    inner_two = grad_normed_two * whole_gain_two[:, None]
    dot_two = jnp.sum(inner_two * hidden, axis=0)
    grad_hidden = (
        scale_two * inner_two
        - hidden * (scale_two * scale_two * scale_two) * dot_two / D
        + upstream_f
    )
    grad_value = (grad_hidden * opening).astype(bf16)
    grad_gate = (grad_hidden * value_part * opening * (1.0 - opening)).astype(bf16)
    grad_gated_bias = jnp.stack(
        [jnp.sum(grad_value.astype(f32), axis=1), jnp.sum(grad_gate.astype(f32), axis=1)]
    )
    grad_gated = (
        contract(whole_one, grad_value, 1, 1),
        contract(whole_one, grad_gate, 1, 1),
    )
    grad_lifted_one = contract(gated_flat[0], grad_value, 1, 0) + contract(
        gated_flat[1], grad_gate, 1, 0
    )
    own_lifted_one = tokens_to_rows(grad_lifted_one.astype(bf16)).astype(f32)
    own_hidden = tokens_to_rows(grad_hidden.astype(bf16)).astype(f32)

    grad_mixed = (own_lifted_one * gelu_pair(mixed.astype(f32))[1]).astype(bf16)
    line_shape = out((features, chunk), f32)
    adj, adj_a, state_p, diagonal, skip_terms = by_channel(
        adjoint_kernel,
        block,
        (grad_mixed, normed_one, table_one, table_two),
        [state_shape, state_shape, state_shape, line_shape, line_shape],
        features * rows * 131072,
    )
    adj_terms = halves(adj)
    adj_before, adj_end = scan(adj_terms, True)
    adjoint = spread(adj_before, incoming(adj_end, True), True)
    (grad_normed_rows,) = by_channel(
        back_kernel,
        block,
        (grad_mixed, scaled(adjoint), table_two, taps, skip_wide),
        [row_shape],
        features * rows * 65536,
    )
    intra = (level[0] * diagonal[:, None], level[1] * diagonal[:, None])
    sum_a = [
        jnp.sum(p, axis=(1, 2)) + jnp.sum(q, axis=2)
        for p, q in zip(cmul(adj_terms, states), intra)
    ]
    wide_chunk = (z_chunk[0][:, None, None], z_chunk[1][:, None, None])
    here = cadd(adj_terms, cmul(wide_chunk, adjoint))
    crossing = cmul(here, states)
    part_a = cmul(halves(adj_a), states)
    part_p = cmul(halves(state_p), adjoint)
    sum_b = [
        jnp.sum(float(chunk) * c + a - p, axis=(1, 2)) + jnp.sum(q * places, axis=2)
        for c, a, p, q in zip(crossing, part_a, part_p, intra)
    ]
    grad_skip = jnp.sum(skip_terms, axis=1)

    grad_normed_one = grad_normed_rows.astype(f32)
    inner_one = grad_normed_one * first_gain[:, None, None]
    grad_first_gain = jnp.sum(grad_normed_one * residual * scale_one, axis=(1, 2))
    dot_one = axis_total(jnp.sum(inner_one * residual, axis=0), "mp")
    grad_inputs = (
        scale_one * inner_one
        - residual * (scale_one * scale_one * scale_one) * dot_one / D
        + own_hidden
    ).reshape(features, contexts, local)

    hidden_all = expand_flat.shape[1]
    hidden_own = hidden_all // mp
    grad_shrink = weight_total(grad_shrink.reshape(mp, hidden_own, D).astype(bf16))
    grad_expand = weight_total(
        grad_expand.astype(bf16).reshape(D, mp, hidden_own).swapaxes(0, 1)
    )
    grad_gated = weight_total(
        jnp.stack(grad_gated, axis=1)
        .astype(bf16)
        .reshape(2 * D, mp, features)
        .swapaxes(0, 1)
    ).reshape(D, 2, features)
    stats = jnp.stack(
        [
            jnp.sum(own_valid * jnp.sum(whole_residual * whole_residual, axis=0)),
            jnp.sum(own_valid * jnp.sum(branch * branch, axis=0)),
            jnp.sum(own_valid * jnp.sum(feed * feed, axis=0)),
            jnp.sum(own_valid),
        ]
    )
    bias_terms = jnp.concatenate(
        [
            grad_gated_bias.reshape(2, mp, features).swapaxes(0, 1).reshape(mp, -1),
            grad_second_gain.reshape(mp, -1),
            grad_expand_bias.reshape(mp, -1),
            grad_shrink_bias.reshape(mp, -1),
            jnp.broadcast_to(stats, (mp, 4)),
        ],
        axis=1,
    )
    bias_own = lax.dynamic_index_in_dim(axis_total(bias_terms, "mp"), mp_me, 0, keepdims=False)
    bias_own, grad_first_gain, grad_skip, sum_a, sum_b = axis_total(
        (bias_own, grad_first_gain, grad_skip, sum_a, sum_b), "seq"
    )

    def form(step, decay, freq, out_real, out_imag):
        c = coefficients(step, decay, freq, out_real, out_imag)
        moved = cmul(coeff, discretized(step, decay, freq))
        return 2.0 * jnp.sum(
            c[0] * sum_a[0] - c[1] * sum_a[1] + moved[0] * sum_b[0] - moved[1] * sum_b[1]
        )

    kernel_grads = jax.grad(form, argnums=(0, 1, 2, 3, 4))(
        step_size, decay_rate, frequency, readout_real, readout_imag
    )
    totals = bias_own[cut[3] + features :]
    count = totals[3]
    rms = jnp.sqrt(totals[:3] / (count * D))
    return (
        result,
        grad_inputs,
        grad_first_gain,
        *kernel_grads,
        grad_skip,
        grad_gated,
        bias_own[: cut[1]].reshape(2, features),
        bias_own[cut[1] : cut[2]],
        grad_expand,
        bias_own[cut[2] : cut[3]],
        grad_shrink,
        bias_own[cut[3] : cut[3] + features],
        rms[0],
        rms[1],
        rms[2],
    )


def solution(mesh):
    placed = (
        P("mp", None, "seq"),
        P(None, "seq"),
        P("mp", None, "seq"),
        P("mp"),
        P("mp"),
        P("mp", None),
        P("mp", None),
        P("mp", None),
        P("mp", None),
        P("mp"),
        P(None, None, "mp"),
        P(None, "mp"),
        P("mp"),
        P(None, "mp"),
        P("mp"),
        P("mp", None),
        P("mp"),
    )
    return jax.shard_map(
        shards,
        mesh=mesh,
        in_specs=placed,
        out_specs=(
            P("mp", None, "seq"),
            P("mp", None, "seq"),
            P("mp"),
            P("mp"),
            P("mp", None),
            P("mp", None),
            P("mp", None),
            P("mp", None),
            P("mp"),
            P(None, None, "mp"),
            P(None, "mp"),
            P("mp"),
            P(None, "mp"),
            P("mp"),
            P("mp", None),
            P("mp"),
            P(),
            P(),
            P(),
        ),
        check_vma=False,
    )
```

```python
import functools

import jax
import jax.numpy as jnp
from jax import lax
from jax.experimental import pallas as pl
from jax.experimental.pallas import tpu as pltpu
from jax.sharding import PartitionSpec as P

D = 1024
epsilon = 1e-05
CHUNK = 128
f32 = jnp.float32
bf16 = jnp.bfloat16


def contract(left, right, left_dim, right_dim):
    return lax.dot_general(
        left, right, (((left_dim,), (right_dim,)), ((), ())), preferred_element_type=f32
    )


def nt(left, right):
    return lax.dot_general(left, right, (((1,), (1,)), ((), ())), preferred_element_type=f32)


def nn(left, right):
    return lax.dot_general(left, right, (((1,), (0,)), ((), ())), preferred_element_type=f32)


def tn(left, right):
    return lax.dot_general(left, right, (((0,), (0,)), ((), ())), preferred_element_type=f32)


def gelu_pair(v):
    k0 = 0.7978845608028654
    k1 = 0.044715
    square = v * v
    t = jnp.tanh(k0 * v * (1.0 + k1 * square))
    half = 0.5 * (1.0 + t)
    return v * half, half + 0.5 * v * (1.0 - t * t) * k0 * (1.0 + 3.0 * k1 * square)


def cmul(a, b):
    return (a[0] * b[0] - a[1] * b[1], a[0] * b[1] + a[1] * b[0])


def cadd(a, b):
    return (a[0] + b[0], a[1] + b[1])


def discretized(step, decay, freq):
    return step[:, None] * (-decay), step[:, None] * freq


def coefficients(step, decay, freq, out_real, out_imag):
    a_real, a_imag = -decay, freq
    w_real, w_imag = discretized(step, decay, freq)
    growth = jnp.exp(w_real)
    minus_real = growth * jnp.cos(w_imag) - 1.0
    minus_imag = growth * jnp.sin(w_imag)
    modulus = a_real * a_real + a_imag * a_imag
    ratio_real = (minus_real * a_real + minus_imag * a_imag) / modulus
    ratio_imag = (minus_imag * a_real - minus_real * a_imag) / modulus
    return (
        out_real * ratio_real - out_imag * ratio_imag,
        out_real * ratio_imag + out_imag * ratio_real,
    )


def power(w, exponent):
    envelope = jnp.exp(w[0] * exponent)
    return envelope * jnp.cos(w[1] * exponent), envelope * jnp.sin(w[1] * exponent)


GROUP = 8


def four(pair, axis=-1):
    return jnp.concatenate([pair[0], pair[1], -pair[1], pair[0]], axis=axis)


def turn(values):
    return pltpu.roll(values, values.shape[1] // 2, 1)


def row_of_chunk(shape, chunks):
    return lax.rem(lax.broadcasted_iota(jnp.int32, shape, 0), chunks)


def groups_of(block):
    size = min(GROUP, block)
    return [range(k, k + size) for k in range(0, block, size)]


def scan_rows(states, pars_ref, group, chunks, backward):
    rows = states[0].shape[0]
    place = row_of_chunk(states[0].shape, chunks)
    step, k = 1, 0
    while step < chunks:
        if backward:
            moved = [
                jnp.where(place < chunks - step, pltpu.roll(s, rows - step, 0), 0.0) for s in states
            ]
        else:
            moved = [jnp.where(place >= step, pltpu.roll(s, step, 0), 0.0) for s in states]
        turned = [turn(m) for m in moved]
        states = [
            s + m * pars_ref[i, 2 * k : 2 * k + 1, :] + t * pars_ref[i, 2 * k + 1 : 2 * k + 2, :]
            for i, s, m, t in zip(group, states, moved, turned)
        ]
        step, k = 2 * step, k + 1
    return states


def entered(terms, into, chunks, backward):
    rows, width = terms.shape
    wide = jnp.concatenate(
        [jnp.broadcast_to(into[b : b + 1], (chunks, width)) for b in range(rows // chunks)], axis=0
    )
    if chunks == 1:
        return wide
    place = row_of_chunk(terms.shape, chunks)
    if backward:
        return jnp.where(place == chunks - 1, wide, pltpu.roll(terms, rows - 1, 0))
    return jnp.where(place == 0, wide, pltpu.roll(terms, 1, 0))


def weighed(states, turned, pars_ref, i):
    last = pars_ref.shape[1]
    return (
        states * pars_ref[i, last - 2 : last - 1, :] + turned * pars_ref[i, last - 1 : last, :]
    ).astype(bf16)


def toeplitz(taps):
    size = taps.shape[-1]
    rolled = pltpu.roll(jnp.broadcast_to(taps, (size, size)), 0, 1, stride=1, stride_axis=0)
    rows = lax.broadcasted_iota(jnp.int32, (size, size), 0)
    lanes = lax.broadcasted_iota(jnp.int32, (size, size), 1)
    return jnp.where(lanes >= rows, rolled, 0.0).astype(bf16)


def reversal(size):
    rows = lax.broadcasted_iota(jnp.int32, (size, size), 0)
    lanes = lax.broadcasted_iota(jnp.int32, (size, size), 1)
    return jnp.where(rows + lanes == size - 1, 1.0, 0.0).astype(bf16)


def circle(turns):
    x = (turns - jnp.floor(turns + 0.5)) * 3.14159265358979
    s = x * x
    sine = x * (
        1.0
        + s
        * (
            -1.0 / 6.0
            + s
            * (
                1.0 / 120.0
                + s * (-1.0 / 5040.0 + s * (1.0 / 362880.0 + s * (-1.0 / 39916800.0)))
            )
        )
    )
    cosine = 1.0 + s * (
        -0.5
        + s
        * (
            1.0 / 24.0
            + s
            * (
                -1.0 / 720.0
                + s * (1.0 / 40320.0 + s * (-1.0 / 3628800.0 + s * (1.0 / 479001600.0)))
            )
        )
    )
    return 1.0 - 2.0 * sine * sine, 2.0 * sine * cosine


def tables_kernel(
    chunk, steps, step_ref, decay_ref, freq_ref, real_ref, imag_ref,
    pars_ref, one_ref, two_ref, taps_ref, line_ref,
):
    block, modes = decay_ref.shape
    size = one_ref.shape[2]
    step = step_ref[...]
    a_real, a_imag = -decay_ref[...], freq_ref[...]
    w_real, turns = step * a_real, step * a_imag * 0.15915494309189535

    def z_power(exponent):
        envelope = jnp.exp(w_real * exponent)
        cosine, sine = circle(turns * exponent)
        return envelope * cosine, envelope * sine

    z = z_power(1.0)
    minus_real, minus_imag = z[0] - 1.0, z[1]
    modulus = 1.0 / (a_real * a_real + a_imag * a_imag)
    ratio = (
        (minus_real * a_real + minus_imag * a_imag) * modulus,
        (minus_imag * a_real - minus_real * a_imag) * modulus,
    )
    c = cmul((real_ref[...], imag_ref[...]), ratio)
    lines = []
    for k in range(steps):
        zk = z_power(float(chunk * 2**k))
        lines += [(zk[0], zk[0], zk[0], zk[0]), (zk[1], zk[1], -zk[1], -zk[1])]
    lines += [(c[0], -c[0], -c[0], c[0]), (c[1], -c[1], c[1], -c[1])]
    for k, line in enumerate(lines):
        pars_ref[:, k, :] = jnp.concatenate(line, axis=-1)
    line_ref[...] = jnp.zeros_like(line_ref)
    for k, line in enumerate((w_real, turns, c[0], c[1], z[0], z[1])):
        line_ref[:, k, 0:modes] = line
    places = lax.broadcasted_iota(jnp.int32, (modes, size), 1).astype(f32)
    flip = reversal(size)
    for i in range(block):
        cols = line_ref[i].T

        def col(k):
            return jnp.broadcast_to(cols[:modes, k : k + 1], (modes, size))

        envelope = jnp.exp(col(0) * places)
        cosine, sine = circle(col(1) * places)
        level = (envelope * cosine, envelope * sine)
        taps_ref[i : i + 1, :] = 2.0 * jnp.sum(
            col(2) * level[0] - col(3) * level[1], axis=0, keepdims=True
        )
        one_ref[i] = four(cmul(level, (col(4), col(5))), 0).astype(bf16)
        two_ref[i] = nn(four(level, 0).astype(bf16), flip).astype(bf16)


def states_kernel(chunks, x_ref, scale_ref, gain_ref, two_ref, pars_ref, u_ref, q_ref, end_ref):
    rows = x_ref.shape[1]
    for group in groups_of(x_ref.shape[0]):
        us = [
            (x_ref[i].astype(f32) * scale_ref[...] * gain_ref[i : i + 1, :]).astype(bf16)
            for i in group
        ]
        qs = [nt(u, two_ref[i]) for i, u in zip(group, us)]
        wholes = scan_rows(qs, pars_ref, group, chunks, False)
        for i, u, q, whole in zip(group, us, qs, wholes):
            u_ref[i] = u
            q_ref[i] = q
            for b in range(rows // chunks):
                last = b * chunks + chunks - 1
                end_ref[i, b : b + 1, :] = whole[last : last + 1, :]


def mix_kernel(
    chunks, u_ref, q_ref, into_ref, one_ref, taps_ref, skip_ref, pars_ref,
    mixed_ref, state_ref, lifted_ref, flat_ref,
):
    block, rows, size = u_ref.shape
    for group in groups_of(block):
        states = [entered(q_ref[i], into_ref[i], chunks, False) for i in group]
        states = scan_rows(states, pars_ref, group, chunks, False)
        for i, s in zip(group, states):
            state_ref[i] = s
        outs = [weighed(s, turn(s), pars_ref, i) for i, s in zip(group, states)]
        near = [nn(u_ref[i], toeplitz(taps_ref[i : i + 1, :])) for i in group]
        ys = [y + nn(o, one_ref[i]) for i, y, o in zip(group, near, outs)]
        mixes = [
            (y + skip_ref[i : i + 1, :] * u_ref[i].astype(f32)).astype(bf16)
            for i, y in zip(group, ys)
        ]
        for i, mixed in zip(group, mixes):
            mixed_ref[i] = mixed
            flat_ref[i * rows : (i + 1) * rows, :] = gelu_pair(mixed.astype(f32))[0]
    for r in range(rows):
        b, j = r // chunks, r % chunks
        lifted_ref[b, :, j * size : (j + 1) * size] = flat_ref[
            pl.ds(r, block, stride=rows), :
        ].astype(bf16)


def ends_kernel(chunks, gl_ref, mixed_ref, one_ref, pars_ref, g_ref, p_ref, end_ref, flat_ref):
    block, rows, size = mixed_ref.shape
    for r in range(rows):
        b, j = r // chunks, r % chunks
        flat_ref[pl.ds(r, block, stride=rows), :] = gl_ref[
            b, :, j * size : (j + 1) * size
        ].astype(f32)
    for group in groups_of(block):
        gs = [
            (
                flat_ref[i * rows : (i + 1) * rows, :] * gelu_pair(mixed_ref[i].astype(f32))[1]
            ).astype(bf16)
            for i in group
        ]
        ps = [nt(g, one_ref[i]) for i, g in zip(group, gs)]
        wholes = scan_rows(ps, pars_ref, group, chunks, True)
        for i, g, p, whole in zip(group, gs, ps, wholes):
            g_ref[i] = g
            p_ref[i] = p
            for b in range(rows // chunks):
                end_ref[i, b : b + 1, :] = whole[b * chunks : b * chunks + 1, :]


def summed(values):
    return jnp.sum(values, axis=0, keepdims=True)


def sums_kernel(g_ref, u_ref, state_ref, p_ref, one_ref, sum_ref):
    block, rows, size = g_ref.shape
    lanes = lax.broadcasted_iota(jnp.int32, (rows, size), 1).astype(f32)
    row_id = lax.broadcasted_iota(jnp.int32, (size, size), 0)
    lane_id = lax.broadcasted_iota(jnp.int32, (size, size), 1)
    places = lane_id[0:1].astype(f32)
    keep = lane_id <= row_id
    flip = reversal(size)
    for group in groups_of(block):
        flipped = [nt(flip, u_ref[i]).astype(bf16) for i in group]
        pas = [nt((g_ref[i].astype(f32) * lanes).astype(bf16), one_ref[i]) for i in group]
        outers = [nn(f, g_ref[i]) for i, f in zip(group, flipped)]
        lags = [
            summed(jnp.where(keep, pltpu.roll(o, 1, 1, stride=1, stride_axis=0), 0.0))
            for o in outers
        ]
        stacked = []
        for lag in lags:
            parts = []
            for v in (lag, lag * places):
                high = v.astype(bf16).astype(f32)
                parts += [high, v - high]
            stacked += [
                jnp.concatenate(parts + [jnp.zeros((4, size), f32)], axis=0).astype(bf16)
            ]
        withins = [nt(s, one_ref[i]) for i, s in zip(group, stacked)]
        for i, pa, within in zip(group, pas, withins):
            states = state_ref[i]
            p = p_ref[i]
            sum_ref[i, 0:1, :] = summed(states * p)
            sum_ref[i, 1:2, :] = summed(states * turn(p))
            sum_ref[i, 2:3, :] = summed(states * pa)
            sum_ref[i, 3:4, :] = summed(states * turn(pa))
            sum_ref[i, 4:5, :] = within[0:1] + within[1:2]
            sum_ref[i, 5:6, :] = within[2:3] + within[3:4]
            sum_ref[i, 6:7, :] = summed(g_ref[i].astype(f32) * u_ref[i].astype(f32))
            sum_ref[i, 7:8, :] = jnp.zeros((1, size), f32)


def back_kernel(
    chunks, g_ref, p_ref, into_ref, u_ref, state_ref, two_ref, taps_ref, skip_ref, pars_ref,
    out_ref, sum_ref, flat_ref,
):
    block, rows, size = g_ref.shape
    lanes = lax.broadcasted_iota(jnp.int32, (rows, size), 1).astype(f32)
    for group in groups_of(block):
        qps = [nt((u_ref[i].astype(f32) * lanes).astype(bf16), two_ref[i]) for i in group]
        near = [nt(g_ref[i], toeplitz(taps_ref[i : i + 1, :])) for i in group]
        adjoints = [entered(p_ref[i], into_ref[i], chunks, True) for i in group]
        adjoints = scan_rows(adjoints, pars_ref, group, chunks, True)
        turned = [turn(a) for a in adjoints]
        outs = [weighed(a, t, pars_ref, i) for i, a, t in zip(group, adjoints, turned)]
        ys = [y + nn(o, two_ref[i]) for i, y, o in zip(group, near, outs)]
        for i, y, qp, adjoint, t in zip(group, ys, qps, adjoints, turned):
            flat_ref[i * rows : (i + 1) * rows, :] = y + skip_ref[i : i + 1, :] * g_ref[i].astype(
                f32
            )
            states = state_ref[i]
            here = p_ref[i] + adjoint * pars_ref[i, 0:1, :] + t * pars_ref[i, 1:2, :]
            sum_ref[i, 0:1, :] = summed(states * here)
            sum_ref[i, 1:2, :] = summed(states * turn(here))
            sum_ref[i, 2:3, :] = summed(adjoint * qp)
            sum_ref[i, 3:4, :] = summed(adjoint * turn(qp))
            sum_ref[i, 4:8, :] = jnp.zeros((4, size), f32)
    for r in range(rows):
        b, j = r // chunks, r % chunks
        out_ref[b, :, j * size : (j + 1) * size] = flat_ref[
            pl.ds(r, block, stride=rows), :
        ].astype(bf16)


def over_blocks(kernel, steps, args, outs, us, scratch=(), ties=(), vmem=40):
    count = len(args)

    def run(*refs):
        kernel(*refs[:count], *refs[count + len(ties) :])

    moved = sum(a.size * a.dtype.itemsize for a, _, _ in args + outs)
    return pl.pallas_call(
        run,
        grid=(steps,),
        in_specs=[pl.BlockSpec(b, m) for _, b, m in args]
        + [pl.BlockSpec(memory_space=pl.ANY) for _ in ties],
        out_specs=[pl.BlockSpec(b, m) for _, b, m in outs],
        out_shape=[o for o, _, _ in outs],
        scratch_shapes=list(scratch),
        compiler_params=pltpu.CompilerParams(vmem_limit_bytes=vmem * 1024 * 1024),
        cost_estimate=pl.CostEstimate(
            flops=int(us * 1e9), bytes_accessed=moved, transcendentals=0
        ),
    )(*[a for a, _, _ in args], *ties)


def along(array, dim, block):
    shape = array.shape
    if dim is None:
        return (array, tuple(shape), lambda i: (0,) * len(shape))
    sizes = tuple(block if d == dim else size for d, size in enumerate(shape))
    return (array, sizes, lambda i: tuple(i if d == dim else 0 for d in range(len(shape))))


def by_channel(kernel, block, channels, args, outs, us, scratch=(), ties=()):
    return over_blocks(
        kernel,
        channels // block,
        [along(a, d, block) for a, d in args],
        [along(o, d, block) for o, d in outs],
        us,
        scratch,
        ties,
    )


def lane_sums(values):
    width = min(128, values.shape[1])
    total = values[:, :width]
    for k in range(1, values.shape[1] // width):
        total = total + values[:, k * width : (k + 1) * width]
    return total


def gated_kernel(
    x_ref, residual_ref, value_w_ref, gate_w_ref, value_b_ref, gate_b_ref, gain_ref,
    hidden_ref, normed_ref, value_ref, opening_ref, line_ref,
):
    x = x_ref[...]
    value = nn(value_w_ref[...], x) + value_b_ref[:, 0:1]
    gate = nn(gate_w_ref[...], x) + gate_b_ref[:, 0:1]
    opening = 1.0 / (1.0 + jnp.exp(-gate))
    branch = value * opening
    residual = residual_ref[...].astype(f32)
    hidden = residual + branch
    features = hidden.shape[0]
    scale = lax.rsqrt(summed(hidden * hidden) / features + epsilon)
    hidden_ref[...] = hidden
    value_ref[...] = value
    opening_ref[...] = opening
    normed_ref[...] = (hidden * scale * gain_ref[:, 0:1]).astype(bf16)
    line_ref[0:1, :] = scale
    line_ref[1:2, :] = summed(residual * residual)
    line_ref[2:3, :] = summed(branch * branch)
    line_ref[3:8, :] = jnp.zeros((5, hidden.shape[1]), f32)


def hidden_kernel(
    blocks, first, normed_ref, upstream_ref, up_a_ref, up_b_ref, down_a_ref, down_b_ref, bias_ref,
    *refs,
):
    if first:
        feed_out, grad_out, shrink_ref, expand_ref, line_ref, up_ref, down_ref = refs
    else:
        feed_in, grad_in, feed_out, grad_out, shrink_ref, expand_ref, line_ref, up_ref, down_ref = (
            refs
        )
    step = pl.program_id(0)

    @pl.when(step < blocks)
    def _():
        up_ref[...] = up_a_ref[...]
        down_ref[...] = down_a_ref[...]

    @pl.when(step >= blocks)
    def _():
        up_ref[...] = up_b_ref[...]
        down_ref[...] = down_b_ref[...]

    @pl.when(step == 0)
    def _():
        if first:
            feed_out[...] = jnp.zeros_like(feed_out)
            grad_out[...] = jnp.zeros_like(grad_out)
        else:
            feed_out[...] = feed_in[...]
            grad_out[...] = grad_in[...]

    expanded = nn(up_ref[...], normed_ref[...]) + bias_ref[:, 0:1]
    lifted, slope = gelu_pair(expanded)
    lifted = lifted.astype(bf16)
    grad = (nn(down_ref[...], upstream_ref[...]) * slope).astype(bf16)
    shrink_ref[...] = nt(lifted, upstream_ref[...]).astype(bf16)
    expand_ref[...] = nt(grad, normed_ref[...]).astype(bf16)
    line_ref[...] = lane_sums(grad.astype(f32))
    feed_out[...] += tn(down_ref[...], lifted)
    grad_out[...] += tn(up_ref[...], grad)


def gated_back_kernel(
    grad_ref, hidden_ref, value_ref, opening_ref, upstream_ref, feed_ref, x_ref, line_ref,
    value_w_ref, gate_w_ref, gain_ref, shrink_b_ref,
    result_ref, lifted_ref, grad_hidden_ref, value_g_ref, gate_g_ref, sums_ref, feed_line_ref,
    value_t, gate_t,
):
    step = pl.program_id(0)

    @pl.when(step == 0)
    def _():
        value_t[...] = jnp.zeros_like(value_t)
        gate_t[...] = jnp.zeros_like(gate_t)
        sums_ref[...] = jnp.zeros_like(sums_ref)

    hidden = hidden_ref[...]
    features = hidden.shape[0]
    scale = line_ref[0:1, :]
    feed = feed_ref[...] + shrink_b_ref[:, 0:1]
    result_ref[...] = (hidden + feed).astype(bf16)
    feed_line_ref[0:1, :] = summed(feed * feed)
    feed_line_ref[1:8, :] = jnp.zeros((7, hidden.shape[1]), f32)
    grad = grad_ref[...]
    inner = grad * gain_ref[:, 0:1]
    dot = summed(inner * hidden) / features
    upstream = upstream_ref[...].astype(f32)
    grad_hidden = scale * inner - hidden * (scale * scale * scale) * dot + upstream
    grad_hidden_ref[...] = grad_hidden.astype(bf16)
    opening = opening_ref[...]
    grad_value = (grad_hidden * opening).astype(bf16)
    grad_gate = (grad_hidden * value_ref[...] * opening * (1.0 - opening)).astype(bf16)
    sums_ref[0] += lane_sums(grad_value.astype(f32))
    sums_ref[1] += lane_sums(grad_gate.astype(f32))
    sums_ref[2] += lane_sums(grad * hidden * scale)
    sums_ref[3] += lane_sums(upstream)
    lifted_ref[...] = (tn(value_w_ref[...], grad_value) + tn(gate_w_ref[...], grad_gate)).astype(
        bf16
    )
    x = x_ref[...]
    value_t[...] += nt(grad_value, x)
    gate_t[...] += nt(grad_gate, x)

    @pl.when(step == pl.num_programs(0) - 1)
    def _():
        value_g_ref[...] = value_t[...].astype(bf16)
        gate_g_ref[...] = gate_t[...].astype(bf16)


def swap(values, axis, bit):
    size = lax.axis_size(axis)
    return lax.ppermute(values, axis, [(i, i ^ bit) for i in range(size)])


def added(a, b):
    return (a.astype(f32) + b.astype(f32)).astype(bf16)


def axis_total(values, axis):
    bit = 1
    while bit < lax.axis_size(axis):
        values = values + swap(values, axis, bit)
        bit *= 2
    return values


def bits_of(axis):
    return [1 << k for k in range(lax.axis_size(axis).bit_length() - 1)]


def down_step(terms, bit):
    if bit == 0:
        return added(terms[:1], swap(terms[1:], "mp", 2))
    me = lax.axis_index("seq")
    half = terms.shape[1] // 2
    mine = (me // bit) % 2
    kept = lax.dynamic_slice_in_dim(terms, mine * half, half, 1)
    sent = lax.dynamic_slice_in_dim(terms, (1 - mine) * half, half, 1)
    return added(kept, swap(sent, "seq", bit))


def up_step(terms, bit):
    me = lax.axis_index("seq")
    there = swap(terms, "seq", bit)
    first = (me // bit) % 2 == 0
    return jnp.concatenate(
        [jnp.where(first, terms, there), jnp.where(first, there, terms)], axis=1
    )


def shards(
    inputs,
    valid,
    cotangent,
    first_gain,
    step_size,
    decay_rate,
    frequency,
    readout_real,
    readout_imag,
    skip_weight,
    gated_weight,
    gated_bias,
    second_gain,
    expand_weight,
    expand_bias,
    shrink_weight,
    shrink_bias,
):
    mp = lax.axis_size("mp")
    seq = lax.axis_size("seq")
    mp_me = lax.axis_index("mp")
    seq_me = lax.axis_index("seq")
    features, contexts, local = inputs.shape
    chunk = min(CHUNK, local)
    chunks = local // chunk
    rows = contexts * chunks
    modes = decay_rate.shape[1]
    own_contexts = contexts // mp
    tokens = own_contexts * local
    hidden_own = expand_weight.shape[1]
    group = features // seq

    def exchanged(values):
        moved = lax.all_to_all(values, "mp", 0, 0, tiled=True)
        moved = moved.reshape(mp, own_contexts, features, local).swapaxes(1, 2)
        return moved.reshape(mp * features, tokens)

    def returned(values):
        moved = values.reshape(mp, features, own_contexts, local).swapaxes(1, 2)
        moved = moved.reshape(mp * own_contexts, features, local)
        return lax.all_to_all(moved, "mp", 0, 0, tiled=True)

    def all_places(own, upper):
        return own, upper, swap(own, "mp", 1), swap(upper, "mp", 1)

    gated_own = gated_weight.transpose(1, 2, 0)
    gated_places = all_places(gated_own, swap(gated_own, "mp", 2))
    small = jnp.concatenate([gated_bias.reshape(-1), second_gain, expand_bias, shrink_bias])
    small_near = jnp.stack([small, swap(small, "mp", 2)])
    small_places = jnp.concatenate([small_near, swap(small_near, "mp", 1)])
    expand_own = expand_weight.T
    part = hidden_own // seq
    slices = jnp.stack(
        [
            lax.dynamic_slice_in_dim(expand_own, seq_me * part, part, 0),
            lax.dynamic_slice_in_dim(shrink_weight, seq_me * part, part, 0),
        ]
    )
    slices = swap(slices, "mp", 2)
    expand_places = all_places(expand_own, lax.all_gather(slices[0], "seq", axis=0, tiled=True))
    shrink_places = all_places(shrink_weight, lax.all_gather(slices[1], "seq", axis=0, tiled=True))

    index = jnp.arange(mp, dtype=jnp.int32)
    device_of = jnp.bitwise_xor(mp_me, (index // 2) + 2 * (index % 2))
    place_of = jnp.bitwise_xor(mp_me, index)
    place_of = (place_of // 2) + 2 * (place_of % 2)

    def in_order(blocks):
        return jnp.concatenate(
            [lax.dynamic_slice_in_dim(blocks, place_of[k], 1, 0) for k in range(mp)]
        )

    def by_place(blocks):
        near = jnp.concatenate(
            [lax.dynamic_slice_in_dim(blocks, device_of[k], 1, 0) for k in range(2)]
        )
        far = jnp.concatenate(
            [lax.dynamic_slice_in_dim(blocks, device_of[k], 1, 0) for k in range(2, mp)]
        )
        return near, far

    gated_flat = in_order(jnp.stack(gated_places)).swapaxes(0, 1).reshape(2, D, D)
    cut = [0, 2 * features]
    cut += [cut[-1] + features]
    cut += [cut[-1] + hidden_own]
    cut += [cut[-1] + features]
    ordered = in_order(small_places)

    def wide(values):
        return jnp.broadcast_to(values[..., None], values.shape + (128,))

    whole_gated_bias = ordered[:, : cut[1]].reshape(mp, 2, features).swapaxes(0, 1).reshape(2, D)
    value_bias, gate_bias = wide(whole_gated_bias[0]), wide(whole_gated_bias[1])
    whole_gain_two = wide(ordered[:, cut[1] : cut[2]].reshape(D))
    whole_shrink_bias = wide(ordered[:, cut[3] :].reshape(D))
    whole_expand_bias = small_places[:, cut[2] : cut[3]]
    near_bias = wide(whole_expand_bias[:2].reshape(-1))
    far_bias = wide(whole_expand_bias[2:].reshape(-1))

    by_context = inputs.swapaxes(0, 1)
    square_one = axis_total(jnp.sum(jnp.square(by_context.astype(f32)), axis=1), "mp")
    scale_one = lax.rsqrt(square_one / D + epsilon)
    scale_rows = scale_one.reshape(rows, chunk)
    x_rows = inputs.reshape(features, rows, chunk)

    w = discretized(step_size, decay_rate, frequency)
    coeff = coefficients(step_size, decay_rate, frequency, readout_real, readout_imag)
    z_device = power(
        tuple(lax.dynamic_slice_in_dim(v, seq_me * group, group, 0) for v in w), float(local)
    )
    z_device = (z_device[0][:, None], z_device[1][:, None])

    def handed(ends, backward):
        sent = ends[..., : 2 * modes].reshape(features, contexts * 2 * modes)
        terms = lax.all_to_all(sent, "seq", 0, 0, tiled=True)
        terms = terms.reshape(seq, group, contexts, 2 * modes)
        state = (jnp.zeros((group, contexts, modes), f32),) * 2
        states = [None] * seq
        for k in range(seq - 1, -1, -1) if backward else range(seq):
            states[k] = jnp.concatenate(state, axis=-1)
            state = cadd(cmul(z_device, state), (terms[k, ..., :modes], terms[k, ..., modes:]))
        states = jnp.stack(states).reshape(features, contexts * 2 * modes)
        states = lax.all_to_all(states, "seq", 0, 0, tiled=True)
        states = states.reshape(features, contexts, 2 * modes)
        return four((states[..., :modes], states[..., modes:]))

    def out(shape, dtype):
        return jax.ShapeDtypeStruct(shape, dtype)

    block = min(16, features)
    state_shape = out((features, rows, 4 * modes), f32)
    end_shape = out((features, contexts, 4 * modes), f32)
    row_shape = out((features, rows, chunk), bf16)
    context_shape = out((contexts, features, local), bf16)
    table_shape = out((features, 4 * modes, chunk), bf16)
    sum_shape = out((features, 8, 4 * modes), f32)
    line_shape = out((features, chunk), f32)
    flat = [pltpu.VMEM((block * rows, chunk), f32)]
    skip_wide = jnp.broadcast_to(skip_weight[:, None], (features, chunk))
    gain_wide = jnp.broadcast_to(first_gain[:, None], (features, chunk))
    scan_steps = max(1, (chunks - 1).bit_length())
    pars, one, two, taps = by_channel(
        functools.partial(tables_kernel, chunk, scan_steps),
        block,
        features,
        [
            (step_size[:, None], 0),
            (decay_rate, 0),
            (frequency, 0),
            (readout_real, 0),
            (readout_imag, 0),
        ],
        [
            (out((features, 2 * scan_steps + 2, 4 * modes), f32), 0),
            (table_shape, 0),
            (table_shape, 0),
            (line_shape, 0),
        ],
        10,
        [pltpu.VMEM((block, 8, 4 * modes), f32)],
    )
    normed_one, terms, ends = by_channel(
        functools.partial(states_kernel, chunks),
        block,
        features,
        [(x_rows, 0), (scale_rows, None), (gain_wide, 0), (two, 0), (pars, 0)],
        [(row_shape, 0), (state_shape, 0), (end_shape, 0)],
        8,
    )
    mixed, states, lifted_one = by_channel(
        functools.partial(mix_kernel, chunks),
        block,
        features,
        [
            (normed_one, 0),
            (terms, 0),
            (handed(ends, False), 0),
            (one, 0),
            (taps, 0),
            (skip_wide, 0),
            (pars, 0),
        ],
        [(row_shape, 0), (state_shape, 0), (context_shape, 1)],
        14,
        flat,
    )

    whole_residual = exchanged(by_context)
    own_valid = lax.dynamic_slice_in_dim(valid, mp_me * own_contexts, own_contexts, 0)
    own_valid = own_valid.reshape(tokens).astype(f32)
    upstream = exchanged(cotangent.swapaxes(0, 1)) * own_valid.astype(bf16)
    whole_one = exchanged(lifted_one)

    token_block = min(256, tokens)
    token_steps = tokens // token_block
    wide_f = out((D, tokens), f32)
    wide_b = out((D, tokens), bf16)
    line_out = out((8, tokens), f32)

    def by_tokens(kernel, args, outs, us, scratch=(), ties=()):
        return over_blocks(
            kernel,
            token_steps,
            [along(a, d, token_block) for a, d in args],
            [along(o, d, token_block) for o, d in outs],
            us,
            scratch,
            ties,
            56,
        )

    hidden, normed_two, value_part, opening, lines = by_tokens(
        gated_kernel,
        [
            (whole_one, 1),
            (whole_residual, 1),
            (gated_flat[0], None),
            (gated_flat[1], None),
            (value_bias, None),
            (gate_bias, None),
            (whole_gain_two, None),
        ],
        [(wide_f, 1), (wide_b, 1), (wide_f, 1), (wide_f, 1), (line_out, 1)],
        12,
    )

    hidden_block = min(256, hidden_own)
    blocks = hidden_own // hidden_block
    near_rows = 2 * hidden_own

    def by_hidden(up, down, bias, carried, ties=()):
        first = carried is None
        low = ((hidden_block, D), lambda i: (jnp.minimum(i, blocks - 1), 0))
        high = ((hidden_block, D), lambda i: (jnp.maximum(i - blocks, 0), 0))
        args = [
            along(normed_two, None, 0),
            along(upstream, None, 0),
            (up[0], *low),
            (up[1], *high),
            (down[0], *low),
            (down[1], *high),
            along(bias, 0, hidden_block),
        ]
        if not first:
            args += [along(c, None, 0) for c in carried]
        grad_shape = out((near_rows, D), bf16)
        return over_blocks(
            functools.partial(hidden_kernel, blocks, first),
            2 * blocks,
            args,
            [
                along(wide_f, None, 0),
                along(wide_f, None, 0),
                along(grad_shape, 0, hidden_block),
                along(grad_shape, 0, hidden_block),
                along(out((near_rows, min(128, tokens)), f32), 0, hidden_block),
            ],
            35,
            [pltpu.VMEM((hidden_block, D), bf16)] * 2,
            ties,
            60,
        )

    feed, grad_normed_two, shrink_far, expand_far, far_lines = by_hidden(
        expand_places[2:], shrink_places[2:], far_bias, None
    )
    feed, grad_normed_two, shrink_near, expand_near, near_lines = by_hidden(
        expand_places[:2], shrink_places[:2], near_bias, (feed, grad_normed_two)
    )

    sums_out = out((4, D, min(128, token_block)), f32)
    gated_g = out((D, D), bf16)
    result, grad_lifted_one, grad_hidden, value_g, gate_g, sums, feed_lines = by_tokens(
        gated_back_kernel,
        [
            (grad_normed_two, 1),
            (hidden, 1),
            (value_part, 1),
            (opening, 1),
            (upstream, 1),
            (feed, 1),
            (whole_one, 1),
            (lines, 1),
            (gated_flat[0], None),
            (gated_flat[1], None),
            (whole_gain_two, None),
            (whole_shrink_bias, None),
        ],
        [
            (wide_b, 1),
            (wide_b, 1),
            (wide_b, 1),
            (gated_g, None),
            (gated_g, None),
            (sums_out, None),
            (line_out, 1),
        ],
        20,
        [pltpu.VMEM((D, D), f32)] * 2,
    )
    own_lifted_one = returned(grad_lifted_one)
    own_hidden = returned(grad_hidden).astype(f32)
    result = returned(result).swapaxes(0, 1)

    bits = bits_of("seq")

    def weight_total(near, far, order):
        near, far = near.reshape(2, -1, D), far.reshape(2, -1, D)
        terms = added(near, swap(far, "mp", 1))
        for bit in order:
            terms = down_step(terms, bit)
        for bit in [bit for bit in order if bit > 0][::-1]:
            terms = up_step(terms, bit)
        return terms[0].astype(f32)

    rotated = bits[1:] + bits[:1] if len(bits) > 1 else bits
    grad_shrink = weight_total(shrink_near, shrink_far, bits + [0])
    grad_expand = weight_total(expand_near, expand_far, [0] + bits).T
    gated_terms = jnp.stack([value_g.reshape(mp, features, D), gate_g.reshape(mp, features, D)], 1)
    grad_gated = weight_total(
        *by_place(gated_terms.reshape(mp, 2 * features, D)), rotated[:1] + [0] + rotated[1:]
    )
    grad_gated = grad_gated.reshape(2, features, D).transpose(2, 0, 1)

    grad_mixed, adj_terms, adj_ends = by_channel(
        functools.partial(ends_kernel, chunks),
        block,
        features,
        [(own_lifted_one, 1), (mixed, 0), (one, 0), (pars, 0)],
        [(row_shape, 0), (state_shape, 0), (end_shape, 0)],
        10,
        flat,
    )
    (sums_one,) = by_channel(
        sums_kernel,
        block,
        features,
        [(grad_mixed, 0), (normed_one, 0), (states, 0), (adj_terms, 0), (one, 0)],
        [(sum_shape, 0)],
        20,
    )
    grad_normed_one, sums_two = by_channel(
        functools.partial(back_kernel, chunks),
        block,
        features,
        [
            (grad_mixed, 0),
            (adj_terms, 0),
            (handed(adj_ends, True), 0),
            (normed_one, 0),
            (states, 0),
            (two, 0),
            (taps, 0),
            (skip_wide, 0),
            (pars, 0),
        ],
        [(context_shape, 1), (sum_shape, 0)],
        14,
        flat,
    )

    residual = by_context.astype(f32)
    grad_normed_one = grad_normed_one.astype(f32)
    inner_one = grad_normed_one * first_gain[:, None]
    wide_scale = scale_one[:, None, :]
    grad_first_gain = jnp.sum(grad_normed_one * residual * wide_scale, axis=(0, 2))
    dot_one = axis_total(jnp.sum(inner_one * residual, axis=1), "mp")[:, None, :]
    grad_inputs = (
        wide_scale * inner_one
        - residual * (wide_scale * wide_scale * wide_scale) * dot_one / D
        + own_hidden
    ).swapaxes(0, 1)

    stats = jnp.stack(
        [
            jnp.sum(own_valid * lines[1]),
            jnp.sum(own_valid * lines[2]),
            jnp.sum(own_valid * feed_lines[0]),
            jnp.sum(own_valid),
        ]
    )
    sums = jnp.sum(sums, axis=2)
    ordered_terms = jnp.concatenate(
        [
            sums[:2].reshape(2, mp, features).swapaxes(0, 1).reshape(mp, -1),
            sums[2].reshape(mp, -1),
            sums[3].reshape(mp, -1),
            jnp.broadcast_to(stats, (mp, 4)),
        ],
        axis=1,
    )
    near, far = by_place(ordered_terms)
    near = jnp.concatenate([near, jnp.sum(near_lines, axis=1).reshape(2, hidden_own)], axis=1)
    far = jnp.concatenate([far, jnp.sum(far_lines, axis=1).reshape(2, hidden_own)], axis=1)
    near = near + swap(far, "mp", 1)
    bias_own = axis_total((near[:1] + swap(near[1:], "mp", 2))[0], "seq")

    def quarter(values, k):
        return values[:, k * modes : (k + 1) * modes]

    def product_sums(lines, k):
        plain, turned = lines[:, k], lines[:, k + 1]
        return (
            quarter(plain, 0) - quarter(plain, 1),
            quarter(turned, 1) + quarter(turned, 3),
        )

    inverse = power(w, -1.0)
    within = [
        cmul(inverse, (quarter(sums_one[:, k], 0), quarter(sums_one[:, k], 1))) for k in (4, 5)
    ]
    sum_a = cadd(product_sums(sums_one, 0), within[0])
    crossing = product_sums(sums_two, 0)
    part_a = product_sums(sums_one, 2)
    part_p = product_sums(sums_two, 2)
    sum_b = [
        float(chunk) * crossing[k] + part_a[k] - part_p[k] + within[1][k] for k in range(2)
    ]
    late = jnp.concatenate(
        [
            *sum_a,
            *sum_b,
            jnp.sum(sums_one[:, 6], axis=1, keepdims=True),
            grad_first_gain[:, None],
        ],
        axis=1,
    )
    late = axis_total(late, "seq")
    sum_a = (quarter(late, 0), quarter(late, 1))
    sum_b = (quarter(late, 2), quarter(late, 3))
    grad_skip = late[:, 4 * modes]
    grad_first_gain = late[:, 4 * modes + 1]

    def form(step, decay, freq, out_real, out_imag):
        c = coefficients(step, decay, freq, out_real, out_imag)
        moved = cmul(coeff, discretized(step, decay, freq))
        return 2.0 * jnp.sum(
            c[0] * sum_a[0] - c[1] * sum_a[1] + moved[0] * sum_b[0] - moved[1] * sum_b[1]
        )

    kernel_grads = jax.grad(form, argnums=(0, 1, 2, 3, 4))(
        step_size, decay_rate, frequency, readout_real, readout_imag
    )
    ends_at = [0, 2 * features, 3 * features, 4 * features, 4 * features + 4]
    totals = bias_own[ends_at[3] : ends_at[4]]
    count = totals[3]
    rms = jnp.sqrt(totals[:3] / (count * D))
    return (
        result,
        grad_inputs,
        grad_first_gain,
        *kernel_grads,
        grad_skip,
        grad_gated,
        bias_own[: ends_at[1]].reshape(2, features),
        bias_own[ends_at[1] : ends_at[2]],
        grad_expand,
        bias_own[ends_at[4] :],
        grad_shrink,
        bias_own[ends_at[2] : ends_at[3]],
        rms[0],
        rms[1],
        rms[2],
    )


def solution(mesh):
    placed = (
        P("mp", None, "seq"),
        P(None, "seq"),
        P("mp", None, "seq"),
        P("mp"),
        P("mp"),
        P("mp", None),
        P("mp", None),
        P("mp", None),
        P("mp", None),
        P("mp"),
        P(None, None, "mp"),
        P(None, "mp"),
        P("mp"),
        P(None, "mp"),
        P("mp"),
        P("mp", None),
        P("mp"),
    )
    return jax.shard_map(
        shards,
        mesh=mesh,
        in_specs=placed,
        out_specs=(
            P("mp", None, "seq"),
            P("mp", None, "seq"),
            P("mp"),
            P("mp"),
            P("mp", None),
            P("mp", None),
            P("mp", None),
            P("mp", None),
            P("mp"),
            P(None, None, "mp"),
            P(None, "mp"),
            P("mp"),
            P(None, "mp"),
            P("mp"),
            P("mp", None),
            P("mp"),
            P(),
            P(),
            P(),
        ),
        check_vma=False,
    )
```

```python
import functools

import jax
import jax.numpy as jnp
from jax import lax
from jax.experimental import pallas as pl
from jax.experimental.pallas import tpu as pltpu
from jax.sharding import PartitionSpec as P

D = 1024
epsilon = 1e-05
CHUNK = 128
f32 = jnp.float32
bf16 = jnp.bfloat16


def contract(left, right, left_dim, right_dim):
    return lax.dot_general(
        left, right, (((left_dim,), (right_dim,)), ((), ())), preferred_element_type=f32
    )


def nt(left, right):
    return lax.dot_general(left, right, (((1,), (1,)), ((), ())), preferred_element_type=f32)


def nn(left, right):
    return lax.dot_general(left, right, (((1,), (0,)), ((), ())), preferred_element_type=f32)


def tn(left, right):
    return lax.dot_general(left, right, (((0,), (0,)), ((), ())), preferred_element_type=f32)


def gelu_pair(v):
    k0 = 0.7978845608028654
    k1 = 0.044715
    square = v * v
    t = jnp.tanh(k0 * v * (1.0 + k1 * square))
    half = 0.5 * (1.0 + t)
    return v * half, half + 0.5 * v * (1.0 - t * t) * k0 * (1.0 + 3.0 * k1 * square)


def cmul(a, b):
    return (a[0] * b[0] - a[1] * b[1], a[0] * b[1] + a[1] * b[0])


def cadd(a, b):
    return (a[0] + b[0], a[1] + b[1])


def discretized(step, decay, freq):
    return step[:, None] * (-decay), step[:, None] * freq


def coefficients(step, decay, freq, out_real, out_imag):
    a_real, a_imag = -decay, freq
    w_real, w_imag = discretized(step, decay, freq)
    growth = jnp.exp(w_real)
    minus_real = growth * jnp.cos(w_imag) - 1.0
    minus_imag = growth * jnp.sin(w_imag)
    modulus = a_real * a_real + a_imag * a_imag
    ratio_real = (minus_real * a_real + minus_imag * a_imag) / modulus
    ratio_imag = (minus_imag * a_real - minus_real * a_imag) / modulus
    return (
        out_real * ratio_real - out_imag * ratio_imag,
        out_real * ratio_imag + out_imag * ratio_real,
    )


def power(w, exponent):
    envelope = jnp.exp(w[0] * exponent)
    return envelope * jnp.cos(w[1] * exponent), envelope * jnp.sin(w[1] * exponent)


GROUP = 8


def four(pair, axis=-1):
    return jnp.concatenate([pair[0], pair[1], -pair[1], pair[0]], axis=axis)


def turn(values):
    return pltpu.roll(values, values.shape[1] // 2, 1)


def row_of_chunk(shape, chunks):
    return lax.rem(lax.broadcasted_iota(jnp.int32, shape, 0), chunks)


def groups_of(block):
    size = min(GROUP, block)
    return [range(k, k + size) for k in range(0, block, size)]


def moved_rows(values, step, chunks, backward):
    rows, width = values.shape
    if chunks == 8:
        cube = values.reshape(rows // 8, 8, width)
        place = lax.broadcasted_iota(jnp.int32, cube.shape, 1)
        if backward:
            cube = jnp.where(place < 8 - step, pltpu.roll(cube, 8 - step, 1), 0.0)
        else:
            cube = jnp.where(place >= step, pltpu.roll(cube, step, 1), 0.0)
        return cube.reshape(rows, width)
    place = row_of_chunk(values.shape, chunks)
    if backward:
        return jnp.where(place < chunks - step, pltpu.roll(values, rows - step, 0), 0.0)
    return jnp.where(place >= step, pltpu.roll(values, step, 0), 0.0)


def scan_rows(states, pars_ref, group, chunks, backward):
    step, k = 1, 0
    while step < chunks:
        moved = [moved_rows(s, step, chunks, backward) for s in states]
        turned = [turn(m) for m in moved]
        states = [
            s + m * pars_ref[i, 2 * k : 2 * k + 1, :] + t * pars_ref[i, 2 * k + 1 : 2 * k + 2, :]
            for i, s, m, t in zip(group, states, moved, turned)
        ]
        step, k = 2 * step, k + 1
    return states


def entered(terms, into, chunks, backward):
    rows, width = terms.shape
    wide = jnp.concatenate(
        [jnp.broadcast_to(into[b : b + 1], (chunks, width)) for b in range(rows // chunks)], axis=0
    )
    if chunks == 1:
        return wide
    place = row_of_chunk(terms.shape, chunks)
    edge = chunks - 1 if backward else 0
    return jnp.where(place == edge, wide, moved_rows(terms, 1, chunks, backward))


def weighed(states, turned, pars_ref, i):
    last = pars_ref.shape[1]
    return (
        states * pars_ref[i, last - 2 : last - 1, :] + turned * pars_ref[i, last - 1 : last, :]
    ).astype(bf16)


def toeplitz(taps):
    size = taps.shape[-1]
    rolled = pltpu.roll(jnp.broadcast_to(taps, (size, size)), 0, 1, stride=1, stride_axis=0)
    rows = lax.broadcasted_iota(jnp.int32, (size, size), 0)
    lanes = lax.broadcasted_iota(jnp.int32, (size, size), 1)
    return jnp.where(lanes >= rows, rolled, 0.0).astype(bf16)


def reversal(size):
    rows = lax.broadcasted_iota(jnp.int32, (size, size), 0)
    lanes = lax.broadcasted_iota(jnp.int32, (size, size), 1)
    return jnp.where(rows + lanes == size - 1, 1.0, 0.0).astype(bf16)


def circle(turns):
    x = (turns - jnp.floor(turns + 0.5)) * 3.14159265358979
    s = x * x
    sine = x * (
        1.0
        + s
        * (
            -1.0 / 6.0
            + s
            * (
                1.0 / 120.0
                + s * (-1.0 / 5040.0 + s * (1.0 / 362880.0 + s * (-1.0 / 39916800.0)))
            )
        )
    )
    cosine = 1.0 + s * (
        -0.5
        + s
        * (
            1.0 / 24.0
            + s
            * (
                -1.0 / 720.0
                + s * (1.0 / 40320.0 + s * (-1.0 / 3628800.0 + s * (1.0 / 479001600.0)))
            )
        )
    )
    return 1.0 - 2.0 * sine * sine, 2.0 * sine * cosine


def tables_kernel(
    chunk, steps, local, step_ref, decay_ref, freq_ref, real_ref, imag_ref,
    pars_ref, whole_ref, one_ref, two_ref, taps_ref, line_ref,
):
    block, modes = decay_ref.shape
    size = one_ref.shape[2]
    step = step_ref[...]
    a_real, a_imag = -decay_ref[...], freq_ref[...]
    w_real, turns = step * a_real, step * a_imag * 0.15915494309189535

    def z_power(exponent):
        envelope = jnp.exp(w_real * exponent)
        cosine, sine = circle(turns * exponent)
        return envelope * cosine, envelope * sine

    z = z_power(1.0)
    minus_real, minus_imag = z[0] - 1.0, z[1]
    modulus = 1.0 / (a_real * a_real + a_imag * a_imag)
    ratio = (
        (minus_real * a_real + minus_imag * a_imag) * modulus,
        (minus_imag * a_real - minus_real * a_imag) * modulus,
    )
    c = cmul((real_ref[...], imag_ref[...]), ratio)
    zk = z_power(float(local))
    whole = [(zk[0], zk[0], zk[0], zk[0]), (zk[1], zk[1], -zk[1], -zk[1])]
    lines = []
    for k in range(steps):
        zk = z_power(float(chunk * 2**k))
        lines += [(zk[0], zk[0], zk[0], zk[0]), (zk[1], zk[1], -zk[1], -zk[1])]
    lines += [(c[0], -c[0], -c[0], c[0]), (c[1], -c[1], c[1], -c[1])]
    for k, line in enumerate(whole):
        whole_ref[:, k, :] = jnp.concatenate(line, axis=-1)
    for k, line in enumerate(lines):
        pars_ref[:, k, :] = jnp.concatenate(line, axis=-1)
    line_ref[...] = jnp.zeros_like(line_ref)
    for k, line in enumerate((w_real, turns, c[0], c[1], z[0], z[1])):
        line_ref[:, k, 0:modes] = line
    places = lax.broadcasted_iota(jnp.int32, (modes, size), 1).astype(f32)
    flip = reversal(size)
    for i in range(block):
        cols = line_ref[i].T

        def col(k):
            return jnp.broadcast_to(cols[:modes, k : k + 1], (modes, size))

        envelope = jnp.exp(col(0) * places)
        cosine, sine = circle(col(1) * places)
        level = (envelope * cosine, envelope * sine)
        taps_ref[i : i + 1, :] = 2.0 * jnp.sum(
            col(2) * level[0] - col(3) * level[1], axis=0, keepdims=True
        )
        one_ref[i] = four(cmul(level, (col(4), col(5))), 0).astype(bf16)
        two_ref[i] = nn(four(level, 0).astype(bf16), flip).astype(bf16)


def states_kernel(
    chunks, x_ref, scale_ref, gain_ref, two_ref, pars_ref, u_ref, q_ref, end_ref, flat_ref
):
    block, rows, size = u_ref.shape
    for r in range(rows):
        b, j = r // chunks, r % chunks
        flat_ref[pl.ds(r, block, stride=rows), :] = x_ref[b, :, j * size : (j + 1) * size].astype(
            f32
        )
    for group in groups_of(block):
        us = [
            (
                flat_ref[i * rows : (i + 1) * rows, :] * scale_ref[...] * gain_ref[i : i + 1, :]
            ).astype(bf16)
            for i in group
        ]
        qs = [nt(u, two_ref[i]) for i, u in zip(group, us)]
        wholes = scan_rows(qs, pars_ref, group, chunks, False)
        for i, u, q, whole in zip(group, us, qs, wholes):
            u_ref[i] = u
            q_ref[i] = q
            for b in range(rows // chunks):
                last = b * chunks + chunks - 1
                end_ref[i, b : b + 1, :] = whole[last : last + 1, :].astype(bf16)


def hand_kernel(seq, backward, terms_ref, pars_ref, out_ref):
    group = terms_ref.shape[0] // seq
    state = jnp.zeros((group,) + terms_ref.shape[1:], f32)
    half = terms_ref.shape[2] // 2
    for k in range(seq - 1, -1, -1) if backward else range(seq):
        out_ref[k * group : (k + 1) * group] = state.astype(bf16)
        state = (
            state * pars_ref[:, 0:1, :]
            + pltpu.roll(state, half, 2) * pars_ref[:, 1:2, :]
            + terms_ref[k * group : (k + 1) * group].astype(f32)
        )


def mix_kernel(
    chunks, u_ref, q_ref, into_ref, one_ref, taps_ref, skip_ref, pars_ref,
    mixed_ref, state_ref, lifted_ref, flat_ref,
):
    block, rows, size = u_ref.shape
    for group in groups_of(block):
        states = [entered(q_ref[i], into_ref[i].astype(f32), chunks, False) for i in group]
        states = scan_rows(states, pars_ref, group, chunks, False)
        for i, s in zip(group, states):
            state_ref[i] = s
        outs = [weighed(s, turn(s), pars_ref, i) for i, s in zip(group, states)]
        near = [nn(u_ref[i], toeplitz(taps_ref[i : i + 1, :])) for i in group]
        ys = [y + nn(o, one_ref[i]) for i, y, o in zip(group, near, outs)]
        mixes = [
            (y + skip_ref[i : i + 1, :] * u_ref[i].astype(f32)).astype(bf16)
            for i, y in zip(group, ys)
        ]
        for i, mixed in zip(group, mixes):
            mixed_ref[i] = mixed
            flat_ref[i * rows : (i + 1) * rows, :] = gelu_pair(mixed.astype(f32))[0]
    for r in range(rows):
        b, j = r // chunks, r % chunks
        lifted_ref[b, :, j * size : (j + 1) * size] = flat_ref[
            pl.ds(r, block, stride=rows), :
        ].astype(bf16)


def ends_kernel(chunks, gl_ref, mixed_ref, one_ref, pars_ref, g_ref, p_ref, end_ref, flat_ref):
    block, rows, size = mixed_ref.shape
    for r in range(rows):
        b, j = r // chunks, r % chunks
        flat_ref[pl.ds(r, block, stride=rows), :] = gl_ref[
            b, :, j * size : (j + 1) * size
        ].astype(f32)
    for group in groups_of(block):
        gs = [
            (
                flat_ref[i * rows : (i + 1) * rows, :] * gelu_pair(mixed_ref[i].astype(f32))[1]
            ).astype(bf16)
            for i in group
        ]
        ps = [nt(g, one_ref[i]) for i, g in zip(group, gs)]
        wholes = scan_rows(ps, pars_ref, group, chunks, True)
        for i, g, p, whole in zip(group, gs, ps, wholes):
            g_ref[i] = g
            p_ref[i] = p
            for b in range(rows // chunks):
                end_ref[i, b : b + 1, :] = whole[b * chunks : b * chunks + 1, :].astype(bf16)


def summed(values):
    return jnp.sum(values, axis=0, keepdims=True)


def sums_kernel(g_ref, u_ref, state_ref, p_ref, one_ref, sum_ref):
    block, rows, size = g_ref.shape
    lanes = lax.broadcasted_iota(jnp.int32, (rows, size), 1).astype(f32)
    row_id = lax.broadcasted_iota(jnp.int32, (size, size), 0)
    lane_id = lax.broadcasted_iota(jnp.int32, (size, size), 1)
    places = lane_id[0:1].astype(f32)
    keep = lane_id <= row_id
    flip = reversal(size)
    for group in groups_of(block):
        flipped = [nt(flip, u_ref[i]).astype(bf16) for i in group]
        pas = [nt((g_ref[i].astype(f32) * lanes).astype(bf16), one_ref[i]) for i in group]
        outers = [nn(f, g_ref[i]) for i, f in zip(group, flipped)]
        lags = [
            summed(jnp.where(keep, pltpu.roll(o, 1, 1, stride=1, stride_axis=0), 0.0))
            for o in outers
        ]
        stacked = []
        for lag in lags:
            parts = []
            for v in (lag, lag * places):
                high = v.astype(bf16).astype(f32)
                parts += [high, v - high]
            stacked += [
                jnp.concatenate(parts + [jnp.zeros((4, size), f32)], axis=0).astype(bf16)
            ]
        withins = [nt(s, one_ref[i]) for i, s in zip(group, stacked)]
        for i, pa, within in zip(group, pas, withins):
            states = state_ref[i]
            p = p_ref[i]
            sum_ref[i, 0:1, :] = summed(states * p)
            sum_ref[i, 1:2, :] = summed(states * turn(p))
            sum_ref[i, 2:3, :] = summed(states * pa)
            sum_ref[i, 3:4, :] = summed(states * turn(pa))
            sum_ref[i, 4:5, :] = within[0:1] + within[1:2]
            sum_ref[i, 5:6, :] = within[2:3] + within[3:4]
            skip = summed(g_ref[i].astype(f32) * u_ref[i].astype(f32))
            sum_ref[i, 6:7, :] = jnp.broadcast_to(jnp.sum(skip, axis=1, keepdims=True), (1, size))
            sum_ref[i, 7:8, :] = jnp.zeros((1, size), f32)


def back_kernel(
    chunks, g_ref, p_ref, into_ref, u_ref, state_ref, two_ref, taps_ref, skip_ref, pars_ref,
    x_ref, scale_ref, gain_ref, out_ref, sum_ref, dot_ref, first_ref, flat_ref,
):
    block, rows, size = g_ref.shape

    @pl.when(pl.program_id(0) == 0)
    def _():
        dot_ref[...] = jnp.zeros_like(dot_ref)

    lanes = lax.broadcasted_iota(jnp.int32, (rows, size), 1).astype(f32)
    for group in groups_of(block):
        qps = [nt((u_ref[i].astype(f32) * lanes).astype(bf16), two_ref[i]) for i in group]
        near = [nt(g_ref[i], toeplitz(taps_ref[i : i + 1, :])) for i in group]
        adjoints = [entered(p_ref[i], into_ref[i].astype(f32), chunks, True) for i in group]
        adjoints = scan_rows(adjoints, pars_ref, group, chunks, True)
        turned = [turn(a) for a in adjoints]
        outs = [weighed(a, t, pars_ref, i) for i, a, t in zip(group, adjoints, turned)]
        ys = [y + nn(o, two_ref[i]) for i, y, o in zip(group, near, outs)]
        for i, y, qp, adjoint, t in zip(group, ys, qps, adjoints, turned):
            flat_ref[i * rows : (i + 1) * rows, :] = y + skip_ref[i : i + 1, :] * g_ref[i].astype(
                f32
            )
            states = state_ref[i]
            here = p_ref[i] + adjoint * pars_ref[i, 0:1, :] + t * pars_ref[i, 1:2, :]
            sum_ref[i, 0:1, :] = summed(states * here)
            sum_ref[i, 1:2, :] = summed(states * turn(here))
            sum_ref[i, 2:3, :] = summed(adjoint * qp)
            sum_ref[i, 3:4, :] = summed(adjoint * turn(qp))
            sum_ref[i, 4:8, :] = jnp.zeros((4, size), f32)
    gain = gain_ref[...]
    first = jnp.zeros((block, size), f32)
    for r in range(rows):
        b, j = r // chunks, r % chunks
        lanes_r = slice(j * size, (j + 1) * size)
        grad = flat_ref[pl.ds(r, block, stride=rows), :].astype(bf16)
        out_ref[b, :, lanes_r] = grad
        product = grad.astype(f32) * x_ref[b, :, lanes_r].astype(f32)
        dot_ref[r : r + 1, :] += summed(product * gain)
        first += product * scale_ref[r : r + 1, :]
    first_ref[...] = first


def last_kernel(
    half, x_ref, low_ref, high_ref, hidden_ref, result_ref, scale_ref, cubic_ref, gain_ref,
    out_ref, copy_ref,
):
    gain = gain_ref[:, 0:1]

    def run(grad_ref):
        for b in range(x_ref.shape[0]):
            out_ref[:, b, :] = (
                scale_ref[b : b + 1, :] * gain * grad_ref[b].astype(f32)
                - cubic_ref[b : b + 1, :] * x_ref[b].astype(f32)
                + hidden_ref[b].astype(f32)
            )
            copy_ref[:, b, :] = result_ref[b]

    @pl.when(pl.program_id(0) < half)
    def _():
        run(low_ref)

    @pl.when(pl.program_id(0) >= half)
    def _():
        run(high_ref)


def over_blocks(kernel, steps, args, outs, us, scratch=(), ties=(), vmem=60):
    count = len(args)

    def run(*refs):
        kernel(*refs[:count], *refs[count + len(ties) :])

    moved = sum(a.size * a.dtype.itemsize for a, _, _ in args + outs)
    return pl.pallas_call(
        run,
        grid=(steps,),
        in_specs=[
            pl.BlockSpec(memory_space=pltpu.SMEM) if b is None else pl.BlockSpec(b, m)
            for _, b, m in args
        ]
        + [pl.BlockSpec(memory_space=pl.ANY) for _ in ties],
        out_specs=[pl.BlockSpec(b, m) for _, b, m in outs],
        out_shape=[o for o, _, _ in outs],
        scratch_shapes=list(scratch),
        compiler_params=pltpu.CompilerParams(vmem_limit_bytes=vmem * 1024 * 1024),
        cost_estimate=pl.CostEstimate(
            flops=int(us * 1e9), bytes_accessed=moved, transcendentals=0
        ),
    )(*[a for a, _, _ in args], *ties)


def along(array, dim, block, first=0):
    shape = array.shape
    if dim is None:
        return (array, tuple(shape), lambda i: (0,) * len(shape))
    sizes = tuple(block if d == dim else size for d, size in enumerate(shape))
    return (
        array,
        sizes,
        lambda i: tuple(i + first if d == dim else 0 for d in range(len(shape))),
    )


def by_channel(kernel, block, channels, args, outs, us, scratch=(), ties=(), first=0):
    return over_blocks(
        kernel,
        channels // block,
        [along(a, d, block, first) if d != "smem" else (a, None, None) for a, d in args],
        [along(o, d, block) for o, d in outs],
        us,
        scratch,
        ties,
    )


def lane_sums(values):
    width = min(128, values.shape[1])
    total = values[:, :width]
    for k in range(1, values.shape[1] // width):
        total = total + values[:, k * width : (k + 1) * width]
    return total


def gated_kernel(mp, at_ref, valid_ref, x_ref, residual_ref, *refs):
    up_refs, w_refs, refs = refs[:mp], refs[mp : 2 * mp], refs[2 * mp :]
    bias_ref, gain_ref, upstream_ref, hidden_ref, normed_ref, *refs = refs
    value_ref, opening_ref, line_ref = refs
    features = w_refs[0].shape[0] // 2

    def rows(k):
        return pl.ds(pl.multiple_of(at_ref[k] * features, features), features)

    for k in range(mp):
        upstream_ref[rows(k), :] = (up_refs[k][...].astype(f32) * valid_ref[...]).astype(bf16)
    x = x_ref[...]
    squares = branches = inner = 0.0
    for k in range(mp):
        own = slice(k * features, (k + 1) * features)
        value = nn(w_refs[k][:features], x) + bias_ref[0, own, 0:1]
        gate = nn(w_refs[k][features:], x) + bias_ref[1, own, 0:1]
        opening = 1.0 / (1.0 + jnp.exp(-gate))
        branch = value * opening
        residual = residual_ref[rows(k), :].astype(f32)
        hidden = residual + branch
        hidden_ref[own, :] = hidden
        value_ref[own, :] = value
        opening_ref[own, :] = opening
        squares += summed(residual * residual)
        branches += summed(branch * branch)
        inner += summed(hidden * hidden)
    scale = lax.rsqrt(inner / (mp * features) + epsilon)
    for k in range(mp):
        own = slice(k * features, (k + 1) * features)
        normed_ref[rows(k), :] = (hidden_ref[own, :] * scale * gain_ref[own, 0:1]).astype(bf16)
    line_ref[0:1, :] = scale
    line_ref[1:2, :] = squares
    line_ref[2:3, :] = branches
    line_ref[3:8, :] = jnp.zeros((5, scale.shape[1]), f32)


def hidden_kernel(
    blocks, first, normed_ref, upstream_ref, up_a_ref, up_b_ref, down_a_ref, down_b_ref, bias_ref,
    *refs,
):
    if first:
        feed_out, grad_out, shrink_ref, expand_ref, line_ref, up_ref, down_ref = refs
    else:
        feed_in, grad_in, feed_out, grad_out, shrink_ref, expand_ref, line_ref, up_ref, down_ref = (
            refs
        )
    step = pl.program_id(0)

    @pl.when(step < blocks)
    def _():
        up_ref[...] = up_a_ref[...]
        down_ref[...] = down_a_ref[...]

    @pl.when(step >= blocks)
    def _():
        up_ref[...] = up_b_ref[...].reshape(up_ref.shape)
        down_ref[...] = down_b_ref[...].reshape(up_ref.shape)

    @pl.when(step == 0)
    def _():
        if first:
            feed_out[...] = jnp.zeros_like(feed_out)
            grad_out[...] = jnp.zeros_like(grad_out)
        else:
            feed_out[...] = feed_in[...]
            grad_out[...] = grad_in[...]

    expanded = nn(up_ref[...], normed_ref[...]) + bias_ref[:, 0:1]
    lifted, slope = gelu_pair(expanded)
    lifted = lifted.astype(bf16)
    grad = (nn(down_ref[...], upstream_ref[...]) * slope).astype(bf16)
    shrink_ref[...] = nt(lifted, upstream_ref[...]).astype(bf16)
    expand_ref[0] = nt(normed_ref[...], grad).astype(bf16)
    line_ref[...] = lane_sums(grad.astype(f32))
    feed_out[...] += tn(down_ref[...], lifted)
    grad_out[...] += tn(up_ref[...], grad)


def gated_back_kernel(
    mp, at_ref, grad_ref, hidden_ref, value_ref, opening_ref, upstream_ref, line_ref, *refs
):
    w_refs, refs = refs[:mp], refs[mp:]
    gain_ref, lifted_ref, grad_hidden_ref, both_ref, sums_ref = refs

    @pl.when(pl.program_id(0) == 0)
    def _():
        sums_ref[...] = jnp.zeros_like(sums_ref)

    features = w_refs[0].shape[0] // 2

    def rows(k):
        return pl.ds(pl.multiple_of(at_ref[k] * features, features), features)

    scale = line_ref[0:1, :]
    dot = 0.0
    for k in range(mp):
        own = slice(k * features, (k + 1) * features)
        dot += summed(grad_ref[rows(k), :] * gain_ref[own, 0:1] * hidden_ref[own, :])
    cubic = scale * scale * scale * dot / (mp * features)
    lifted = 0.0
    for k in range(mp):
        own = slice(k * features, (k + 1) * features)
        hidden = hidden_ref[own, :]
        grad = grad_ref[rows(k), :]
        upstream = upstream_ref[rows(k), :].astype(f32)
        grad_hidden = scale * grad * gain_ref[own, 0:1] - hidden * cubic + upstream
        grad_hidden_ref[rows(k), :] = grad_hidden.astype(bf16)
        opening = opening_ref[own, :]
        grad_value = grad_hidden * opening
        grad_gate = (grad_value * value_ref[own, :] * (1.0 - opening)).astype(bf16)
        grad_value = grad_value.astype(bf16)
        sums_ref[k, 0] += lane_sums(grad_value.astype(f32))
        sums_ref[k, 1] += lane_sums(grad_gate.astype(f32))
        sums_ref[k, 2] += lane_sums(grad * hidden * scale)
        sums_ref[k, 3] += lane_sums(upstream)
        both = jnp.concatenate([grad_value, grad_gate], axis=0)
        both_ref[2 * k * features : 2 * (k + 1) * features, :] = both
        lifted += tn(w_refs[k][...], both)
    lifted_ref[...] = lifted.astype(bf16)


def gated_terms_kernel(
    features, at_ref, both_ref, x_ref, hidden_ref, feed_ref, bias_ref,
    near_ref, far_ref, result_ref, line_ref,
):
    step = pl.program_id(0)
    terms = nt(x_ref[...], both_ref[...]).astype(bf16)
    rows = pl.ds(pl.multiple_of(at_ref[step] * features, features), features)
    feed = feed_ref[rows, :] + bias_ref[:, 0:1]
    result_ref[rows, :] = (hidden_ref[...] + feed).astype(bf16)

    @pl.when(step == 0)
    def _():
        line_ref[...] = jnp.zeros_like(line_ref)

    line_ref[0:1, :] += summed(feed * feed)

    @pl.when(step < 2)
    def _():
        near_ref[0] = terms

    @pl.when(step >= 2)
    def _():
        far_ref[0] = terms


def swap(values, axis, bit):
    size = lax.axis_size(axis)
    return lax.ppermute(values, axis, [(i, i ^ bit) for i in range(size)])


def added(a, b):
    return (a.astype(f32) + b.astype(f32)).astype(bf16)


def axis_total(values, axis):
    bit = 1
    while bit < lax.axis_size(axis):
        values = values + swap(values, axis, bit)
        bit *= 2
    return values


def bits_of(axis):
    return [1 << k for k in range(lax.axis_size(axis).bit_length() - 1)]


def axis_of(bit):
    return 0 if bit == 0 else 1 + len(bits_of("seq")) - bit.bit_length()


def sent_down(terms, bit):
    if bit == 0:
        return terms[:1], terms[1:], swap(terms[1:], "mp", 2)
    mine = (lax.axis_index("seq") // bit) % 2
    kept = lax.dynamic_slice_in_dim(terms, mine, 1, axis_of(bit))
    sent = lax.dynamic_slice_in_dim(terms, 1 - mine, 1, axis_of(bit))
    return kept, sent, swap(sent, "seq", bit)


def up_step(terms, bit):
    there = swap(terms, "seq", bit)
    first = (lax.axis_index("seq") // bit) % 2 == 0
    return jnp.concatenate(
        [jnp.where(first, terms, there), jnp.where(first, there, terms)], axis=axis_of(bit)
    )


def shards(
    inputs,
    valid,
    cotangent,
    first_gain,
    step_size,
    decay_rate,
    frequency,
    readout_real,
    readout_imag,
    skip_weight,
    gated_weight,
    gated_bias,
    second_gain,
    expand_weight,
    expand_bias,
    shrink_weight,
    shrink_bias,
):
    mp = lax.axis_size("mp")
    seq = lax.axis_size("seq")
    mp_me = lax.axis_index("mp")
    seq_me = lax.axis_index("seq")
    features, contexts, local = inputs.shape
    chunk = min(CHUNK, local)
    chunks = local // chunk
    rows = contexts * chunks
    modes = decay_rate.shape[1]
    tokens = local
    hidden_own = expand_weight.shape[1]
    group = features // seq

    bits_at = [(k // 2) + 2 * (k % 2) for k in range(mp)]
    device_at = [jnp.bitwise_xor(mp_me, bit) for bit in bits_at]
    at = jnp.stack(device_at).astype(jnp.int32)

    def exchanged(values):
        sent = [lax.dynamic_index_in_dim(values, device_at[k], 0, keepdims=False) for k in range(mp)]
        return [sent[0]] + [swap(sent[k], "mp", bits_at[k]) for k in range(1, mp)]

    def returned(values):
        return lax.all_to_all(values.reshape(mp, features, local), "mp", 0, 0, tiled=True)

    def after(value, earlier):
        return lax.optimization_barrier((value, earlier))[0]

    def all_places(own, upper):
        return own, upper, swap(own, "mp", 1), swap(upper, "mp", 1)

    gated_own = gated_weight.transpose(1, 2, 0).reshape(2 * features, D)
    small = jnp.concatenate([gated_bias.reshape(-1), second_gain, expand_bias, shrink_bias])
    by_context = inputs.swapaxes(0, 1)
    squares = jnp.sum(jnp.square(by_context.astype(f32)), axis=1)
    sent = jnp.concatenate([squares.reshape(-1), small])
    flats = [sent] + [swap(sent, "mp", bits_at[k]) for k in range(1, mp)]
    small_places = jnp.stack([v[contexts * local :] for v in flats])
    square_one = sum(v[: contexts * local] for v in flats).reshape(contexts, local)

    expand_own = expand_weight.T
    part = hidden_own // seq

    slices_sent = jnp.stack(
        [
            lax.dynamic_slice_in_dim(expand_own, seq_me * part, part, 0),
            lax.dynamic_slice_in_dim(shrink_weight, seq_me * part, part, 0),
        ]
    )
    slices = swap(slices_sent, "mp", 2)
    residual = lax.all_to_all(by_context, "mp", 0, 0, tiled=True)
    expand_far = swap(expand_own, "mp", 1)

    cut = [0, 2 * features]
    cut += [cut[-1] + features]
    cut += [cut[-1] + hidden_own]
    cut += [cut[-1] + features]

    def wide(values):
        return jnp.broadcast_to(values[..., None], values.shape + (128,))

    gated_bias_wide = wide(
        small_places[:, : cut[1]].reshape(mp, 2, features).swapaxes(0, 1).reshape(2, D)
    )
    gain_two_wide = wide(small_places[:, cut[1] : cut[2]].reshape(D))
    shrink_bias_wide = wide(small_places[:, cut[3] :].reshape(D))
    near_bias = wide(small_places[:2, cut[2] : cut[3]].reshape(-1))
    far_bias = wide(small_places[2:, cut[2] : cut[3]].reshape(-1))

    scale_one = lax.rsqrt(square_one / D + epsilon)
    scale_rows = scale_one.reshape(rows, chunk)

    w = discretized(step_size, decay_rate, frequency)
    coeff = coefficients(step_size, decay_rate, frequency, readout_real, readout_imag)

    def handed(ends, backward, ties=()):
        terms = lax.all_to_all(ends, "seq", 0, 0, tiled=True)
        (states,) = over_blocks(
            functools.partial(hand_kernel, seq, backward),
            1,
            [along(terms, None, 0), along(z_device, None, 0)],
            [along(out(terms.shape, bf16), None, 0)],
            3,
            (),
            ties,
        )
        return lax.all_to_all(states, "seq", 0, 0, tiled=True)

    def out(shape, dtype):
        return jax.ShapeDtypeStruct(shape, dtype)

    block = min(16, features)
    state_shape = out((features, rows, 4 * modes), f32)
    end_shape = out((features, contexts, 4 * modes), bf16)
    row_shape = out((features, rows, chunk), bf16)
    context_shape = out((contexts, features, local), bf16)
    table_shape = out((features, 4 * modes, chunk), bf16)
    sum_shape = out((features, 8, 4 * modes), f32)
    line_shape = out((features, chunk), f32)
    flat = [pltpu.VMEM((block * rows, chunk), f32)]
    skip_wide = jnp.broadcast_to(skip_weight[:, None], (features, chunk))
    gain_wide = jnp.broadcast_to(first_gain[:, None], (features, chunk))
    scan_steps = max(1, (chunks - 1).bit_length())
    pars, whole_pars, one, two, taps = by_channel(
        functools.partial(tables_kernel, chunk, scan_steps, local),
        block,
        features,
        [
            (step_size[:, None], 0),
            (decay_rate, 0),
            (frequency, 0),
            (readout_real, 0),
            (readout_imag, 0),
        ],
        [
            (out((features, 2 * scan_steps + 2, 4 * modes), f32), 0),
            (out((features, 2, 4 * modes), f32), 0),
            (table_shape, 0),
            (table_shape, 0),
            (line_shape, 0),
        ],
        10,
        [pltpu.VMEM((block, 8, 4 * modes), f32)],
        (sent, slices_sent, by_context),
    )
    gated_upper = swap(gated_own, "mp", 2)
    shrink_far = swap(shrink_weight, "mp", 1)
    z_device = lax.dynamic_slice_in_dim(whole_pars, seq_me * group, group, 0)
    cotangent_by_context = after(cotangent.swapaxes(0, 1), taps)
    upstream_parts = exchanged(cotangent_by_context)
    normed_one, terms, ends = by_channel(
        functools.partial(states_kernel, chunks),
        block,
        features,
        [(by_context, 1), (scale_rows, None), (gain_wide, 0), (two, 0), (pars, 0)],
        [(row_shape, 0), (state_shape, 0), (end_shape, 0)],
        8,
        flat,
        (slices, residual, expand_far, cotangent_by_context),
    )
    upper = lax.all_gather(after(slices, normed_one), "seq", axis=0)
    gated_places = (
        gated_own,
        gated_upper,
        swap(after(gated_own, normed_one), "mp", 1),
        swap(gated_upper, "mp", 1),
    )
    states_in = handed(ends, False, (shrink_far,))
    mixed, states, lifted_one = by_channel(
        functools.partial(mix_kernel, chunks),
        block,
        features,
        [
            (normed_one, 0),
            (terms, 0),
            (states_in, 0),
            (one, 0),
            (taps, 0),
            (skip_wide, 0),
            (pars, 0),
        ],
        [(row_shape, 0), (state_shape, 0), (context_shape, 1)],
        14,
        flat,
        (gated_upper,),
    )


    lifted_sent = after(lifted_one, (*upstream_parts, *gated_places))
    whole_one = lax.all_to_all(lifted_sent, "mp", 0, 0, tiled=True).reshape(D, tokens)
    upper_far = swap(after(upper, whole_one), "mp", 1)
    own_valid = lax.dynamic_slice_in_dim(valid, mp_me, 1, 0).astype(f32)

    token_block = min(256, tokens)
    token_steps = tokens // token_block
    wide_f = out((D, tokens), f32)
    wide_b = out((D, tokens), bf16)
    line_out = out((8, tokens), f32)

    def by_tokens(kernel, args, outs, us, scratch=(), ties=()):
        return over_blocks(
            kernel,
            token_steps,
            [along(a, d, token_block) if d != "smem" else (a, None, None) for a, d in args],
            [along(o, d, token_block) for o, d in outs],
            us,
            scratch,
            ties,
            60,
        )

    upstream, hidden, normed_two, value_part, opening, lines = by_tokens(
        functools.partial(gated_kernel, mp),
        [
            (at, "smem"),
            (own_valid, 1),
            (whole_one, 1),
            (residual.reshape(D, tokens), 1),
            *[(part_k, 1) for part_k in upstream_parts],
            *[(w_place, None) for w_place in gated_places],
            (gated_bias_wide, None),
            (gain_two_wide, None),
        ],
        [
            (wide_b, 1),
            (wide_f, 1),
            (wide_b, 1),
            (wide_f, 1),
            (wide_f, 1),
            (line_out, 1),
        ],
        12,
    )

    hidden_block = min(256, hidden_own)
    blocks = hidden_own // hidden_block
    near_rows = 2 * hidden_own

    parts = hidden_block // part
    low = ((hidden_block, D), lambda i: (jnp.minimum(i, blocks - 1), 0))
    grad_shape = out((near_rows, D), bf16)

    def half(which):
        return ((parts, 1, part, D), lambda i: (jnp.maximum(i - blocks, 0), which, 0, 0))

    def by_hidden(up, down, both, bias, carried, ties=()):
        first = carried is None
        args = [
            along(normed_two, None, 0),
            along(upstream, None, 0),
            (up, *low),
            (both, *half(0)),
            (down, *low),
            (both, *half(1)),
            along(bias, 0, hidden_block),
        ]
        if not first:
            args += [along(c, None, 0) for c in carried]
        return over_blocks(
            functools.partial(hidden_kernel, blocks, first),
            2 * blocks,
            args,
            [
                along(wide_f, None, 0),
                along(wide_f, None, 0),
                along(grad_shape, 0, hidden_block),
                (
                    out((2, D, hidden_own), bf16),
                    (1, D, hidden_block),
                    lambda i: (i // blocks, 0, i % blocks),
                ),
                along(out((near_rows, min(128, tokens)), f32), 0, hidden_block),
            ],
            38,
            [pltpu.VMEM((hidden_block, D), bf16)] * 2,
            ties,
        )

    feed, grad_normed_two, shrink_far_g, expand_far_g, far_lines = by_hidden(
        expand_far, shrink_far, upper_far, far_bias, None
    )
    core_shrink, core_expand = swap(shrink_far_g, "mp", 1), swap(expand_far_g, "mp", 1)
    feed, grad_normed_two, shrink_near_g, expand_near_g, near_lines = by_hidden(
        expand_own, shrink_weight, upper, near_bias, (feed, grad_normed_two)
    )
    bits = bits_of("seq")
    split = (2,) * (1 + len(bits))
    cubes = split + (-1, D)
    first, second, third, rest = bits[0], bits[1], bits[2], bits[3:]
    upper_bit = 0
    s_kept, s_sent, s_there = sent_down(added(shrink_near_g, core_shrink).reshape(cubes), first)
    e_kept, e_sent, e_there = sent_down(added(expand_near_g, core_expand).reshape(split + (-1, hidden_own)), second)

    def onwards(kept, there, bit):
        return sent_down(added(kept, there), bit)

    sums_out = out((mp, 4, features, min(128, token_block)), f32)
    grad_lifted_one, grad_hidden, both_g, sums = by_tokens(
        functools.partial(gated_back_kernel, mp),
        [
            (at, "smem"),
            (grad_normed_two, 1),
            (hidden, 1),
            (value_part, 1),
            (opening, 1),
            (upstream, 1),
            (lines, 1),
            *[(w_place, None) for w_place in gated_places],
            (gain_two_wide, None),
        ],
        [(wide_b, 1), (wide_b, 1), (out((2 * D, tokens), bf16), 1), (sums_out, None)],
        14,
        (),
        (s_sent, e_sent),
    )
    own_lifted_one = returned(grad_lifted_one)
    gated_near, gated_far, result, feed_lines = over_blocks(
        functools.partial(gated_terms_kernel, features),
        mp,
        [
            (at, None, None),
            along(both_g, 0, 2 * features),
            along(whole_one, None, 0),
            along(hidden, 0, features),
            along(feed, None, 0),
            along(shrink_bias_wide, 0, features),
        ],
        [
            (
                out((2, D, 2 * features), bf16),
                (1, D, 2 * features),
                lambda i: (jnp.minimum(i, 1), 0, 0),
            ),
            (
                out((2, D, 2 * features), bf16),
                (1, D, 2 * features),
                lambda i: (jnp.maximum(i - 2, 0), 0, 0),
            ),
            along(wide_b, None, 0),
            along(line_out, None, 0),
        ],
        10,
    )
    core_gated = swap(gated_far, "mp", 1)

    grad_mixed, adj_terms, adj_ends = by_channel(
        functools.partial(ends_kernel, chunks),
        block,
        features,
        [(own_lifted_one, 1), (mixed, 0), (one, 0), (pars, 0)],
        [(row_shape, 0), (state_shape, 0), (end_shape, 0)],
        10,
        flat,
        (s_there, e_there, core_gated),
    )
    s_kept, s_sent, s_there = onwards(s_kept, s_there, second)
    e_kept, e_sent, e_there = onwards(e_kept, e_there, first)
    g_kept, g_sent, g_there = sent_down(added(gated_near, core_gated).reshape(split + (-1, 2 * features)), first)
    adjoint_in = handed(adj_ends, True, (s_sent, e_sent, g_sent))
    s_kept, s_sent, s_there = onwards(s_kept, s_there, third)
    e_kept, e_sent, e_there = onwards(e_kept, e_there, upper_bit)
    (sums_one,) = by_channel(
        sums_kernel,
        block,
        features,
        [(grad_mixed, 0), (normed_one, 0), (states, 0), (adj_terms, 0), (one, 0)],
        [(sum_shape, 0)],
        20,
        (),
        (s_sent, e_sent, adjoint_in),
    )
    own_hidden = returned(after(grad_hidden, adjoint_in))
    s_there, e_there, g_there = after((s_there, e_there, g_there), sums_one)
    g_kept, g_sent, g_there = onwards(g_kept, g_there, upper_bit)
    s_kept, s_sent, s_there = onwards(s_kept, s_there, upper_bit)
    e_kept, e_sent, e_there = onwards(e_kept, e_there, third)
    half = features // 2 // block
    back_args = [
        (grad_mixed, 0),
        (adj_terms, 0),
        (adjoint_in, 0),
        (normed_one, 0),
        (states, 0),
        (two, 0),
        (taps, 0),
        (skip_wide, 0),
        (pars, 0),
        (by_context, 1),
        (scale_rows, None),
        (gain_wide, 0),
    ]

    def back(first_block, ties):
        return by_channel(
            functools.partial(back_kernel, chunks),
            block,
            features // 2,
            back_args,
            [
                (out((contexts, features // 2, local), bf16), 1),
                (out((features // 2, 8, 4 * modes), f32), 0),
                (out((rows, chunk), f32), None),
                (out((features // 2, chunk), f32), 0),
            ],
            12,
            flat,
            ties,
            first_block,
        )

    def up(values, bit):
        return up_step(values, bit)

    def exchange(values, bit):
        return added(values, swap(values, "seq", bit))

    low = back(0, (s_sent, e_sent, g_sent, sums_one, own_hidden))
    result = returned(after(result, own_hidden))
    s_there, e_there, g_there = after((s_there, e_there, g_there), low[2])
    s_all, e_all, g_all = added(s_kept, s_there), added(e_kept, e_there), added(g_kept, g_there)
    for bit in rest:
        s_all, e_all = (added(*sent_down(v, bit)[::2]) for v in (s_all, e_all))
        g_all = exchange(g_all, bit)
    high = back(half, (s_all, e_all, g_all, low[2], result))
    for bit in rest[::-1]:
        s_all, e_all = up(s_all, bit), up(e_all, bit)
    s_all, e_all, g_all = up(s_all, third), up(e_all, first), exchange(g_all, second)
    s_all, e_all, g_all = after((s_all, e_all, g_all), high[2])
    grad_first_gain = jnp.sum(jnp.concatenate([low[3], high[3]]), axis=1)

    dot_one = axis_total(low[2] + high[2], "mp").reshape(contexts, local)
    cubic = scale_one * scale_one * scale_one * dot_one / D
    grad_inputs, result = over_blocks(
        functools.partial(last_kernel, half),
        features // block,
        [
            along(by_context, 1, block),
            (low[0], (contexts, block, local), lambda i: (0, jnp.minimum(i, half - 1), 0)),
            (high[0], (contexts, block, local), lambda i: (0, jnp.maximum(i - half, 0), 0)),
            along(own_hidden, 1, block),
            along(result, 1, block),
            along(scale_one, None, 0),
            along(cubic, None, 0),
            along(gain_wide, 0, block),
        ],
        [along(out(inputs.shape, f32), 0, block), along(out(inputs.shape, bf16), 0, block)],
        8,
    )
    s_all, e_all, g_all = up(s_all, second), up(e_all, third), exchange(g_all, third)
    s_all, e_all, g_all = after((s_all, e_all, g_all), grad_inputs)

    stats = jnp.stack(
        [
            jnp.sum(own_valid[0] * lines[1]),
            jnp.sum(own_valid[0] * lines[2]),
            jnp.sum(own_valid[0] * feed_lines[0]),
            jnp.sum(own_valid[0]),
        ]
    )
    sums = jnp.sum(sums, axis=3).reshape(mp, 4 * features)
    sums = jnp.concatenate([sums, jnp.broadcast_to(stats, (mp, 4))], axis=1)
    near = jnp.concatenate([sums[:2], jnp.sum(near_lines, axis=1).reshape(2, hidden_own)], axis=1)
    far = jnp.concatenate([sums[2:], jnp.sum(far_lines, axis=1).reshape(2, hidden_own)], axis=1)
    near = near + swap(far, "mp", 1)
    bias_size = near.shape[1]

    def quarter(values, k):
        return values[:, k * modes : (k + 1) * modes]

    def product_sums(lines, k):
        plain, turned = lines[:, k], lines[:, k + 1]
        return (
            quarter(plain, 0) - quarter(plain, 1),
            quarter(turned, 1) + quarter(turned, 3),
        )

    inverse = power(w, -1.0)
    within = [
        cmul(inverse, (quarter(sums_one[:, k], 0), quarter(sums_one[:, k], 1))) for k in (4, 5)
    ]
    sum_a = cadd(product_sums(sums_one, 0), within[0])
    def both_halves(k):
        pairs = [product_sums(part_k[1], k) for part_k in (low, high)]
        return tuple(jnp.concatenate(v) for v in zip(*pairs))

    crossing = both_halves(0)
    part_a = product_sums(sums_one, 2)
    part_p = both_halves(2)
    sum_b = [
        float(chunk) * crossing[k] + part_a[k] - part_p[k] + within[1][k] for k in range(2)
    ]
    lines_late = jnp.concatenate(
        [sums_one[:, 6, 0], grad_first_gain, near.reshape(-1)]
    )
    width = 4 * modes
    pad = -lines_late.shape[0] % width
    late = jnp.concatenate(
        [
            jnp.concatenate([*sum_a, *sum_b], axis=1),
            jnp.pad(lines_late, (0, pad)).reshape(-1, width),
        ],
        axis=0,
    )
    s_all, e_all, g_all = up(s_all, first), up(e_all, second), up(g_all, first)
    late = axis_total(late, "seq")
    grad_shrink = s_all.reshape(-1, D).astype(f32)
    grad_expand = e_all.reshape(D, hidden_own).astype(f32)
    grad_gated = g_all.reshape(D, 2, features).astype(f32)
    lines_late = late[features:].reshape(-1)
    late = late[:features]
    sum_a = (quarter(late, 0), quarter(late, 1))
    sum_b = (quarter(late, 2), quarter(late, 3))
    grad_skip = lines_late[:features]
    grad_first_gain = lines_late[features : 2 * features]
    bias_own = lines_late[2 * features : 2 * features + 2 * bias_size].reshape(2, bias_size)
    bias_own = bias_own[0] + swap(bias_own[1], "mp", 2)

    def form(step, decay, freq, out_real, out_imag):
        c = coefficients(step, decay, freq, out_real, out_imag)
        moved = cmul(coeff, discretized(step, decay, freq))
        return 2.0 * jnp.sum(
            c[0] * sum_a[0] - c[1] * sum_a[1] + moved[0] * sum_b[0] - moved[1] * sum_b[1]
        )

    kernel_grads = jax.grad(form, argnums=(0, 1, 2, 3, 4))(
        step_size, decay_rate, frequency, readout_real, readout_imag
    )
    ends_at = [0, 2 * features, 3 * features, 4 * features, 4 * features + 4]
    totals = bias_own[ends_at[3] : ends_at[4]]
    count = totals[3]
    rms = jnp.sqrt(totals[:3] / (count * D))
    return (
        result,
        grad_inputs,
        grad_first_gain,
        *kernel_grads,
        grad_skip,
        grad_gated,
        bias_own[: ends_at[1]].reshape(2, features),
        bias_own[ends_at[1] : ends_at[2]],
        grad_expand,
        bias_own[ends_at[4] :],
        grad_shrink,
        bias_own[ends_at[2] : ends_at[3]],
        rms[0],
        rms[1],
        rms[2],
    )


def solution(mesh):
    placed = (
        P("mp", None, "seq"),
        P(None, "seq"),
        P("mp", None, "seq"),
        P("mp"),
        P("mp"),
        P("mp", None),
        P("mp", None),
        P("mp", None),
        P("mp", None),
        P("mp"),
        P(None, None, "mp"),
        P(None, "mp"),
        P("mp"),
        P(None, "mp"),
        P("mp"),
        P("mp", None),
        P("mp"),
    )
    return jax.shard_map(
        shards,
        mesh=mesh,
        in_specs=placed,
        out_specs=(
            P("mp", None, "seq"),
            P("mp", None, "seq"),
            P("mp"),
            P("mp"),
            P("mp", None),
            P("mp", None),
            P("mp", None),
            P("mp", None),
            P("mp"),
            P(None, None, "mp"),
            P(None, "mp"),
            P("mp"),
            P(None, "mp"),
            P("mp"),
            P("mp", None),
            P("mp"),
            P(),
            P(),
            P(),
        ),
        check_vma=False,
    )
```

```python
import functools

import jax
import jax.numpy as jnp
from jax import lax
from jax.experimental import pallas as pl
from jax.experimental.pallas import tpu as pltpu
from jax.sharding import PartitionSpec as P

D = 1024
epsilon = 1e-05
CHUNK = 128
f32 = jnp.float32
bf16 = jnp.bfloat16


def contract(left, right, left_dim, right_dim):
    return lax.dot_general(
        left, right, (((left_dim,), (right_dim,)), ((), ())), preferred_element_type=f32
    )


def nt(left, right):
    return lax.dot_general(left, right, (((1,), (1,)), ((), ())), preferred_element_type=f32)


def nn(left, right):
    return lax.dot_general(left, right, (((1,), (0,)), ((), ())), preferred_element_type=f32)


def tn(left, right):
    return lax.dot_general(left, right, (((0,), (0,)), ((), ())), preferred_element_type=f32)


def gelu_pair(v):
    k0 = 0.7978845608028654
    k1 = 0.044715
    square = v * v
    t = jnp.tanh(k0 * v * (1.0 + k1 * square))
    half = 0.5 * (1.0 + t)
    return v * half, half + 0.5 * v * (1.0 - t * t) * k0 * (1.0 + 3.0 * k1 * square)


def cmul(a, b):
    return (a[0] * b[0] - a[1] * b[1], a[0] * b[1] + a[1] * b[0])


def cadd(a, b):
    return (a[0] + b[0], a[1] + b[1])


def discretized(step, decay, freq):
    return step[:, None] * (-decay), step[:, None] * freq


def coefficients(step, decay, freq, out_real, out_imag):
    a_real, a_imag = -decay, freq
    w_real, w_imag = discretized(step, decay, freq)
    growth = jnp.exp(w_real)
    minus_real = growth * jnp.cos(w_imag) - 1.0
    minus_imag = growth * jnp.sin(w_imag)
    modulus = a_real * a_real + a_imag * a_imag
    ratio_real = (minus_real * a_real + minus_imag * a_imag) / modulus
    ratio_imag = (minus_imag * a_real - minus_real * a_imag) / modulus
    return (
        out_real * ratio_real - out_imag * ratio_imag,
        out_real * ratio_imag + out_imag * ratio_real,
    )


def power(w, exponent):
    envelope = jnp.exp(w[0] * exponent)
    return envelope * jnp.cos(w[1] * exponent), envelope * jnp.sin(w[1] * exponent)


GROUP = 8


def four(pair, axis=-1):
    return jnp.concatenate([pair[0], pair[1], -pair[1], pair[0]], axis=axis)


def turn(values):
    return pltpu.roll(values, values.shape[1] // 2, 1)


def row_of_chunk(shape, chunks):
    return lax.rem(lax.broadcasted_iota(jnp.int32, shape, 0), chunks)


def groups_of(block):
    size = min(GROUP, block)
    return [range(k, k + size) for k in range(0, block, size)]


def moved_rows(values, step, chunks, backward):
    rows, width = values.shape
    if chunks == 8:
        cube = values.reshape(rows // 8, 8, width)
        place = lax.broadcasted_iota(jnp.int32, cube.shape, 1)
        if backward:
            cube = jnp.where(place < 8 - step, pltpu.roll(cube, 8 - step, 1), 0.0)
        else:
            cube = jnp.where(place >= step, pltpu.roll(cube, step, 1), 0.0)
        return cube.reshape(rows, width)
    place = row_of_chunk(values.shape, chunks)
    if backward:
        return jnp.where(place < chunks - step, pltpu.roll(values, rows - step, 0), 0.0)
    return jnp.where(place >= step, pltpu.roll(values, step, 0), 0.0)


def scan_rows(states, pars_ref, group, chunks, backward):
    step, k = 1, 0
    while step < chunks:
        moved = [moved_rows(s, step, chunks, backward) for s in states]
        turned = [turn(m) for m in moved]
        states = [
            s + m * pars_ref[i, 2 * k : 2 * k + 1, :] + t * pars_ref[i, 2 * k + 1 : 2 * k + 2, :]
            for i, s, m, t in zip(group, states, moved, turned)
        ]
        step, k = 2 * step, k + 1
    return states


def entered(terms, into, chunks, backward):
    rows, width = terms.shape
    wide = jnp.concatenate(
        [jnp.broadcast_to(into[b : b + 1], (chunks, width)) for b in range(rows // chunks)], axis=0
    )
    if chunks == 1:
        return wide
    place = row_of_chunk(terms.shape, chunks)
    edge = chunks - 1 if backward else 0
    return jnp.where(place == edge, wide, moved_rows(terms, 1, chunks, backward))


def weighed(states, turned, pars_ref, i):
    last = pars_ref.shape[1]
    return (
        states * pars_ref[i, last - 2 : last - 1, :] + turned * pars_ref[i, last - 1 : last, :]
    ).astype(bf16)


def toeplitz(taps):
    size = taps.shape[-1]
    rolled = pltpu.roll(jnp.broadcast_to(taps, (size, size)), 0, 1, stride=1, stride_axis=0)
    rows = lax.broadcasted_iota(jnp.int32, (size, size), 0)
    lanes = lax.broadcasted_iota(jnp.int32, (size, size), 1)
    return jnp.where(lanes >= rows, rolled, 0.0).astype(bf16)


def reversal(size):
    rows = lax.broadcasted_iota(jnp.int32, (size, size), 0)
    lanes = lax.broadcasted_iota(jnp.int32, (size, size), 1)
    return jnp.where(rows + lanes == size - 1, 1.0, 0.0).astype(bf16)


def circle(turns):
    x = (turns - jnp.floor(turns + 0.5)) * 3.14159265358979
    s = x * x
    sine = x * (
        1.0
        + s
        * (
            -1.0 / 6.0
            + s
            * (
                1.0 / 120.0
                + s * (-1.0 / 5040.0 + s * (1.0 / 362880.0 + s * (-1.0 / 39916800.0)))
            )
        )
    )
    cosine = 1.0 + s * (
        -0.5
        + s
        * (
            1.0 / 24.0
            + s
            * (
                -1.0 / 720.0
                + s * (1.0 / 40320.0 + s * (-1.0 / 3628800.0 + s * (1.0 / 479001600.0)))
            )
        )
    )
    return 1.0 - 2.0 * sine * sine, 2.0 * sine * cosine


def tables_kernel(
    chunk, steps, local, step_ref, decay_ref, freq_ref, real_ref, imag_ref,
    pars_ref, whole_ref, one_ref, two_ref, taps_ref, line_ref,
):
    block, modes = decay_ref.shape
    size = one_ref.shape[2]
    step = step_ref[...]
    a_real, a_imag = -decay_ref[...], freq_ref[...]
    w_real, turns = step * a_real, step * a_imag * 0.15915494309189535

    def z_power(exponent):
        envelope = jnp.exp(w_real * exponent)
        cosine, sine = circle(turns * exponent)
        return envelope * cosine, envelope * sine

    z = z_power(1.0)
    minus_real, minus_imag = z[0] - 1.0, z[1]
    modulus = 1.0 / (a_real * a_real + a_imag * a_imag)
    ratio = (
        (minus_real * a_real + minus_imag * a_imag) * modulus,
        (minus_imag * a_real - minus_real * a_imag) * modulus,
    )
    c = cmul((real_ref[...], imag_ref[...]), ratio)
    zk = z_power(float(local))
    whole = [(zk[0], zk[0], zk[0], zk[0]), (zk[1], zk[1], -zk[1], -zk[1])]
    lines = []
    for k in range(steps):
        zk = z_power(float(chunk * 2**k))
        lines += [(zk[0], zk[0], zk[0], zk[0]), (zk[1], zk[1], -zk[1], -zk[1])]
    lines += [(c[0], -c[0], -c[0], c[0]), (c[1], -c[1], c[1], -c[1])]
    for k, line in enumerate(whole):
        whole_ref[:, k, :] = jnp.concatenate(line, axis=-1)
    for k, line in enumerate(lines):
        pars_ref[:, k, :] = jnp.concatenate(line, axis=-1)
    line_ref[...] = jnp.zeros_like(line_ref)
    for k, line in enumerate((w_real, turns, c[0], c[1], z[0], z[1])):
        line_ref[:, k, 0:modes] = line
    places = lax.broadcasted_iota(jnp.int32, (modes, size), 1).astype(f32)
    flip = reversal(size)
    for i in range(block):
        cols = line_ref[i].T

        def col(k):
            return jnp.broadcast_to(cols[:modes, k : k + 1], (modes, size))

        envelope = jnp.exp(col(0) * places)
        cosine, sine = circle(col(1) * places)
        level = (envelope * cosine, envelope * sine)
        taps_ref[i : i + 1, :] = 2.0 * jnp.sum(
            col(2) * level[0] - col(3) * level[1], axis=0, keepdims=True
        )
        one_ref[i] = four(cmul(level, (col(4), col(5))), 0).astype(bf16)
        two_ref[i] = nn(four(level, 0).astype(bf16), flip).astype(bf16)


def states_kernel(
    chunks, x_ref, scale_ref, gain_ref, two_ref, pars_ref, u_ref, q_ref, end_ref, flat_ref
):
    block, rows, size = u_ref.shape
    for r in range(rows):
        b, j = r // chunks, r % chunks
        flat_ref[pl.ds(r, block, stride=rows), :] = x_ref[b, :, j * size : (j + 1) * size].astype(
            f32
        )
    for group in groups_of(block):
        us = [
            (
                flat_ref[i * rows : (i + 1) * rows, :] * scale_ref[...] * gain_ref[i : i + 1, :]
            ).astype(bf16)
            for i in group
        ]
        qs = [nt(u, two_ref[i]) for i, u in zip(group, us)]
        wholes = scan_rows(qs, pars_ref, group, chunks, False)
        for i, u, q, whole in zip(group, us, qs, wholes):
            u_ref[i] = u
            q_ref[i] = q
            for b in range(rows // chunks):
                last = b * chunks + chunks - 1
                end_ref[i, b : b + 1, :] = whole[last : last + 1, :].astype(bf16)


def hand_kernel(seq, backward, terms_ref, pars_ref, out_ref):
    group = terms_ref.shape[0] // seq
    state = jnp.zeros((group,) + terms_ref.shape[1:], f32)
    half = terms_ref.shape[2] // 2
    for k in range(seq - 1, -1, -1) if backward else range(seq):
        out_ref[k * group : (k + 1) * group] = state.astype(bf16)
        state = (
            state * pars_ref[:, 0:1, :]
            + pltpu.roll(state, half, 2) * pars_ref[:, 1:2, :]
            + terms_ref[k * group : (k + 1) * group].astype(f32)
        )


def mix_kernel(
    chunks, u_ref, q_ref, into_ref, one_ref, taps_ref, skip_ref, pars_ref,
    mixed_ref, state_ref, lifted_ref, flat_ref,
):
    block, rows, size = u_ref.shape
    for group in groups_of(block):
        states = [entered(q_ref[i], into_ref[i].astype(f32), chunks, False) for i in group]
        states = scan_rows(states, pars_ref, group, chunks, False)
        for i, s in zip(group, states):
            state_ref[i] = s
        outs = [weighed(s, turn(s), pars_ref, i) for i, s in zip(group, states)]
        near = [nn(u_ref[i], toeplitz(taps_ref[i : i + 1, :])) for i in group]
        ys = [y + nn(o, one_ref[i]) for i, y, o in zip(group, near, outs)]
        mixes = [
            (y + skip_ref[i : i + 1, :] * u_ref[i].astype(f32)).astype(bf16)
            for i, y in zip(group, ys)
        ]
        for i, mixed in zip(group, mixes):
            mixed_ref[i] = mixed
            flat_ref[i * rows : (i + 1) * rows, :] = gelu_pair(mixed.astype(f32))[0]
    for r in range(rows):
        b, j = r // chunks, r % chunks
        lifted_ref[b, :, j * size : (j + 1) * size] = flat_ref[
            pl.ds(r, block, stride=rows), :
        ].astype(bf16)


def ends_kernel(chunks, gl_ref, mixed_ref, one_ref, pars_ref, g_ref, p_ref, end_ref, flat_ref):
    block, rows, size = mixed_ref.shape
    for r in range(rows):
        b, j = r // chunks, r % chunks
        flat_ref[pl.ds(r, block, stride=rows), :] = gl_ref[
            b, :, j * size : (j + 1) * size
        ].astype(f32)
    for group in groups_of(block):
        gs = [
            (
                flat_ref[i * rows : (i + 1) * rows, :] * gelu_pair(mixed_ref[i].astype(f32))[1]
            ).astype(bf16)
            for i in group
        ]
        ps = [nt(g, one_ref[i]) for i, g in zip(group, gs)]
        wholes = scan_rows(ps, pars_ref, group, chunks, True)
        for i, g, p, whole in zip(group, gs, ps, wholes):
            g_ref[i] = g
            p_ref[i] = p
            for b in range(rows // chunks):
                end_ref[i, b : b + 1, :] = whole[b * chunks : b * chunks + 1, :].astype(bf16)


def summed(values):
    return jnp.sum(values, axis=0, keepdims=True)


def sums_kernel(g_ref, u_ref, state_ref, p_ref, one_ref, sum_ref):
    block, rows, size = g_ref.shape
    lanes = lax.broadcasted_iota(jnp.int32, (rows, size), 1).astype(f32)
    row_id = lax.broadcasted_iota(jnp.int32, (size, size), 0)
    lane_id = lax.broadcasted_iota(jnp.int32, (size, size), 1)
    places = lane_id[0:1].astype(f32)
    keep = lane_id <= row_id
    flip = reversal(size)
    for group in groups_of(block):
        flipped = [nt(flip, u_ref[i]).astype(bf16) for i in group]
        pas = [nt((g_ref[i].astype(f32) * lanes).astype(bf16), one_ref[i]) for i in group]
        outers = [nn(f, g_ref[i]) for i, f in zip(group, flipped)]
        lags = [
            summed(jnp.where(keep, pltpu.roll(o, 1, 1, stride=1, stride_axis=0), 0.0))
            for o in outers
        ]
        stacked = []
        for lag in lags:
            parts = []
            for v in (lag, lag * places):
                high = v.astype(bf16).astype(f32)
                parts += [high, v - high]
            stacked += [
                jnp.concatenate(parts + [jnp.zeros((4, size), f32)], axis=0).astype(bf16)
            ]
        withins = [nt(s, one_ref[i]) for i, s in zip(group, stacked)]
        for i, pa, within in zip(group, pas, withins):
            states = state_ref[i]
            p = p_ref[i]
            sum_ref[0, i : i + 1, :] = summed(states * p)
            sum_ref[1, i : i + 1, :] = summed(states * turn(p))
            sum_ref[2, i : i + 1, :] = summed(states * pa)
            sum_ref[3, i : i + 1, :] = summed(states * turn(pa))
            sum_ref[4, i : i + 1, :] = within[0:1] + within[1:2]
            sum_ref[5, i : i + 1, :] = within[2:3] + within[3:4]
            skip = summed(g_ref[i].astype(f32) * u_ref[i].astype(f32))
            sum_ref[6, i : i + 1, :] = jnp.broadcast_to(jnp.sum(skip, axis=1, keepdims=True), (1, size))


def back_kernel(
    chunks, g_ref, p_ref, into_ref, u_ref, state_ref, two_ref, taps_ref, skip_ref, pars_ref,
    x_ref, scale_ref, gain_ref, out_ref, sum_ref, dot_ref, first_ref, flat_ref,
):
    block, rows, size = g_ref.shape

    @pl.when(pl.program_id(0) == 0)
    def _():
        dot_ref[...] = jnp.zeros_like(dot_ref)

    lanes = lax.broadcasted_iota(jnp.int32, (rows, size), 1).astype(f32)
    for group in groups_of(block):
        qps = [nt((u_ref[i].astype(f32) * lanes).astype(bf16), two_ref[i]) for i in group]
        near = [nt(g_ref[i], toeplitz(taps_ref[i : i + 1, :])) for i in group]
        adjoints = [entered(p_ref[i], into_ref[i].astype(f32), chunks, True) for i in group]
        adjoints = scan_rows(adjoints, pars_ref, group, chunks, True)
        turned = [turn(a) for a in adjoints]
        outs = [weighed(a, t, pars_ref, i) for i, a, t in zip(group, adjoints, turned)]
        ys = [y + nn(o, two_ref[i]) for i, y, o in zip(group, near, outs)]
        for i, y, qp, adjoint, t in zip(group, ys, qps, adjoints, turned):
            flat_ref[i * rows : (i + 1) * rows, :] = y + skip_ref[i : i + 1, :] * g_ref[i].astype(
                f32
            )
            states = state_ref[i]
            here = p_ref[i] + adjoint * pars_ref[i, 0:1, :] + t * pars_ref[i, 1:2, :]
            sum_ref[0, i : i + 1, :] = summed(states * here)
            sum_ref[1, i : i + 1, :] = summed(states * turn(here))
            sum_ref[2, i : i + 1, :] = summed(adjoint * qp)
            sum_ref[3, i : i + 1, :] = summed(adjoint * turn(qp))
    gain = gain_ref[...]
    first = jnp.zeros((block, size), f32)
    for r in range(rows):
        b, j = r // chunks, r % chunks
        lanes_r = slice(j * size, (j + 1) * size)
        grad = flat_ref[pl.ds(r, block, stride=rows), :].astype(bf16)
        out_ref[b, :, lanes_r] = grad
        product = grad.astype(f32) * x_ref[b, :, lanes_r].astype(f32)
        dot_ref[r : r + 1, :] += summed(product * gain)
        first += product * scale_ref[r : r + 1, :]
    first_ref[...] = first


def last_kernel(
    half, x_ref, low_ref, high_ref, hidden_ref, scale_ref, cubic_ref, gain_ref, out_ref
):
    gain = gain_ref[:, 0:1]

    def run(grad_ref):
        for b in range(x_ref.shape[0]):
            out_ref[:, b, :] = (
                scale_ref[b : b + 1, :] * gain * grad_ref[b].astype(f32)
                - cubic_ref[b : b + 1, :] * x_ref[b].astype(f32)
                + hidden_ref[b].astype(f32)
            )

    @pl.when(pl.program_id(0) < half)
    def _():
        run(low_ref)

    @pl.when(pl.program_id(0) >= half)
    def _():
        run(high_ref)


def turned_kernel(values_ref, out_ref):
    for b in range(values_ref.shape[0]):
        out_ref[:, b, :] = values_ref[b]


def over_blocks(kernel, steps, args, outs, us, scratch=(), ties=(), vmem=60):
    count = len(args)

    def run(*refs):
        kernel(*refs[:count], *refs[count + len(ties) :])

    moved = sum(a.size * a.dtype.itemsize for a, _, _ in args + outs)
    return pl.pallas_call(
        run,
        grid=(steps,),
        in_specs=[
            pl.BlockSpec(memory_space=pltpu.SMEM) if b is None else pl.BlockSpec(b, m)
            for _, b, m in args
        ]
        + [pl.BlockSpec(memory_space=pl.ANY) for _ in ties],
        out_specs=[pl.BlockSpec(b, m) for _, b, m in outs],
        out_shape=[o for o, _, _ in outs],
        scratch_shapes=list(scratch),
        compiler_params=pltpu.CompilerParams(vmem_limit_bytes=vmem * 1024 * 1024),
        cost_estimate=pl.CostEstimate(
            flops=int(us * 1e9), bytes_accessed=moved, transcendentals=0
        ),
    )(*[a for a, _, _ in args], *ties)


def along(array, dim, block, first=0):
    shape = array.shape
    if dim is None:
        return (array, tuple(shape), lambda i: (0,) * len(shape))
    sizes = tuple(block if d == dim else size for d, size in enumerate(shape))
    return (
        array,
        sizes,
        lambda i: tuple(i + first if d == dim else 0 for d in range(len(shape))),
    )


def by_channel(kernel, block, channels, args, outs, us, scratch=(), ties=(), first=0):
    return over_blocks(
        kernel,
        channels // block,
        [along(a, d, block, first) if d != "smem" else (a, None, None) for a, d in args],
        [along(o, d, block) for o, d in outs],
        us,
        scratch,
        ties,
    )


def lane_sums(values):
    width = min(128, values.shape[1])
    total = values[:, :width]
    for k in range(1, values.shape[1] // width):
        total = total + values[:, k * width : (k + 1) * width]
    return total


def gated_kernel(mp, at_ref, valid_ref, x_ref, residual_ref, *refs):
    up_refs, w_refs, refs = refs[:mp], refs[mp : 2 * mp], refs[2 * mp :]
    bias_ref, gain_ref, upstream_ref, hidden_ref, normed_ref, *refs = refs
    value_ref, opening_ref, line_ref = refs
    features = w_refs[0].shape[0] // 2

    def rows(k):
        return pl.ds(pl.multiple_of(at_ref[k] * features, features), features)

    for k in range(mp):
        upstream_ref[rows(k), :] = (up_refs[k][...].astype(f32) * valid_ref[...]).astype(bf16)
    x = x_ref[...]
    squares = branches = inner = 0.0
    for k in range(mp):
        own = slice(k * features, (k + 1) * features)
        value = nn(w_refs[k][:features], x) + bias_ref[0, own, 0:1]
        gate = nn(w_refs[k][features:], x) + bias_ref[1, own, 0:1]
        opening = 1.0 / (1.0 + jnp.exp(-gate))
        branch = value * opening
        residual = residual_ref[rows(k), :].astype(f32)
        hidden = residual + branch
        hidden_ref[own, :] = hidden
        value_ref[own, :] = value
        opening_ref[own, :] = opening
        squares += summed(residual * residual)
        branches += summed(branch * branch)
        inner += summed(hidden * hidden)
    scale = lax.rsqrt(inner / (mp * features) + epsilon)
    for k in range(mp):
        own = slice(k * features, (k + 1) * features)
        normed_ref[rows(k), :] = (hidden_ref[own, :] * scale * gain_ref[own, 0:1]).astype(bf16)
    line_ref[0:1, :] = scale
    line_ref[1:2, :] = squares
    line_ref[2:3, :] = branches
    line_ref[3:8, :] = jnp.zeros((5, scale.shape[1]), f32)


def hidden_kernel(
    blocks, first, normed_ref, upstream_ref, up_a_ref, up_b_ref, down_a_ref, down_b_ref, bias_ref,
    *refs,
):
    if first:
        feed_out, grad_out, shrink_ref, expand_ref, line_ref, up_ref, down_ref = refs
    else:
        feed_in, grad_in, feed_out, grad_out, shrink_ref, expand_ref, line_ref, up_ref, down_ref = (
            refs
        )
    step = pl.program_id(0)

    @pl.when(step < blocks)
    def _():
        up_ref[...] = up_a_ref[...]
        down_ref[...] = down_a_ref[...]

    @pl.when(step >= blocks)
    def _():
        up_ref[...] = up_b_ref[...].reshape(up_ref.shape)
        down_ref[...] = down_b_ref[...].reshape(up_ref.shape)

    @pl.when(step == 0)
    def _():
        if first:
            feed_out[...] = jnp.zeros_like(feed_out)
            grad_out[...] = jnp.zeros_like(grad_out)
        else:
            feed_out[...] = feed_in[...]
            grad_out[...] = grad_in[...]

    expanded = nn(up_ref[...], normed_ref[...]) + bias_ref[:, 0:1]
    lifted, slope = gelu_pair(expanded)
    lifted = lifted.astype(bf16)
    grad = (nn(down_ref[...], upstream_ref[...]) * slope).astype(bf16)
    shrink_ref[...] = nt(lifted, upstream_ref[...]).astype(bf16)
    expand_ref[0] = nt(normed_ref[...], grad).astype(bf16)
    line_ref[...] = lane_sums(grad.astype(f32))
    feed_out[...] += tn(down_ref[...], lifted)
    grad_out[...] += tn(up_ref[...], grad)


def gated_back_kernel(
    mp, at_ref, grad_ref, hidden_ref, value_ref, opening_ref, upstream_ref, line_ref, *refs
):
    w_refs, refs = refs[:mp], refs[mp:]
    gain_ref, lifted_ref, grad_hidden_ref, both_ref, sums_ref = refs

    @pl.when(pl.program_id(0) == 0)
    def _():
        sums_ref[...] = jnp.zeros_like(sums_ref)

    features = w_refs[0].shape[0] // 2

    def rows(k):
        return pl.ds(pl.multiple_of(at_ref[k] * features, features), features)

    scale = line_ref[0:1, :]
    dot = 0.0
    for k in range(mp):
        own = slice(k * features, (k + 1) * features)
        dot += summed(grad_ref[rows(k), :] * gain_ref[own, 0:1] * hidden_ref[own, :])
    cubic = scale * scale * scale * dot / (mp * features)
    lifted = 0.0
    for k in range(mp):
        own = slice(k * features, (k + 1) * features)
        hidden = hidden_ref[own, :]
        grad = grad_ref[rows(k), :]
        upstream = upstream_ref[rows(k), :].astype(f32)
        grad_hidden = scale * grad * gain_ref[own, 0:1] - hidden * cubic + upstream
        grad_hidden_ref[rows(k), :] = grad_hidden.astype(bf16)
        opening = opening_ref[own, :]
        grad_value = grad_hidden * opening
        grad_gate = (grad_value * value_ref[own, :] * (1.0 - opening)).astype(bf16)
        grad_value = grad_value.astype(bf16)
        sums_ref[k, 0] += lane_sums(grad_value.astype(f32))
        sums_ref[k, 1] += lane_sums(grad_gate.astype(f32))
        sums_ref[k, 2] += lane_sums(grad * hidden * scale)
        sums_ref[k, 3] += lane_sums(upstream)
        both = jnp.concatenate([grad_value, grad_gate], axis=0)
        both_ref[2 * k * features : 2 * (k + 1) * features, :] = both
        lifted += tn(w_refs[k][...], both)
    lifted_ref[...] = lifted.astype(bf16)


def gated_terms_kernel(
    features, at_ref, both_ref, x_ref, hidden_ref, feed_ref, bias_ref,
    near_ref, far_ref, result_ref, line_ref,
):
    step = pl.program_id(0)
    terms = nt(x_ref[...], both_ref[...]).astype(bf16)
    rows = pl.ds(pl.multiple_of(at_ref[step] * features, features), features)
    feed = feed_ref[rows, :] + bias_ref[:, 0:1]
    result_ref[rows, :] = (hidden_ref[...] + feed).astype(bf16)

    @pl.when(step == 0)
    def _():
        line_ref[...] = jnp.zeros_like(line_ref)

    line_ref[0:1, :] += summed(feed * feed)

    @pl.when(step < 2)
    def _():
        near_ref[0] = terms

    @pl.when(step >= 2)
    def _():
        far_ref[0] = terms


def swap(values, axis, bit):
    size = lax.axis_size(axis)
    return lax.ppermute(values, axis, [(i, i ^ bit) for i in range(size)])


def added(a, b):
    return (a.astype(f32) + b.astype(f32)).astype(bf16)


def axis_total(values, axis):
    bit = 1
    while bit < lax.axis_size(axis):
        values = values + swap(values, axis, bit)
        bit *= 2
    return values


def bits_of(axis):
    return [1 << k for k in range(lax.axis_size(axis).bit_length() - 1)]


def axis_of(bit):
    return 0 if bit == 0 else 1 + len(bits_of("seq")) - bit.bit_length()


def sent_down(terms, bit):
    if bit == 0:
        return terms[:1], terms[1:], swap(terms[1:], "mp", 2)
    mine = (lax.axis_index("seq") // bit) % 2
    kept = lax.dynamic_slice_in_dim(terms, mine, 1, axis_of(bit))
    sent = lax.dynamic_slice_in_dim(terms, 1 - mine, 1, axis_of(bit))
    return kept, sent, swap(sent, "seq", bit)


def up_step(terms, bit, gate):
    there = lax.optimization_barrier((swap(terms, "seq", bit), gate))[0]
    first = (lax.axis_index("seq") // bit) % 2 == 0
    return jnp.concatenate(
        [jnp.where(first, terms, there), jnp.where(first, there, terms)], axis=axis_of(bit)
    )


def shards(
    inputs,
    valid,
    cotangent,
    first_gain,
    step_size,
    decay_rate,
    frequency,
    readout_real,
    readout_imag,
    skip_weight,
    gated_weight,
    gated_bias,
    second_gain,
    expand_weight,
    expand_bias,
    shrink_weight,
    shrink_bias,
):
    mp = lax.axis_size("mp")
    seq = lax.axis_size("seq")
    mp_me = lax.axis_index("mp")
    seq_me = lax.axis_index("seq")
    features, contexts, local = inputs.shape
    chunk = min(CHUNK, local)
    chunks = local // chunk
    rows = contexts * chunks
    modes = decay_rate.shape[1]
    tokens = local
    hidden_own = expand_weight.shape[1]
    group = features // seq

    bits_at = [(k // 2) + 2 * (k % 2) for k in range(mp)]
    device_at = [jnp.bitwise_xor(mp_me, bit) for bit in bits_at]
    at = jnp.stack(device_at).astype(jnp.int32)

    def exchanged(values):
        sent = [lax.dynamic_index_in_dim(values, device_at[k], 0, keepdims=False) for k in range(mp)]
        return [sent[0]] + [swap(sent[k], "mp", bits_at[k]) for k in range(1, mp)]

    def returned(values):
        return lax.all_to_all(values.reshape(mp, features, local), "mp", 0, 0, tiled=True)

    def after(value, earlier):
        return lax.optimization_barrier((value, earlier))[0]

    def all_places(own, upper):
        return own, upper, swap(own, "mp", 1), swap(upper, "mp", 1)

    gated_own = gated_weight.transpose(1, 2, 0).reshape(2 * features, D)
    small = jnp.concatenate([gated_bias.reshape(-1), second_gain, expand_bias, shrink_bias])
    by_context = inputs.swapaxes(0, 1)
    squares = jnp.sum(jnp.square(by_context.astype(f32)), axis=1)
    sent = jnp.concatenate([squares.reshape(-1), small])
    flats = [sent] + [swap(sent, "mp", bits_at[k]) for k in range(1, mp)]
    small_places = jnp.stack([v[contexts * local :] for v in flats])
    square_one = sum(v[: contexts * local] for v in flats).reshape(contexts, local)

    part = hidden_own // seq

    expand_own = after(expand_weight, sent).T
    slices_sent = jnp.stack(
        [
            lax.dynamic_slice_in_dim(expand_own, seq_me * part, part, 0),
            lax.dynamic_slice_in_dim(shrink_weight, seq_me * part, part, 0),
        ]
    )
    slices = swap(slices_sent, "mp", 2)
    residual = lax.all_to_all(by_context, "mp", 0, 0, tiled=True)
    expand_far = swap(expand_own, "mp", 1)

    cut = [0, 2 * features]
    cut += [cut[-1] + features]
    cut += [cut[-1] + hidden_own]
    cut += [cut[-1] + features]

    def wide(values):
        return jnp.broadcast_to(values[..., None], values.shape + (128,))

    gated_bias_wide = wide(
        small_places[:, : cut[1]].reshape(mp, 2, features).swapaxes(0, 1).reshape(2, D)
    )
    gain_two_wide = wide(small_places[:, cut[1] : cut[2]].reshape(D))
    shrink_bias_wide = wide(small_places[:, cut[3] :].reshape(D))
    near_bias = wide(small_places[:2, cut[2] : cut[3]].reshape(-1))
    far_bias = wide(small_places[2:, cut[2] : cut[3]].reshape(-1))

    scale_one = lax.rsqrt(square_one / D + epsilon)
    scale_rows = scale_one.reshape(rows, chunk)

    w = discretized(step_size, decay_rate, frequency)
    coeff = coefficients(step_size, decay_rate, frequency, readout_real, readout_imag)

    def handed(ends, backward, ties=()):
        terms = lax.all_to_all(ends, "seq", 0, 0, tiled=True)
        (states,) = over_blocks(
            functools.partial(hand_kernel, seq, backward),
            1,
            [along(terms, None, 0), along(z_device, None, 0)],
            [along(out(terms.shape, bf16), None, 0)],
            3,
            (),
            ties,
        )
        return lax.all_to_all(states, "seq", 0, 0, tiled=True)

    def out(shape, dtype):
        return jax.ShapeDtypeStruct(shape, dtype)

    block, small_block = min(32, features), min(16, features)
    state_shape = out((features, rows, 4 * modes), f32)
    end_shape = out((features, contexts, 4 * modes), bf16)
    row_shape = out((features, rows, chunk), bf16)
    context_shape = out((contexts, features, local), bf16)
    table_shape = out((features, 4 * modes, chunk), bf16)
    sum_shape = out((7, features, 4 * modes), f32)
    line_shape = out((features, chunk), f32)
    flat = [pltpu.VMEM((block * rows, chunk), f32)]
    small_flat = [pltpu.VMEM((small_block * rows, chunk), f32)]
    skip_wide = jnp.broadcast_to(skip_weight[:, None], (features, chunk))
    gain_wide = jnp.broadcast_to(first_gain[:, None], (features, chunk))
    scan_steps = max(1, (chunks - 1).bit_length())
    pars, whole_pars, one, two, taps = by_channel(
        functools.partial(tables_kernel, chunk, scan_steps, local),
        small_block,
        features,
        [
            (step_size[:, None], 0),
            (decay_rate, 0),
            (frequency, 0),
            (readout_real, 0),
            (readout_imag, 0),
        ],
        [
            (out((features, 2 * scan_steps + 2, 4 * modes), f32), 0),
            (out((features, 2, 4 * modes), f32), 0),
            (table_shape, 0),
            (table_shape, 0),
            (line_shape, 0),
        ],
        10,
        [pltpu.VMEM((small_block, 8, 4 * modes), f32)],
        (sent,),
    )
    gated_upper = swap(gated_own, "mp", 2)
    shrink_far = swap(shrink_weight, "mp", 1)
    z_device = lax.dynamic_slice_in_dim(whole_pars, seq_me * group, group, 0)
    normed_one, terms, ends = by_channel(
        functools.partial(states_kernel, chunks),
        block,
        features,
        [(by_context, 1), (scale_rows, None), (gain_wide, 0), (two, 0), (pars, 0)],
        [(row_shape, 0), (state_shape, 0), (end_shape, 0)],
        8,
        flat,
        (slices_sent, residual),
    )
    upper = lax.all_gather(after(slices, normed_one), "seq", axis=0)
    upstream_parts = exchanged(after(cotangent, normed_one).swapaxes(0, 1))
    gated_places = (
        gated_own,
        gated_upper,
        swap(after(gated_own, normed_one), "mp", 1),
        swap(gated_upper, "mp", 1),
    )
    states_in = handed(ends, False, (shrink_far,))
    mixed, states, lifted_one = by_channel(
        functools.partial(mix_kernel, chunks),
        block,
        features,
        [
            (normed_one, 0),
            (terms, 0),
            (states_in, 0),
            (one, 0),
            (taps, 0),
            (skip_wide, 0),
            (pars, 0),
        ],
        [(row_shape, 0), (state_shape, 0), (context_shape, 1)],
        14,
        flat,
        (gated_upper,),
    )


    lifted_sent = after(lifted_one, (*upstream_parts, *gated_places))
    whole_one = lax.all_to_all(lifted_sent, "mp", 0, 0, tiled=True).reshape(D, tokens)
    upper_far = swap(after(upper, whole_one), "mp", 1)
    own_valid = lax.dynamic_slice_in_dim(valid, mp_me, 1, 0).astype(f32)

    token_block = min(256, tokens)
    token_steps = tokens // token_block
    wide_f = out((D, tokens), f32)
    wide_b = out((D, tokens), bf16)
    line_out = out((8, tokens), f32)

    def by_tokens(kernel, args, outs, us, scratch=(), ties=()):
        return over_blocks(
            kernel,
            token_steps,
            [along(a, d, token_block) if d != "smem" else (a, None, None) for a, d in args],
            [along(o, d, token_block) for o, d in outs],
            us,
            scratch,
            ties,
            60,
        )

    upstream, hidden, normed_two, value_part, opening, lines = by_tokens(
        functools.partial(gated_kernel, mp),
        [
            (at, "smem"),
            (own_valid, 1),
            (whole_one, 1),
            (residual.reshape(D, tokens), 1),
            *[(part_k, 1) for part_k in upstream_parts],
            *[(w_place, None) for w_place in gated_places],
            (gated_bias_wide, None),
            (gain_two_wide, None),
        ],
        [
            (wide_b, 1),
            (wide_f, 1),
            (wide_b, 1),
            (wide_f, 1),
            (wide_f, 1),
            (line_out, 1),
        ],
        12,
    )

    hidden_block = min(256, hidden_own)
    blocks = hidden_own // hidden_block
    near_rows = 2 * hidden_own

    parts = hidden_block // part
    low = ((hidden_block, D), lambda i: (jnp.minimum(i, blocks - 1), 0))
    grad_shape = out((near_rows, D), bf16)

    def half(which):
        return ((parts, 1, part, D), lambda i: (jnp.maximum(i - blocks, 0), which, 0, 0))

    def by_hidden(up, down, both, bias, carried, ties=()):
        first = carried is None
        args = [
            along(normed_two, None, 0),
            along(upstream, None, 0),
            (up, *low),
            (both, *half(0)),
            (down, *low),
            (both, *half(1)),
            along(bias, 0, hidden_block),
        ]
        if not first:
            args += [along(c, None, 0) for c in carried]
        return over_blocks(
            functools.partial(hidden_kernel, blocks, first),
            2 * blocks,
            args,
            [
                along(wide_f, None, 0),
                along(wide_f, None, 0),
                along(grad_shape, 0, hidden_block),
                (
                    out((2, D, hidden_own), bf16),
                    (1, D, hidden_block),
                    lambda i: (i // blocks, 0, i % blocks),
                ),
                along(out((near_rows, min(128, tokens)), f32), 0, hidden_block),
            ],
            38,
            [pltpu.VMEM((hidden_block, D), bf16)] * 2,
            ties,
        )

    feed, grad_normed_two, shrink_far_g, expand_far_g, far_lines = by_hidden(
        expand_far, shrink_far, upper_far, far_bias, None
    )
    core_shrink, core_expand = swap(shrink_far_g, "mp", 1), swap(expand_far_g, "mp", 1)
    feed, grad_normed_two, shrink_near_g, expand_near_g, near_lines = by_hidden(
        expand_own, shrink_weight, upper, near_bias, (feed, grad_normed_two)
    )
    bits = bits_of("seq")
    split = (2,) * (1 + len(bits))
    cubes = split + (-1, D)
    first, second, third, rest = bits[0], bits[1], bits[2], bits[3:]
    upper_bit = 0
    s_kept, s_sent, s_there = sent_down(added(shrink_near_g, core_shrink).reshape(cubes), first)
    e_kept, e_sent, e_there = sent_down(added(expand_near_g, core_expand).reshape(split + (-1, hidden_own)), second)

    def onwards(kept, there, bit):
        return sent_down(added(kept, there), bit)

    sums_out = out((mp, 4, features, min(128, token_block)), f32)
    grad_lifted_one, grad_hidden, both_g, sums = by_tokens(
        functools.partial(gated_back_kernel, mp),
        [
            (at, "smem"),
            (grad_normed_two, 1),
            (hidden, 1),
            (value_part, 1),
            (opening, 1),
            (upstream, 1),
            (lines, 1),
            *[(w_place, None) for w_place in gated_places],
            (gain_two_wide, None),
        ],
        [(wide_b, 1), (wide_b, 1), (out((2 * D, tokens), bf16), 1), (sums_out, None)],
        14,
        (),
        (s_sent, e_sent),
    )
    own_lifted_one = returned(grad_lifted_one)
    gated_near, gated_far, result, feed_lines = over_blocks(
        functools.partial(gated_terms_kernel, features),
        mp,
        [
            (at, None, None),
            along(both_g, 0, 2 * features),
            along(whole_one, None, 0),
            along(hidden, 0, features),
            along(feed, None, 0),
            along(shrink_bias_wide, 0, features),
        ],
        [
            (
                out((2, D, 2 * features), bf16),
                (1, D, 2 * features),
                lambda i: (jnp.minimum(i, 1), 0, 0),
            ),
            (
                out((2, D, 2 * features), bf16),
                (1, D, 2 * features),
                lambda i: (jnp.maximum(i - 2, 0), 0, 0),
            ),
            along(wide_b, None, 0),
            along(line_out, None, 0),
        ],
        10,
    )
    core_gated = swap(gated_far, "mp", 1)

    grad_mixed, adj_terms, adj_ends = by_channel(
        functools.partial(ends_kernel, chunks),
        block,
        features,
        [(own_lifted_one, 1), (mixed, 0), (one, 0), (pars, 0)],
        [(row_shape, 0), (state_shape, 0), (end_shape, 0)],
        10,
        flat,
        (s_there, e_there, core_gated),
    )
    s_kept, s_sent, s_there = onwards(s_kept, s_there, second)
    e_kept, e_sent, e_there = onwards(e_kept, e_there, first)
    g_kept, g_sent, g_there = sent_down(added(gated_near, core_gated).reshape(split + (-1, 2 * features)), first)
    adjoint_in = handed(adj_ends, True, (s_sent, e_sent, g_sent))
    s_kept, s_sent, s_there = onwards(s_kept, s_there, third)
    e_kept, e_sent, e_there = onwards(e_kept, e_there, upper_bit)
    (sums_one,) = by_channel(
        sums_kernel,
        small_block,
        features,
        [(grad_mixed, 0), (normed_one, 0), (states, 0), (adj_terms, 0), (one, 0)],
        [(sum_shape, 1)],
        20,
        (),
        (s_sent, e_sent, adjoint_in),
    )
    own_hidden = returned(after(grad_hidden, adjoint_in))
    s_there, e_there, g_there = after((s_there, e_there, g_there), sums_one)
    g_kept, g_sent, g_there = onwards(g_kept, g_there, upper_bit)
    s_kept, s_sent, s_there = onwards(s_kept, s_there, upper_bit)
    e_kept, e_sent, e_there = onwards(e_kept, e_there, third)
    half = features // 2 // small_block
    back_args = [
        (grad_mixed, 0),
        (adj_terms, 0),
        (adjoint_in, 0),
        (normed_one, 0),
        (states, 0),
        (two, 0),
        (taps, 0),
        (skip_wide, 0),
        (pars, 0),
        (by_context, 1),
        (scale_rows, None),
        (gain_wide, 0),
    ]

    def back(first_block, ties):
        return by_channel(
            functools.partial(back_kernel, chunks),
            small_block,
            features // 2,
            back_args,
            [
                (out((contexts, features // 2, local), bf16), 1),
                (out((4, features // 2, 4 * modes), f32), 1),
                (out((rows, chunk), f32), None),
                (out((features // 2, chunk), f32), 0),
            ],
            12,
            small_flat,
            ties,
            first_block,
        )

    def exchange(values, bit, gate):
        return added(values, after(swap(values, "seq", bit), gate))

    low = back(0, (s_sent, e_sent, g_sent, sums_one, own_hidden))
    s_there, e_there, g_there = after((s_there, e_there, g_there), low[2])
    s_all, e_all, g_all = added(s_kept, s_there), added(e_kept, e_there), added(g_kept, g_there)
    for bit in rest:
        s_all, e_all = (added(*sent_down(v, bit)[::2]) for v in (s_all, e_all))
        g_all = exchange(g_all, bit, low[2])
    both_parts = jnp.stack([s_all.reshape(-1, D), e_all.reshape(-1, hidden_own)])
    both_all = lax.all_gather(both_parts, "seq", axis=0)
    high = back(half, (both_parts, g_all, low[2]))
    g_all = exchange(g_all, third, high[2])
    result = returned(after(result, (own_hidden, low[2])))
    grad_first_gain = jnp.sum(jnp.concatenate([low[3], high[3]]), axis=1)

    dot_one = axis_total(low[2] + high[2], "mp").reshape(contexts, local)
    cubic = scale_one * scale_one * scale_one * dot_one / D
    (grad_inputs,) = over_blocks(
        functools.partial(last_kernel, half),
        features // small_block,
        [
            along(by_context, 1, small_block),
            (low[0], (contexts, small_block, local), lambda i: (0, jnp.minimum(i, half - 1), 0)),
            (high[0], (contexts, small_block, local), lambda i: (0, jnp.maximum(i - half, 0), 0)),
            along(own_hidden, 1, small_block),
            along(scale_one, None, 0),
            along(cubic, None, 0),
            along(gain_wide, 0, small_block),
        ],
        [along(out(inputs.shape, f32), 0, small_block)],
        8,
    )

    stats = jnp.stack(
        [
            jnp.sum(own_valid[0] * lines[1]),
            jnp.sum(own_valid[0] * lines[2]),
            jnp.sum(own_valid[0] * feed_lines[0]),
            jnp.sum(own_valid[0]),
        ]
    )
    sums = jnp.sum(sums, axis=3).reshape(mp, 4 * features)
    sums = jnp.concatenate([sums, jnp.broadcast_to(stats, (mp, 4))], axis=1)
    near = jnp.concatenate([sums[:2], jnp.sum(near_lines, axis=1).reshape(2, hidden_own)], axis=1)
    far = jnp.concatenate([sums[2:], jnp.sum(far_lines, axis=1).reshape(2, hidden_own)], axis=1)
    near = near + swap(far, "mp", 1)
    bias_size = near.shape[1]

    def quarter(values, k):
        return values[:, k * modes : (k + 1) * modes]

    def product_sums(lines, k):
        plain, turned = lines[k], lines[k + 1]
        return (
            quarter(plain, 0) - quarter(plain, 1),
            quarter(turned, 1) + quarter(turned, 3),
        )

    inverse = power(w, -1.0)
    within = [
        cmul(inverse, (quarter(sums_one[k], 0), quarter(sums_one[k], 1))) for k in (4, 5)
    ]
    sum_a = cadd(product_sums(sums_one, 0), within[0])
    def both_halves(k):
        pairs = [product_sums(part_k[1], k) for part_k in (low, high)]
        return tuple(jnp.concatenate(v) for v in zip(*pairs))

    crossing = both_halves(0)
    part_a = product_sums(sums_one, 2)
    part_p = both_halves(2)
    sum_b = [
        float(chunk) * crossing[k] + part_a[k] - part_p[k] + within[1][k] for k in range(2)
    ]
    lines_late = jnp.concatenate(
        [sums_one[6, :, 0], grad_first_gain, near.reshape(-1)]
    )
    width = 4 * modes
    pad = -lines_late.shape[0] % width
    late = jnp.concatenate(
        [
            jnp.concatenate([*sum_a, *sum_b], axis=1),
            jnp.pad(lines_late, (0, pad)).reshape(-1, width),
        ],
        axis=0,
    )
    for bit in bits:
        late = late + swap(late, "seq", bit)
    g_all = exchange(g_all, second, grad_inputs)
    g_all = up_step(g_all, first, late)
    result = result.reshape(contexts, features, local)
    (result,) = by_channel(
        turned_kernel, 2 * block, features, [(result, 1)], [(out(inputs.shape, bf16), 0)], 5
    )
    grad_shrink = both_all[:, 0].reshape(-1, D).astype(f32)
    grad_expand = both_all[:, 1].reshape(D, hidden_own).astype(f32)
    grad_gated = g_all.reshape(D, 2, features).astype(f32)
    lines_late = late[features:].reshape(-1)
    late = late[:features]
    sum_a = (quarter(late, 0), quarter(late, 1))
    sum_b = (quarter(late, 2), quarter(late, 3))
    grad_skip = lines_late[:features]
    grad_first_gain = lines_late[features : 2 * features]
    bias_own = lines_late[2 * features : 2 * features + 2 * bias_size].reshape(2, bias_size)
    bias_own = bias_own[0] + swap(bias_own[1], "mp", 2)

    def form(step, decay, freq, out_real, out_imag):
        c = coefficients(step, decay, freq, out_real, out_imag)
        moved = cmul(coeff, discretized(step, decay, freq))
        return 2.0 * jnp.sum(
            c[0] * sum_a[0] - c[1] * sum_a[1] + moved[0] * sum_b[0] - moved[1] * sum_b[1]
        )

    kernel_grads = jax.grad(form, argnums=(0, 1, 2, 3, 4))(
        step_size, decay_rate, frequency, readout_real, readout_imag
    )
    ends_at = [0, 2 * features, 3 * features, 4 * features, 4 * features + 4]
    totals = bias_own[ends_at[3] : ends_at[4]]
    count = totals[3]
    rms = jnp.sqrt(totals[:3] / (count * D))
    return (
        result,
        grad_inputs,
        grad_first_gain,
        *kernel_grads,
        grad_skip,
        grad_gated,
        bias_own[: ends_at[1]].reshape(2, features),
        bias_own[ends_at[1] : ends_at[2]],
        grad_expand,
        bias_own[ends_at[4] :],
        grad_shrink,
        bias_own[ends_at[2] : ends_at[3]],
        rms[0],
        rms[1],
        rms[2],
    )


def solution(mesh):
    placed = (
        P("mp", None, "seq"),
        P(None, "seq"),
        P("mp", None, "seq"),
        P("mp"),
        P("mp"),
        P("mp", None),
        P("mp", None),
        P("mp", None),
        P("mp", None),
        P("mp"),
        P(None, None, "mp"),
        P(None, "mp"),
        P("mp"),
        P(None, "mp"),
        P("mp"),
        P("mp", None),
        P("mp"),
    )
    return jax.shard_map(
        shards,
        mesh=mesh,
        in_specs=placed,
        out_specs=(
            P("mp", None, "seq"),
            P("mp", None, "seq"),
            P("mp"),
            P("mp"),
            P("mp", None),
            P("mp", None),
            P("mp", None),
            P("mp", None),
            P("mp"),
            P(None, None, "mp"),
            P(None, "mp"),
            P("mp"),
            P(None, "mp"),
            P("mp"),
            P("mp", None),
            P("mp"),
            P(),
            P(),
            P(),
        ),
        check_vma=False,
    )
```

```python
import functools

import jax
import jax.numpy as jnp
from jax import lax
from jax.experimental import pallas as pl
from jax.experimental.pallas import tpu as pltpu
from jax.sharding import PartitionSpec as P

D = 1024
epsilon = 1e-05
CHUNK = 128
f32 = jnp.float32
bf16 = jnp.bfloat16


def contract(left, right, left_dim, right_dim):
    return lax.dot_general(
        left, right, (((left_dim,), (right_dim,)), ((), ())), preferred_element_type=f32
    )


def nt(left, right):
    return lax.dot_general(left, right, (((1,), (1,)), ((), ())), preferred_element_type=f32)


def nn(left, right):
    return lax.dot_general(left, right, (((1,), (0,)), ((), ())), preferred_element_type=f32)


def tn(left, right):
    return lax.dot_general(left, right, (((0,), (0,)), ((), ())), preferred_element_type=f32)


def gelu_pair(v):
    k0 = 0.7978845608028654
    k1 = 0.044715
    square = v * v
    t = jnp.tanh(k0 * v * (1.0 + k1 * square))
    half = 0.5 * (1.0 + t)
    return v * half, half + 0.5 * v * (1.0 - t * t) * k0 * (1.0 + 3.0 * k1 * square)


def cmul(a, b):
    return (a[0] * b[0] - a[1] * b[1], a[0] * b[1] + a[1] * b[0])


def cadd(a, b):
    return (a[0] + b[0], a[1] + b[1])


def discretized(step, decay, freq):
    return step[:, None] * (-decay), step[:, None] * freq


def coefficients(step, decay, freq, out_real, out_imag):
    a_real, a_imag = -decay, freq
    w_real, w_imag = discretized(step, decay, freq)
    growth = jnp.exp(w_real)
    minus_real = growth * jnp.cos(w_imag) - 1.0
    minus_imag = growth * jnp.sin(w_imag)
    modulus = a_real * a_real + a_imag * a_imag
    ratio_real = (minus_real * a_real + minus_imag * a_imag) / modulus
    ratio_imag = (minus_imag * a_real - minus_real * a_imag) / modulus
    return (
        out_real * ratio_real - out_imag * ratio_imag,
        out_real * ratio_imag + out_imag * ratio_real,
    )


def power(w, exponent):
    envelope = jnp.exp(w[0] * exponent)
    return envelope * jnp.cos(w[1] * exponent), envelope * jnp.sin(w[1] * exponent)


GROUP = 8


def four(pair, axis=-1):
    return jnp.concatenate([pair[0], pair[1], -pair[1], pair[0]], axis=axis)


def turn(values):
    return pltpu.roll(values, values.shape[1] // 2, 1)


def row_of_chunk(shape, chunks):
    return lax.rem(lax.broadcasted_iota(jnp.int32, shape, 0), chunks)


def groups_of(block):
    size = min(GROUP, block)
    return [range(k, k + size) for k in range(0, block, size)]


def moved_rows(values, step, chunks, backward):
    rows, width = values.shape
    if chunks == 8:
        cube = values.reshape(rows // 8, 8, width)
        place = lax.broadcasted_iota(jnp.int32, cube.shape, 1)
        if backward:
            cube = jnp.where(place < 8 - step, pltpu.roll(cube, 8 - step, 1), 0.0)
        else:
            cube = jnp.where(place >= step, pltpu.roll(cube, step, 1), 0.0)
        return cube.reshape(rows, width)
    place = row_of_chunk(values.shape, chunks)
    if backward:
        return jnp.where(place < chunks - step, pltpu.roll(values, rows - step, 0), 0.0)
    return jnp.where(place >= step, pltpu.roll(values, step, 0), 0.0)


def scan_rows(states, pars_ref, group, chunks, backward):
    step, k = 1, 0
    while step < chunks:
        moved = [moved_rows(s, step, chunks, backward) for s in states]
        turned = [turn(m) for m in moved]
        states = [
            s + m * pars_ref[i, 2 * k : 2 * k + 1, :] + t * pars_ref[i, 2 * k + 1 : 2 * k + 2, :]
            for i, s, m, t in zip(group, states, moved, turned)
        ]
        step, k = 2 * step, k + 1
    return states


def entered(terms, into, chunks, backward):
    rows, width = terms.shape
    wide = jnp.concatenate(
        [jnp.broadcast_to(into[b : b + 1], (chunks, width)) for b in range(rows // chunks)], axis=0
    )
    if chunks == 1:
        return wide
    place = row_of_chunk(terms.shape, chunks)
    edge = chunks - 1 if backward else 0
    return jnp.where(place == edge, wide, moved_rows(terms, 1, chunks, backward))


def weighed(states, turned, pars_ref, i):
    last = pars_ref.shape[1]
    return (
        states * pars_ref[i, last - 2 : last - 1, :] + turned * pars_ref[i, last - 1 : last, :]
    ).astype(bf16)


def toeplitz(taps):
    size = taps.shape[-1]
    rolled = pltpu.roll(jnp.broadcast_to(taps, (size, size)), 0, 1, stride=1, stride_axis=0)
    rows = lax.broadcasted_iota(jnp.int32, (size, size), 0)
    lanes = lax.broadcasted_iota(jnp.int32, (size, size), 1)
    return jnp.where(lanes >= rows, rolled, 0.0).astype(bf16)


def reversal(size):
    rows = lax.broadcasted_iota(jnp.int32, (size, size), 0)
    lanes = lax.broadcasted_iota(jnp.int32, (size, size), 1)
    return jnp.where(rows + lanes == size - 1, 1.0, 0.0).astype(bf16)


def circle(turns):
    x = (turns - jnp.floor(turns + 0.5)) * 3.14159265358979
    s = x * x
    sine = x * (
        1.0
        + s
        * (
            -1.0 / 6.0
            + s
            * (
                1.0 / 120.0
                + s * (-1.0 / 5040.0 + s * (1.0 / 362880.0 + s * (-1.0 / 39916800.0)))
            )
        )
    )
    cosine = 1.0 + s * (
        -0.5
        + s
        * (
            1.0 / 24.0
            + s
            * (
                -1.0 / 720.0
                + s * (1.0 / 40320.0 + s * (-1.0 / 3628800.0 + s * (1.0 / 479001600.0)))
            )
        )
    )
    return 1.0 - 2.0 * sine * sine, 2.0 * sine * cosine


def tables_kernel(
    chunk, steps, local, step_ref, decay_ref, freq_ref, real_ref, imag_ref,
    pars_ref, whole_ref, one_ref, two_ref, taps_ref, line_ref,
):
    block, modes = decay_ref.shape
    size = one_ref.shape[2]
    step = step_ref[...]
    a_real, a_imag = -decay_ref[...], freq_ref[...]
    w_real, turns = step * a_real, step * a_imag * 0.15915494309189535

    def z_power(exponent):
        envelope = jnp.exp(w_real * exponent)
        cosine, sine = circle(turns * exponent)
        return envelope * cosine, envelope * sine

    z = z_power(1.0)
    minus_real, minus_imag = z[0] - 1.0, z[1]
    modulus = 1.0 / (a_real * a_real + a_imag * a_imag)
    ratio = (
        (minus_real * a_real + minus_imag * a_imag) * modulus,
        (minus_imag * a_real - minus_real * a_imag) * modulus,
    )
    c = cmul((real_ref[...], imag_ref[...]), ratio)
    zk = z_power(float(local))
    whole = [(zk[0], zk[0], zk[0], zk[0]), (zk[1], zk[1], -zk[1], -zk[1])]
    lines = []
    for k in range(steps):
        zk = z_power(float(chunk * 2**k))
        lines += [(zk[0], zk[0], zk[0], zk[0]), (zk[1], zk[1], -zk[1], -zk[1])]
    lines += [(c[0], -c[0], -c[0], c[0]), (c[1], -c[1], c[1], -c[1])]
    for k, line in enumerate(whole):
        whole_ref[:, k, :] = jnp.concatenate(line, axis=-1)
    for k, line in enumerate(lines):
        pars_ref[:, k, :] = jnp.concatenate(line, axis=-1)
    line_ref[...] = jnp.zeros_like(line_ref)
    for k, line in enumerate((w_real, turns, c[0], c[1], z[0], z[1])):
        line_ref[:, k, 0:modes] = line
    places = lax.broadcasted_iota(jnp.int32, (modes, size), 1).astype(f32)
    flip = reversal(size)
    for i in range(block):
        cols = line_ref[i].T

        def col(k):
            return jnp.broadcast_to(cols[:modes, k : k + 1], (modes, size))

        envelope = jnp.exp(col(0) * places)
        cosine, sine = circle(col(1) * places)
        level = (envelope * cosine, envelope * sine)
        taps_ref[i : i + 1, :] = 2.0 * jnp.sum(
            col(2) * level[0] - col(3) * level[1], axis=0, keepdims=True
        )
        one_ref[i] = four(cmul(level, (col(4), col(5))), 0).astype(bf16)
        two_ref[i] = nn(four(level, 0).astype(bf16), flip).astype(bf16)


def states_kernel(
    chunks, x_ref, scale_ref, gain_ref, two_ref, pars_ref, u_ref, q_ref, end_ref, flat_ref
):
    block, rows, size = u_ref.shape
    for r in range(rows):
        b, j = r // chunks, r % chunks
        flat_ref[pl.ds(r, block, stride=rows), :] = x_ref[b, :, j * size : (j + 1) * size].astype(
            f32
        )
    for group in groups_of(block):
        us = [
            (
                flat_ref[i * rows : (i + 1) * rows, :] * scale_ref[...] * gain_ref[i : i + 1, :]
            ).astype(bf16)
            for i in group
        ]
        qs = [nt(u, two_ref[i]) for i, u in zip(group, us)]
        wholes = scan_rows(qs, pars_ref, group, chunks, False)
        for i, u, q, whole in zip(group, us, qs, wholes):
            u_ref[i] = u
            q_ref[i] = q
            for b in range(rows // chunks):
                last = b * chunks + chunks - 1
                end_ref[i, b : b + 1, :] = whole[last : last + 1, :].astype(bf16)


def hand_kernel(seq, backward, terms_ref, pars_ref, out_ref):
    group = terms_ref.shape[0] // seq
    state = jnp.zeros((group,) + terms_ref.shape[1:], f32)
    half = terms_ref.shape[2] // 2
    for k in range(seq - 1, -1, -1) if backward else range(seq):
        out_ref[k * group : (k + 1) * group] = state.astype(bf16)
        state = (
            state * pars_ref[:, 0:1, :]
            + pltpu.roll(state, half, 2) * pars_ref[:, 1:2, :]
            + terms_ref[k * group : (k + 1) * group].astype(f32)
        )


def mix_kernel(
    chunks, u_ref, q_ref, into_ref, one_ref, taps_ref, skip_ref, pars_ref,
    mixed_ref, state_ref, lifted_ref, flat_ref,
):
    block, rows, size = u_ref.shape
    for group in groups_of(block):
        states = [entered(q_ref[i], into_ref[i].astype(f32), chunks, False) for i in group]
        states = scan_rows(states, pars_ref, group, chunks, False)
        for i, s in zip(group, states):
            state_ref[i] = s
        outs = [weighed(s, turn(s), pars_ref, i) for i, s in zip(group, states)]
        near = [nn(u_ref[i], toeplitz(taps_ref[i : i + 1, :])) for i in group]
        ys = [y + nn(o, one_ref[i]) for i, y, o in zip(group, near, outs)]
        mixes = [
            (y + skip_ref[i : i + 1, :] * u_ref[i].astype(f32)).astype(bf16)
            for i, y in zip(group, ys)
        ]
        for i, mixed in zip(group, mixes):
            mixed_ref[i] = mixed
            flat_ref[i * rows : (i + 1) * rows, :] = gelu_pair(mixed.astype(f32))[0]
    for r in range(rows):
        b, j = r // chunks, r % chunks
        lifted_ref[b, :, j * size : (j + 1) * size] = flat_ref[
            pl.ds(r, block, stride=rows), :
        ].astype(bf16)


def ends_kernel(chunks, gl_ref, mixed_ref, one_ref, pars_ref, g_ref, p_ref, end_ref, flat_ref):
    block, rows, size = mixed_ref.shape
    for r in range(rows):
        b, j = r // chunks, r % chunks
        flat_ref[pl.ds(r, block, stride=rows), :] = gl_ref[
            b, :, j * size : (j + 1) * size
        ].astype(f32)
    for group in groups_of(block):
        gs = [
            (
                flat_ref[i * rows : (i + 1) * rows, :] * gelu_pair(mixed_ref[i].astype(f32))[1]
            ).astype(bf16)
            for i in group
        ]
        ps = [nt(g, one_ref[i]) for i, g in zip(group, gs)]
        wholes = scan_rows(ps, pars_ref, group, chunks, True)
        for i, g, p, whole in zip(group, gs, ps, wholes):
            g_ref[i] = g
            p_ref[i] = p
            for b in range(rows // chunks):
                end_ref[i, b : b + 1, :] = whole[b * chunks : b * chunks + 1, :].astype(bf16)


def summed(values):
    return jnp.sum(values, axis=0, keepdims=True)


def sums_kernel(g_ref, u_ref, state_ref, p_ref, one_ref, sum_ref):
    block, rows, size = g_ref.shape
    lanes = lax.broadcasted_iota(jnp.int32, (rows, size), 1).astype(f32)
    row_id = lax.broadcasted_iota(jnp.int32, (size, size), 0)
    lane_id = lax.broadcasted_iota(jnp.int32, (size, size), 1)
    places = lane_id[0:1].astype(f32)
    keep = lane_id <= row_id
    flip = reversal(size)
    for group in groups_of(block):
        flipped = [nt(flip, u_ref[i]).astype(bf16) for i in group]
        pas = [nt((g_ref[i].astype(f32) * lanes).astype(bf16), one_ref[i]) for i in group]
        outers = [nn(f, g_ref[i]) for i, f in zip(group, flipped)]
        lags = [
            summed(jnp.where(keep, pltpu.roll(o, 1, 1, stride=1, stride_axis=0), 0.0))
            for o in outers
        ]
        stacked = []
        for lag in lags:
            parts = []
            for v in (lag, lag * places):
                high = v.astype(bf16).astype(f32)
                parts += [high, v - high]
            stacked += [
                jnp.concatenate(parts + [jnp.zeros((4, size), f32)], axis=0).astype(bf16)
            ]
        withins = [nt(s, one_ref[i]) for i, s in zip(group, stacked)]
        for i, pa, within in zip(group, pas, withins):
            states = state_ref[i]
            p = p_ref[i]
            sum_ref[0, i : i + 1, :] = summed(states * p)
            sum_ref[1, i : i + 1, :] = summed(states * turn(p))
            sum_ref[2, i : i + 1, :] = summed(states * pa)
            sum_ref[3, i : i + 1, :] = summed(states * turn(pa))
            sum_ref[4, i : i + 1, :] = within[0:1] + within[1:2]
            sum_ref[5, i : i + 1, :] = within[2:3] + within[3:4]
            skip = summed(g_ref[i].astype(f32) * u_ref[i].astype(f32))
            sum_ref[6, i : i + 1, :] = jnp.broadcast_to(jnp.sum(skip, axis=1, keepdims=True), (1, size))


def back_kernel(
    chunks, g_ref, p_ref, into_ref, u_ref, state_ref, two_ref, taps_ref, skip_ref, pars_ref,
    x_ref, scale_ref, gain_ref, out_ref, sum_ref, dot_ref, first_ref, flat_ref,
):
    block, rows, size = g_ref.shape

    @pl.when(pl.program_id(0) == 0)
    def _():
        dot_ref[...] = jnp.zeros_like(dot_ref)

    lanes = lax.broadcasted_iota(jnp.int32, (rows, size), 1).astype(f32)
    for group in groups_of(block):
        qps = [nt((u_ref[i].astype(f32) * lanes).astype(bf16), two_ref[i]) for i in group]
        near = [nt(g_ref[i], toeplitz(taps_ref[i : i + 1, :])) for i in group]
        adjoints = [entered(p_ref[i], into_ref[i].astype(f32), chunks, True) for i in group]
        adjoints = scan_rows(adjoints, pars_ref, group, chunks, True)
        turned = [turn(a) for a in adjoints]
        outs = [weighed(a, t, pars_ref, i) for i, a, t in zip(group, adjoints, turned)]
        ys = [y + nn(o, two_ref[i]) for i, y, o in zip(group, near, outs)]
        for i, y, qp, adjoint, t in zip(group, ys, qps, adjoints, turned):
            flat_ref[i * rows : (i + 1) * rows, :] = y + skip_ref[i : i + 1, :] * g_ref[i].astype(
                f32
            )
            states = state_ref[i]
            here = p_ref[i] + adjoint * pars_ref[i, 0:1, :] + t * pars_ref[i, 1:2, :]
            sum_ref[0, i : i + 1, :] = summed(states * here)
            sum_ref[1, i : i + 1, :] = summed(states * turn(here))
            sum_ref[2, i : i + 1, :] = summed(adjoint * qp)
            sum_ref[3, i : i + 1, :] = summed(adjoint * turn(qp))
    gain = gain_ref[...]
    first = jnp.zeros((block, size), f32)
    for r in range(rows):
        b, j = r // chunks, r % chunks
        lanes_r = slice(j * size, (j + 1) * size)
        grad = flat_ref[pl.ds(r, block, stride=rows), :].astype(bf16)
        out_ref[b, :, lanes_r] = grad
        product = grad.astype(f32) * x_ref[b, :, lanes_r].astype(f32)
        dot_ref[r : r + 1, :] += summed(product * gain)
        first += product * scale_ref[r : r + 1, :]
    first_ref[...] = first


def last_kernel(
    half, x_ref, low_ref, high_ref, hidden_ref, scale_ref, cubic_ref, gain_ref, out_ref
):
    gain = gain_ref[:, 0:1]

    def run(grad_ref):
        for b in range(x_ref.shape[0]):
            out_ref[:, b, :] = (
                scale_ref[b : b + 1, :] * gain * grad_ref[b].astype(f32)
                - cubic_ref[b : b + 1, :] * x_ref[b].astype(f32)
                + hidden_ref[b].astype(f32)
            )

    @pl.when(pl.program_id(0) < half)
    def _():
        run(low_ref)

    @pl.when(pl.program_id(0) >= half)
    def _():
        run(high_ref)


def turned_kernel(values_ref, out_ref):
    for b in range(values_ref.shape[0]):
        out_ref[:, b, :] = values_ref[b]


def over_blocks(kernel, steps, args, outs, us, scratch=(), ties=(), vmem=60):
    count = len(args)

    def run(*refs):
        kernel(*refs[:count], *refs[count + len(ties) :])

    moved = sum(a.size * a.dtype.itemsize for a, _, _ in args + outs)
    return pl.pallas_call(
        run,
        grid=(steps,),
        in_specs=[
            pl.BlockSpec(memory_space=pltpu.SMEM) if b is None else pl.BlockSpec(b, m)
            for _, b, m in args
        ]
        + [pl.BlockSpec(memory_space=pl.ANY) for _ in ties],
        out_specs=[pl.BlockSpec(b, m) for _, b, m in outs],
        out_shape=[o for o, _, _ in outs],
        scratch_shapes=list(scratch),
        compiler_params=pltpu.CompilerParams(vmem_limit_bytes=vmem * 1024 * 1024),
        cost_estimate=pl.CostEstimate(
            flops=int(us * 1e9), bytes_accessed=moved, transcendentals=0
        ),
    )(*[a for a, _, _ in args], *ties)


def along(array, dim, block, first=0):
    shape = array.shape
    if dim is None:
        return (array, tuple(shape), lambda i: (0,) * len(shape))
    sizes = tuple(block if d == dim else size for d, size in enumerate(shape))
    return (
        array,
        sizes,
        lambda i: tuple(i + first if d == dim else 0 for d in range(len(shape))),
    )


def by_channel(kernel, block, channels, args, outs, us, scratch=(), ties=(), first=0):
    return over_blocks(
        kernel,
        channels // block,
        [along(a, d, block, first) if d != "smem" else (a, None, None) for a, d in args],
        [along(o, d, block) for o, d in outs],
        us,
        scratch,
        ties,
    )


def lane_sums(values):
    width = min(128, values.shape[1])
    total = values[:, :width]
    for k in range(1, values.shape[1] // width):
        total = total + values[:, k * width : (k + 1) * width]
    return total


def gated_kernel(mp, at_ref, valid_ref, x_ref, residual_ref, *refs):
    up_refs, w_refs, refs = refs[:mp], refs[mp : 2 * mp], refs[2 * mp :]
    bias_ref, gain_ref, upstream_ref, hidden_ref, normed_ref, *refs = refs
    value_ref, opening_ref, line_ref = refs
    features = w_refs[0].shape[0] // 2

    def rows(k):
        return pl.ds(pl.multiple_of(at_ref[k] * features, features), features)

    for k in range(mp):
        upstream_ref[rows(k), :] = (up_refs[k][...].astype(f32) * valid_ref[...]).astype(bf16)
    x = x_ref[...]
    squares = branches = inner = 0.0
    for k in range(mp):
        own = slice(k * features, (k + 1) * features)
        value = nn(w_refs[k][:features], x) + bias_ref[0, own, 0:1]
        gate = nn(w_refs[k][features:], x) + bias_ref[1, own, 0:1]
        opening = 1.0 / (1.0 + jnp.exp(-gate))
        branch = value * opening
        residual = residual_ref[rows(k), :].astype(f32)
        hidden = residual + branch
        hidden_ref[own, :] = hidden
        value_ref[own, :] = value
        opening_ref[own, :] = opening
        squares += summed(residual * residual)
        branches += summed(branch * branch)
        inner += summed(hidden * hidden)
    scale = lax.rsqrt(inner / (mp * features) + epsilon)
    for k in range(mp):
        own = slice(k * features, (k + 1) * features)
        normed_ref[rows(k), :] = (hidden_ref[own, :] * scale * gain_ref[own, 0:1]).astype(bf16)
    line_ref[0:1, :] = scale
    line_ref[1:2, :] = squares
    line_ref[2:3, :] = branches
    line_ref[3:8, :] = jnp.zeros((5, scale.shape[1]), f32)


def hidden_kernel(
    blocks, first, normed_ref, upstream_ref, up_a_ref, up_b_ref, down_a_ref, down_b_ref, bias_ref,
    *refs,
):
    if first:
        feed_out, grad_out, shrink_ref, expand_ref, line_ref, up_ref, down_ref = refs
    else:
        feed_in, grad_in, feed_out, grad_out, shrink_ref, expand_ref, line_ref, up_ref, down_ref = (
            refs
        )
    step = pl.program_id(0)

    @pl.when(step < blocks)
    def _():
        up_ref[...] = up_a_ref[...]
        down_ref[...] = down_a_ref[...]

    @pl.when(step >= blocks)
    def _():
        up_ref[...] = up_b_ref[...].reshape(up_ref.shape)
        down_ref[...] = down_b_ref[...].reshape(up_ref.shape)

    @pl.when(step == 0)
    def _():
        if first:
            feed_out[...] = jnp.zeros_like(feed_out)
            grad_out[...] = jnp.zeros_like(grad_out)
        else:
            feed_out[...] = feed_in[...]
            grad_out[...] = grad_in[...]

    expanded = nn(up_ref[...], normed_ref[...]) + bias_ref[:, 0:1]
    lifted, slope = gelu_pair(expanded)
    lifted = lifted.astype(bf16)
    grad = (nn(down_ref[...], upstream_ref[...]) * slope).astype(bf16)
    shrink_ref[...] = nt(lifted, upstream_ref[...]).astype(bf16)
    expand_ref[0] = nt(normed_ref[...], grad).astype(bf16)
    line_ref[...] = lane_sums(grad.astype(f32))
    feed_out[...] += tn(down_ref[...], lifted)
    grad_out[...] += tn(up_ref[...], grad)


def gated_back_kernel(
    mp, at_ref, grad_ref, hidden_ref, value_ref, opening_ref, upstream_ref, line_ref, *refs
):
    w_refs, refs = refs[:mp], refs[mp:]
    gain_ref, lifted_ref, grad_hidden_ref, both_ref, sums_ref = refs

    @pl.when(pl.program_id(0) == 0)
    def _():
        sums_ref[...] = jnp.zeros_like(sums_ref)

    features = w_refs[0].shape[0] // 2

    def rows(k):
        return pl.ds(pl.multiple_of(at_ref[k] * features, features), features)

    scale = line_ref[0:1, :]
    dot = 0.0
    for k in range(mp):
        own = slice(k * features, (k + 1) * features)
        dot += summed(grad_ref[rows(k), :] * gain_ref[own, 0:1] * hidden_ref[own, :])
    cubic = scale * scale * scale * dot / (mp * features)
    lifted = 0.0
    for k in range(mp):
        own = slice(k * features, (k + 1) * features)
        hidden = hidden_ref[own, :]
        grad = grad_ref[rows(k), :]
        upstream = upstream_ref[rows(k), :].astype(f32)
        grad_hidden = scale * grad * gain_ref[own, 0:1] - hidden * cubic + upstream
        grad_hidden_ref[rows(k), :] = grad_hidden.astype(bf16)
        opening = opening_ref[own, :]
        grad_value = grad_hidden * opening
        grad_gate = (grad_value * value_ref[own, :] * (1.0 - opening)).astype(bf16)
        grad_value = grad_value.astype(bf16)
        sums_ref[k, 0] += lane_sums(grad_value.astype(f32))
        sums_ref[k, 1] += lane_sums(grad_gate.astype(f32))
        sums_ref[k, 2] += lane_sums(grad * hidden * scale)
        sums_ref[k, 3] += lane_sums(upstream)
        both = jnp.concatenate([grad_value, grad_gate], axis=0)
        both_ref[2 * k * features : 2 * (k + 1) * features, :] = both
        lifted += tn(w_refs[k][...], both)
    lifted_ref[...] = lifted.astype(bf16)


def gated_terms_kernel(
    features, at_ref, both_ref, x_ref, hidden_ref, feed_ref, bias_ref,
    near_ref, far_ref, result_ref, line_ref,
):
    step = pl.program_id(0)
    terms = nt(x_ref[...], both_ref[...]).astype(bf16)
    rows = pl.ds(pl.multiple_of(at_ref[step] * features, features), features)
    feed = feed_ref[rows, :] + bias_ref[:, 0:1]
    result_ref[rows, :] = (hidden_ref[...] + feed).astype(bf16)

    @pl.when(step == 0)
    def _():
        line_ref[...] = jnp.zeros_like(line_ref)

    line_ref[0:1, :] += summed(feed * feed)

    @pl.when(step < 2)
    def _():
        near_ref[0] = terms

    @pl.when(step >= 2)
    def _():
        far_ref[0] = terms


def swap(values, axis, bit):
    size = lax.axis_size(axis)
    return lax.ppermute(values, axis, [(i, i ^ bit) for i in range(size)])


def added(a, b):
    return (a.astype(f32) + b.astype(f32)).astype(bf16)


def axis_total(values, axis):
    bit = 1
    while bit < lax.axis_size(axis):
        values = values + swap(values, axis, bit)
        bit *= 2
    return values


def bits_of(axis):
    return [1 << k for k in range(lax.axis_size(axis).bit_length() - 1)]


def axis_of(bit):
    return 0 if bit == 0 else 1 + len(bits_of("seq")) - bit.bit_length()


def sent_down(terms, bit):
    if bit == 0:
        return terms[:1], terms[1:], swap(terms[1:], "mp", 2)
    mine = (lax.axis_index("seq") // bit) % 2
    kept = lax.dynamic_slice_in_dim(terms, mine, 1, axis_of(bit))
    sent = lax.dynamic_slice_in_dim(terms, 1 - mine, 1, axis_of(bit))
    return kept, sent, swap(sent, "seq", bit)


def up_step(terms, bit, gate):
    there = lax.optimization_barrier((swap(terms, "seq", bit), gate))[0]
    first = (lax.axis_index("seq") // bit) % 2 == 0
    return jnp.concatenate(
        [jnp.where(first, terms, there), jnp.where(first, there, terms)], axis=axis_of(bit)
    )


def shards(
    inputs,
    valid,
    cotangent,
    first_gain,
    step_size,
    decay_rate,
    frequency,
    readout_real,
    readout_imag,
    skip_weight,
    gated_weight,
    gated_bias,
    second_gain,
    expand_weight,
    expand_bias,
    shrink_weight,
    shrink_bias,
):
    mp = lax.axis_size("mp")
    seq = lax.axis_size("seq")
    mp_me = lax.axis_index("mp")
    seq_me = lax.axis_index("seq")
    features, contexts, local = inputs.shape
    chunk = min(CHUNK, local)
    chunks = local // chunk
    rows = contexts * chunks
    modes = decay_rate.shape[1]
    tokens = local
    hidden_own = expand_weight.shape[1]
    group = features // seq

    bits_at = [(k // 2) + 2 * (k % 2) for k in range(mp)]
    device_at = [jnp.bitwise_xor(mp_me, bit) for bit in bits_at]
    at = jnp.stack(device_at).astype(jnp.int32)

    def exchanged(values):
        sent = [lax.dynamic_index_in_dim(values, device_at[k], 0, keepdims=False) for k in range(mp)]
        return [sent[0]] + [swap(sent[k], "mp", bits_at[k]) for k in range(1, mp)]

    def returned(values):
        return lax.all_to_all(values.reshape(mp, features, local), "mp", 0, 0, tiled=True)

    def after(value, earlier):
        return lax.optimization_barrier((value, earlier))[0]

    def all_places(own, upper):
        return own, upper, swap(own, "mp", 1), swap(upper, "mp", 1)

    gated_own = gated_weight.transpose(1, 2, 0).reshape(2 * features, D)
    small = jnp.concatenate([gated_bias.reshape(-1), second_gain, expand_bias, shrink_bias])
    by_context = inputs.swapaxes(0, 1)
    squares = jnp.sum(jnp.square(by_context.astype(f32)), axis=1)
    sent = jnp.concatenate([squares.reshape(-1), small])
    flats = [sent] + [swap(sent, "mp", bits_at[k]) for k in range(1, mp)]
    small_places = jnp.stack([v[contexts * local :] for v in flats])
    square_one = sum(v[: contexts * local] for v in flats).reshape(contexts, local)

    part = hidden_own // seq

    expand_own = after(expand_weight, sent).T
    slices_sent = jnp.stack(
        [
            lax.dynamic_slice_in_dim(expand_own, seq_me * part, part, 0),
            lax.dynamic_slice_in_dim(shrink_weight, seq_me * part, part, 0),
        ]
    )
    slices = swap(slices_sent, "mp", 2)
    residual = lax.all_to_all(by_context, "mp", 0, 0, tiled=True)
    expand_far = swap(expand_own, "mp", 1)

    cut = [0, 2 * features]
    cut += [cut[-1] + features]
    cut += [cut[-1] + hidden_own]
    cut += [cut[-1] + features]

    def wide(values):
        return jnp.broadcast_to(values[..., None], values.shape + (128,))

    gated_bias_wide = wide(
        small_places[:, : cut[1]].reshape(mp, 2, features).swapaxes(0, 1).reshape(2, D)
    )
    gain_two_wide = wide(small_places[:, cut[1] : cut[2]].reshape(D))
    shrink_bias_wide = wide(small_places[:, cut[3] :].reshape(D))
    near_bias = wide(small_places[:2, cut[2] : cut[3]].reshape(-1))
    far_bias = wide(small_places[2:, cut[2] : cut[3]].reshape(-1))

    scale_one = lax.rsqrt(square_one / D + epsilon)
    scale_rows = scale_one.reshape(rows, chunk)

    w = discretized(step_size, decay_rate, frequency)
    coeff = coefficients(step_size, decay_rate, frequency, readout_real, readout_imag)

    def handed(ends, backward, ties=()):
        terms = lax.all_to_all(ends, "seq", 0, 0, tiled=True)
        (states,) = over_blocks(
            functools.partial(hand_kernel, seq, backward),
            1,
            [along(terms, None, 0), along(z_device, None, 0)],
            [along(out(terms.shape, bf16), None, 0)],
            3,
            (),
            ties,
        )
        return lax.all_to_all(states, "seq", 0, 0, tiled=True)

    def out(shape, dtype):
        return jax.ShapeDtypeStruct(shape, dtype)

    block, small_block = min(32, features), min(16, features)
    state_shape = out((features, rows, 4 * modes), f32)
    end_shape = out((features, contexts, 4 * modes), bf16)
    row_shape = out((features, rows, chunk), bf16)
    context_shape = out((contexts, features, local), bf16)
    table_shape = out((features, 4 * modes, chunk), bf16)
    sum_shape = out((7, features, 4 * modes), f32)
    line_shape = out((features, chunk), f32)
    flat = [pltpu.VMEM((block * rows, chunk), f32)]
    small_flat = [pltpu.VMEM((small_block * rows, chunk), f32)]
    skip_wide = jnp.broadcast_to(skip_weight[:, None], (features, chunk))
    gain_wide = jnp.broadcast_to(first_gain[:, None], (features, chunk))
    scan_steps = max(1, (chunks - 1).bit_length())
    pars, whole_pars, one, two, taps = by_channel(
        functools.partial(tables_kernel, chunk, scan_steps, local),
        small_block,
        features,
        [
            (step_size[:, None], 0),
            (decay_rate, 0),
            (frequency, 0),
            (readout_real, 0),
            (readout_imag, 0),
        ],
        [
            (out((features, 2 * scan_steps + 2, 4 * modes), f32), 0),
            (out((features, 2, 4 * modes), f32), 0),
            (table_shape, 0),
            (table_shape, 0),
            (line_shape, 0),
        ],
        10,
        [pltpu.VMEM((small_block, 8, 4 * modes), f32)],
        (sent,),
    )
    gated_upper = swap(gated_own, "mp", 2)
    shrink_far = swap(shrink_weight, "mp", 1)
    z_device = lax.dynamic_slice_in_dim(whole_pars, seq_me * group, group, 0)
    normed_one, terms, ends = by_channel(
        functools.partial(states_kernel, chunks),
        block,
        features,
        [(by_context, 1), (scale_rows, None), (gain_wide, 0), (two, 0), (pars, 0)],
        [(row_shape, 0), (state_shape, 0), (end_shape, 0)],
        8,
        flat,
        (slices_sent, residual),
    )
    upper = lax.all_gather(after(slices, normed_one), "seq", axis=0)
    upstream_parts = exchanged(after(cotangent, normed_one).swapaxes(0, 1))
    gated_places = (
        gated_own,
        gated_upper,
        swap(after(gated_own, normed_one), "mp", 1),
        swap(gated_upper, "mp", 1),
    )
    states_in = handed(ends, False, (shrink_far,))
    mixed, states, lifted_one = by_channel(
        functools.partial(mix_kernel, chunks),
        block,
        features,
        [
            (normed_one, 0),
            (terms, 0),
            (states_in, 0),
            (one, 0),
            (taps, 0),
            (skip_wide, 0),
            (pars, 0),
        ],
        [(row_shape, 0), (state_shape, 0), (context_shape, 1)],
        14,
        flat,
        (gated_upper,),
    )


    lifted_sent = after(lifted_one, (*upstream_parts, *gated_places))
    whole_one = lax.all_to_all(lifted_sent, "mp", 0, 0, tiled=True).reshape(D, tokens)
    upper_far = swap(after(upper, whole_one), "mp", 1)
    own_valid = lax.dynamic_slice_in_dim(valid, mp_me, 1, 0).astype(f32)

    token_block = min(256, tokens)
    token_steps = tokens // token_block
    wide_f = out((D, tokens), f32)
    wide_b = out((D, tokens), bf16)
    line_out = out((8, tokens), f32)

    def by_tokens(kernel, args, outs, us, scratch=(), ties=()):
        return over_blocks(
            kernel,
            token_steps,
            [along(a, d, token_block) if d != "smem" else (a, None, None) for a, d in args],
            [along(o, d, token_block) for o, d in outs],
            us,
            scratch,
            ties,
            60,
        )

    upstream, hidden, normed_two, value_part, opening, lines = by_tokens(
        functools.partial(gated_kernel, mp),
        [
            (at, "smem"),
            (own_valid, 1),
            (whole_one, 1),
            (residual.reshape(D, tokens), 1),
            *[(part_k, 1) for part_k in upstream_parts],
            *[(w_place, None) for w_place in gated_places],
            (gated_bias_wide, None),
            (gain_two_wide, None),
        ],
        [
            (wide_b, 1),
            (wide_f, 1),
            (wide_b, 1),
            (wide_f, 1),
            (wide_f, 1),
            (line_out, 1),
        ],
        12,
    )

    hidden_block = min(256, hidden_own)
    blocks = hidden_own // hidden_block
    near_rows = 2 * hidden_own

    parts = hidden_block // part
    low = ((hidden_block, D), lambda i: (jnp.minimum(i, blocks - 1), 0))
    grad_shape = out((near_rows, D), bf16)

    def half(which):
        return ((parts, 1, part, D), lambda i: (jnp.maximum(i - blocks, 0), which, 0, 0))

    def by_hidden(up, down, both, bias, carried, ties=()):
        first = carried is None
        args = [
            along(normed_two, None, 0),
            along(upstream, None, 0),
            (up, *low),
            (both, *half(0)),
            (down, *low),
            (both, *half(1)),
            along(bias, 0, hidden_block),
        ]
        if not first:
            args += [along(c, None, 0) for c in carried]
        return over_blocks(
            functools.partial(hidden_kernel, blocks, first),
            2 * blocks,
            args,
            [
                along(wide_f, None, 0),
                along(wide_f, None, 0),
                along(grad_shape, 0, hidden_block),
                (
                    out((2, D, hidden_own), bf16),
                    (1, D, hidden_block),
                    lambda i: (i // blocks, 0, i % blocks),
                ),
                along(out((near_rows, min(128, tokens)), f32), 0, hidden_block),
            ],
            38,
            [pltpu.VMEM((hidden_block, D), bf16)] * 2,
            ties,
        )

    feed, grad_normed_two, shrink_far_g, expand_far_g, far_lines = by_hidden(
        expand_far, shrink_far, upper_far, far_bias, None
    )
    core_shrink, core_expand = swap(shrink_far_g, "mp", 1), swap(expand_far_g, "mp", 1)
    feed, grad_normed_two, shrink_near_g, expand_near_g, near_lines = by_hidden(
        expand_own, shrink_weight, upper, near_bias, (feed, grad_normed_two)
    )
    bits = bits_of("seq")
    split = (2,) * (1 + len(bits))
    cubes = split + (-1, D)
    first, second, third, rest = bits[0], bits[1], bits[2], bits[3:]
    upper_bit = 0
    def onwards(kept, there, bit):
        if bit == upper_bit:
            stays, sent = (added(kept[part_k], there[part_k]) for part_k in (slice(0, 1), slice(1, 2)))
            return stays, sent, swap(sent, "mp", 2)
        mine = (seq_me // bit) % 2
        stays, sent = (
            added(
                lax.dynamic_slice_in_dim(kept, which, 1, axis_of(bit)),
                lax.dynamic_slice_in_dim(there, which, 1, axis_of(bit)),
            )
            for which in (mine, 1 - mine)
        )
        return stays, sent, swap(sent, "seq", bit)

    s_kept, s_sent, s_there = onwards(
        shrink_near_g.reshape(cubes), core_shrink.reshape(cubes), first
    )
    wide_cubes = split + (-1, hidden_own)
    e_kept, e_sent, e_there = onwards(
        expand_near_g.reshape(wide_cubes), core_expand.reshape(wide_cubes), second
    )

    sums_out = out((mp, 4, features, min(128, token_block)), f32)
    grad_lifted_one, grad_hidden, both_g, sums = by_tokens(
        functools.partial(gated_back_kernel, mp),
        [
            (at, "smem"),
            (grad_normed_two, 1),
            (hidden, 1),
            (value_part, 1),
            (opening, 1),
            (upstream, 1),
            (lines, 1),
            *[(w_place, None) for w_place in gated_places],
            (gain_two_wide, None),
        ],
        [(wide_b, 1), (wide_b, 1), (out((2 * D, tokens), bf16), 1), (sums_out, None)],
        14,
        (),
        (s_sent, e_sent),
    )
    own_lifted_one = returned(grad_lifted_one)
    gated_near, gated_far, result, feed_lines = over_blocks(
        functools.partial(gated_terms_kernel, features),
        mp,
        [
            (at, None, None),
            along(both_g, 0, 2 * features),
            along(whole_one, None, 0),
            along(hidden, 0, features),
            along(feed, None, 0),
            along(shrink_bias_wide, 0, features),
        ],
        [
            (
                out((2, D, 2 * features), bf16),
                (1, D, 2 * features),
                lambda i: (jnp.minimum(i, 1), 0, 0),
            ),
            (
                out((2, D, 2 * features), bf16),
                (1, D, 2 * features),
                lambda i: (jnp.maximum(i - 2, 0), 0, 0),
            ),
            along(wide_b, None, 0),
            along(line_out, None, 0),
        ],
        10,
    )
    core_gated = swap(gated_far, "mp", 1)

    grad_mixed, adj_terms, adj_ends = by_channel(
        functools.partial(ends_kernel, chunks),
        block,
        features,
        [(own_lifted_one, 1), (mixed, 0), (one, 0), (pars, 0)],
        [(row_shape, 0), (state_shape, 0), (end_shape, 0)],
        10,
        flat,
        (s_there, e_there, core_gated),
    )
    s_kept, s_sent, s_there = onwards(s_kept, s_there, second)
    e_kept, e_sent, e_there = onwards(e_kept, e_there, first)
    g_kept, g_sent, g_there = sent_down(added(gated_near, core_gated).reshape(split + (-1, 2 * features)), first)
    adjoint_in = handed(adj_ends, True, (s_sent, e_sent, g_sent))
    s_kept, s_sent, s_there = onwards(s_kept, s_there, third)
    e_kept, e_sent, e_there = onwards(e_kept, e_there, upper_bit)
    (sums_one,) = by_channel(
        sums_kernel,
        small_block,
        features,
        [(grad_mixed, 0), (normed_one, 0), (states, 0), (adj_terms, 0), (one, 0)],
        [(sum_shape, 1)],
        20,
        (),
        (s_sent, e_sent, adjoint_in),
    )
    own_hidden = returned(after(grad_hidden, adjoint_in))
    s_there, e_there, g_there = after((s_there, e_there, g_there), sums_one)
    g_kept, g_sent, g_there = onwards(g_kept, g_there, upper_bit)
    s_kept, s_sent, s_there = onwards(s_kept, s_there, upper_bit)
    e_kept, e_sent, e_there = onwards(e_kept, e_there, third)
    half = features // 2 // small_block
    back_args = [
        (grad_mixed, 0),
        (adj_terms, 0),
        (adjoint_in, 0),
        (normed_one, 0),
        (states, 0),
        (two, 0),
        (taps, 0),
        (skip_wide, 0),
        (pars, 0),
        (by_context, 1),
        (scale_rows, None),
        (gain_wide, 0),
    ]

    def back(first_block, ties):
        return by_channel(
            functools.partial(back_kernel, chunks),
            small_block,
            features // 2,
            back_args,
            [
                (out((contexts, features // 2, local), bf16), 1),
                (out((4, features // 2, 4 * modes), f32), 1),
                (out((rows, chunk), f32), None),
                (out((features // 2, chunk), f32), 0),
            ],
            12,
            small_flat,
            ties,
            first_block,
        )

    def exchange(values, bit, gate):
        return added(values, after(swap(values, "seq", bit), gate))

    low = back(0, (s_sent, e_sent, g_sent, sums_one, own_hidden))
    s_there, e_there, g_there = after((s_there, e_there, g_there), low[2])
    s_all, e_all, g_all = added(s_kept, s_there), added(e_kept, e_there), added(g_kept, g_there)
    for bit in rest:
        s_all, e_all = (added(*sent_down(v, bit)[::2]) for v in (s_all, e_all))
        g_all = exchange(g_all, bit, low[2])
    both_parts = jnp.stack([s_all.reshape(-1, D), e_all.reshape(-1, hidden_own)])
    both_all = lax.all_gather(both_parts, "seq", axis=0)
    high = back(half, (both_parts, g_all, low[2]))
    there = [swap(g_all, "seq", mask) for mask in (second, third, second + third)]
    there = after(there, high[2])
    g_all = sum(v.astype(f32) for v in [g_all] + there).astype(bf16)
    result = returned(after(result, (own_hidden, low[2])))
    grad_first_gain = jnp.sum(jnp.concatenate([low[3], high[3]]), axis=1)

    dot_one = axis_total(low[2] + high[2], "mp").reshape(contexts, local)
    cubic = scale_one * scale_one * scale_one * dot_one / D
    (grad_inputs,) = over_blocks(
        functools.partial(last_kernel, half),
        features // small_block,
        [
            along(by_context, 1, small_block),
            (low[0], (contexts, small_block, local), lambda i: (0, jnp.minimum(i, half - 1), 0)),
            (high[0], (contexts, small_block, local), lambda i: (0, jnp.maximum(i - half, 0), 0)),
            along(own_hidden, 1, small_block),
            along(scale_one, None, 0),
            along(cubic, None, 0),
            along(gain_wide, 0, small_block),
        ],
        [along(out(inputs.shape, f32), 0, small_block)],
        8,
    )

    stats = jnp.stack(
        [
            jnp.sum(own_valid[0] * lines[1]),
            jnp.sum(own_valid[0] * lines[2]),
            jnp.sum(own_valid[0] * feed_lines[0]),
            jnp.sum(own_valid[0]),
        ]
    )
    sums = jnp.sum(sums, axis=3).reshape(mp, 4 * features)
    sums = jnp.concatenate([sums, jnp.broadcast_to(stats, (mp, 4))], axis=1)
    near = jnp.concatenate([sums[:2], jnp.sum(near_lines, axis=1).reshape(2, hidden_own)], axis=1)
    far = jnp.concatenate([sums[2:], jnp.sum(far_lines, axis=1).reshape(2, hidden_own)], axis=1)
    near = near + swap(far, "mp", 1)
    bias_size = near.shape[1]

    def quarter(values, k):
        return values[:, k * modes : (k + 1) * modes]

    def product_sums(lines, k):
        plain, turned = lines[k], lines[k + 1]
        return (
            quarter(plain, 0) - quarter(plain, 1),
            quarter(turned, 1) + quarter(turned, 3),
        )

    inverse = power(w, -1.0)
    within = [
        cmul(inverse, (quarter(sums_one[k], 0), quarter(sums_one[k], 1))) for k in (4, 5)
    ]
    sum_a = cadd(product_sums(sums_one, 0), within[0])
    def both_halves(k):
        pairs = [product_sums(part_k[1], k) for part_k in (low, high)]
        return tuple(jnp.concatenate(v) for v in zip(*pairs))

    crossing = both_halves(0)
    part_a = product_sums(sums_one, 2)
    part_p = both_halves(2)
    sum_b = [
        float(chunk) * crossing[k] + part_a[k] - part_p[k] + within[1][k] for k in range(2)
    ]
    lines_late = jnp.concatenate(
        [sums_one[6, :, 0], grad_first_gain, near.reshape(-1)]
    )
    width = 4 * modes
    pad = -lines_late.shape[0] % width
    late = jnp.concatenate(
        [
            jnp.concatenate([*sum_a, *sum_b], axis=1),
            jnp.pad(lines_late, (0, pad)).reshape(-1, width),
        ],
        axis=0,
    )
    for bit in bits:
        if bit == third:
            late = after(late, g_all)
        late = late + swap(late, "seq", bit)
    g_all = up_step(g_all, first, grad_inputs)
    result = result.reshape(contexts, features, local)
    (result,) = by_channel(
        turned_kernel, 2 * block, features, [(result, 1)], [(out(inputs.shape, bf16), 0)], 5
    )
    grad_shrink = both_all[:, 0].reshape(-1, D).astype(f32)
    grad_expand = both_all[:, 1].reshape(D, hidden_own).astype(f32)
    grad_gated = g_all.reshape(D, 2, features).astype(f32)
    lines_late = late[features:].reshape(-1)
    late = late[:features]
    sum_a = (quarter(late, 0), quarter(late, 1))
    sum_b = (quarter(late, 2), quarter(late, 3))
    grad_skip = lines_late[:features]
    grad_first_gain = lines_late[features : 2 * features]
    bias_own = lines_late[2 * features : 2 * features + 2 * bias_size].reshape(2, bias_size)
    bias_own = bias_own[0] + swap(bias_own[1], "mp", 2)

    def form(step, decay, freq, out_real, out_imag):
        c = coefficients(step, decay, freq, out_real, out_imag)
        moved = cmul(coeff, discretized(step, decay, freq))
        return 2.0 * jnp.sum(
            c[0] * sum_a[0] - c[1] * sum_a[1] + moved[0] * sum_b[0] - moved[1] * sum_b[1]
        )

    kernel_grads = jax.grad(form, argnums=(0, 1, 2, 3, 4))(
        step_size, decay_rate, frequency, readout_real, readout_imag
    )
    ends_at = [0, 2 * features, 3 * features, 4 * features, 4 * features + 4]
    totals = bias_own[ends_at[3] : ends_at[4]]
    count = totals[3]
    rms = jnp.sqrt(totals[:3] / (count * D))
    return (
        result,
        grad_inputs,
        grad_first_gain,
        *kernel_grads,
        grad_skip,
        grad_gated,
        bias_own[: ends_at[1]].reshape(2, features),
        bias_own[ends_at[1] : ends_at[2]],
        grad_expand,
        bias_own[ends_at[4] :],
        grad_shrink,
        bias_own[ends_at[2] : ends_at[3]],
        rms[0],
        rms[1],
        rms[2],
    )


def solution(mesh):
    placed = (
        P("mp", None, "seq"),
        P(None, "seq"),
        P("mp", None, "seq"),
        P("mp"),
        P("mp"),
        P("mp", None),
        P("mp", None),
        P("mp", None),
        P("mp", None),
        P("mp"),
        P(None, None, "mp"),
        P(None, "mp"),
        P("mp"),
        P(None, "mp"),
        P("mp"),
        P("mp", None),
        P("mp"),
    )
    return jax.shard_map(
        shards,
        mesh=mesh,
        in_specs=placed,
        out_specs=(
            P("mp", None, "seq"),
            P("mp", None, "seq"),
            P("mp"),
            P("mp"),
            P("mp", None),
            P("mp", None),
            P("mp", None),
            P("mp", None),
            P("mp"),
            P(None, None, "mp"),
            P(None, "mp"),
            P("mp"),
            P(None, "mp"),
            P("mp"),
            P("mp", None),
            P("mp"),
            P(),
            P(),
            P(),
        ),
        check_vma=False,
    )
```
